256 devices in a mesh: seq: 64 (over z, x, core), head: 4 (over y).
Axes of the slice: x: 4, y: 4, z: 8, core: 2. Of those that a mesh axis runs over, the one named last changes fastest.
Arguments:
- layer_input: bfloat16 [32768, 4096], P('seq', 'head'), may hold values from -6 to 6
- gate_weight: bfloat16 [4096, 128], P('head'), may hold values from -0.09375 to 0.09375
- queries: bfloat16 [32768, 2048], P('seq', 'head'), may hold values from -3 to 3
- key_vectors: bfloat16 [32768, 2048], P('seq', 'head'), may hold values from -3 to 3
- value_vectors: bfloat16 [32768, 2048], P('seq', 'head'), may hold values from -3 to 3
- grad_output: bfloat16 [32768, 2048], P('seq', 'head'), may hold values from -6 to 6
- reach_level: int32 [512], P('seq'), may hold values from 1 to 7
Outputs:
- grad_queries: bfloat16 [32768, 2048], P('seq', 'head')
- grad_keys: bfloat16 [32768, 2048], P('seq', 'head')
- grad_values: bfloat16 [32768, 2048], P('seq', 'head')
- grad_gate_weight: float32 [4096, 128], P('head')
The draws below stay inside these ranges and needn't reach their ends.
All inputs are finite; a program needn't handle non-finite values.
Results may differ from the reference program's by a relative error of at most 0.0057.
Values may be sent and summed in bfloat16 or wider, within the bound.
No kernel may reach another device: no remote copies, remote signals or barrier semaphores. Data moves between devices by JAX's collectives and lax.ppermute only.
A program may use at most 64 MiB of HBM per device.

```python
import math
import jax
import jax.numpy as jnp
from jax import lax

DX = 4096
HEADS = 16
HEAD_DIM = 128
SPAN = 64
LEVELS = 8
NCH_DEV = 8
NCHUNKS = 512
TOKENS = 32768
N_SEQ = 64


def with_ends(drawn, stream_key, smallest, top_value):
    index_at = [jax.random.randint(jax.random.fold_in(stream_key, axis), (), 0, length) for axis, length in enumerate(drawn.shape)]
    widest = drawn.shape.index(max(drawn.shape))
    neighbour = index_at[:widest] + [(index_at[widest] + 1) % drawn.shape[widest]] + index_at[widest + 1:]
    return drawn.at[tuple(index_at)].set(smallest).at[tuple(neighbour)].set(top_value)


def block_levels(stream_key, shape, shards, smallest, largest):
    loudness, own = 1.0, jax.random.fold_in(stream_key, 6)
    for dim, blocks in shards:
        draws = jnp.exp(jax.random.uniform(jax.random.fold_in(own, dim), (blocks,), jnp.float32, smallest / len(shards), largest / len(shards)))
        loudness = loudness * jnp.repeat(draws, shape[dim] // blocks).reshape([-1 if axis == dim else 1 for axis in range(len(shape))])
    return loudness


def centred(own_key, shape, scale, bound, split=(), dtype=jnp.bfloat16):
    result = jax.random.normal(own_key, shape, jnp.float32) * scale
    if len(split) > 0:
        result = block_levels(own_key, shape, split, -0.22, 0.18) * result
    return jnp.clip(result, min=-bound, max=bound).astype(dtype)


def setup_inputs(seed: int = 0) -> dict:
    streams_of = jax.random.split(jax.random.key(seed), 8)
    layer_input = centred(streams_of[0], (TOKENS, DX), 1.0, 6.0, ((0, 64), (1, 4)))
    gate_weight = centred(streams_of[1], (DX, HEADS * LEVELS), DX ** -0.5, 0.09375, ((0, 4),))
    queries = centred(streams_of[2], (TOKENS, HEADS * HEAD_DIM), 0.5, 3.0, ((0, 64), (1, 4)))
    key_vectors = centred(streams_of[3], (TOKENS, HEADS * HEAD_DIM), 0.5, 3.0, ((0, 64), (1, 4)))
    value_vectors = centred(streams_of[4], (TOKENS, HEADS * HEAD_DIM), 0.5, 3.0, ((0, 64), (1, 4)))
    grad_output = centred(streams_of[5], (TOKENS, HEADS * HEAD_DIM), 1.0, 6.0, ((0, 64), (1, 4)))
    reach_level = with_ends(jax.random.randint(streams_of[6], (NCHUNKS,), 1, LEVELS), jax.random.fold_in(streams_of[6], 1), 1, LEVELS - 1).astype(jnp.int32)
    return dict(layer_input=layer_input, gate_weight=gate_weight, queries=queries, key_vectors=key_vectors, value_vectors=value_vectors, grad_output=grad_output, reach_level=reach_level)


def span_level(first, second):
    xored = jnp.bitwise_xor(first, second)
    total = jnp.zeros(xored.shape, jnp.int32)
    for power_idx in range(LEVELS - 1):
        total = total + (xored >= 1 << power_idx).astype(jnp.int32)
    return total

def reference(layer_input, gate_weight, queries, key_vectors, value_vectors, grad_output, reach_level):
    tok_count = NCH_DEV * SPAN
    blocks = N_SEQ
    span_bits = NCH_DEV.bit_length() - 1
    inv_dim = 1.0 / HEAD_DIM
    logits = jnp.dot(layer_input, gate_weight, preferred_element_type=jnp.float32)
    gates = jax.nn.sigmoid(logits).reshape(TOKENS, HEADS, LEVELS)
    allowed = (jnp.arange(LEVELS)[None, :] <= reach_level[:, None]).astype(jnp.float32)
    allowed_tok = jnp.repeat(allowed, SPAN, axis=0)
    weight = gates * allowed_tok[:, None, :]
    query_blk = queries.reshape(blocks, tok_count, HEADS, HEAD_DIM)
    key_blk = key_vectors.reshape(blocks, tok_count, HEADS, HEAD_DIM)
    value_blk = value_vectors.reshape(blocks, tok_count, HEADS, HEAD_DIM)
    grad_blk = grad_output.reshape(blocks, tok_count, HEADS, HEAD_DIM)
    weight_blk = weight.reshape(blocks, tok_count, HEADS, LEVELS)
    span_index = jnp.arange(NCH_DEV)
    local_level = span_level(span_index[:, None], span_index[None, :])
    onehot = (local_level[:, :, None] == jnp.arange(LEVELS)[None, None, :]).astype(jnp.float32)
    tok_onehot = jnp.repeat(onehot, SPAN, axis=0)
    positions = jnp.arange(tok_count)
    causal = (positions[None, :] <= positions[:, None]).astype(jnp.float32)
    cross_levels = list(range(span_bits + 1, LEVELS))

    def states(operands):
        query_d, key_d, value_d, grad_d, weight_d = operands
        query_f = query_d.astype(jnp.float32)
        grad_f = grad_d.astype(jnp.float32)
        block_state = jnp.einsum('shp,shq->hpq', key_d.astype(jnp.float32), value_d.astype(jnp.float32)) * inv_dim
        level_list = []
        for level in cross_levels:
            gated = (weight_d[:, :, level, None] * query_f).astype(jnp.bfloat16).astype(jnp.float32)
            level_list.append(jnp.einsum('thp,thq->hpq', gated, grad_f) * inv_dim)
        return (block_state, jnp.stack(level_list))
    state_all, level_grad = lax.map(states, (query_blk, key_blk, value_blk, grad_blk, weight_blk))
    block_index = jnp.arange(blocks)
    block_level = span_level(block_index[:, None] * NCH_DEV, block_index[None, :] * NCH_DEV)
    earlier = block_index[None, :] < block_index[:, None]
    forward_list = []
    backward_sum = jnp.zeros(state_all.shape, jnp.float32)
    for slot, level in enumerate(cross_levels):
        select = ((block_level == level) & earlier).astype(jnp.float32)
        forward_list.append(jnp.einsum('de,ehpq->dhpq', select, state_all, precision=lax.Precision.HIGHEST))
        backward_sum = backward_sum + jnp.einsum('ed,dhpq->ehpq', select.T, level_grad[:, slot], precision=lax.Precision.HIGHEST)
    level_state = jnp.stack(forward_list, axis=1).astype(jnp.bfloat16)
    later_state = backward_sum.astype(jnp.bfloat16)

    def finish(operands):
        query_d, key_d, value_d, grad_d, weight_d, level_d, later_d = operands
        query_f = query_d.astype(jnp.float32)
        key_f = key_d.astype(jnp.float32)
        value_f = value_d.astype(jnp.float32)
        grad_f = grad_d.astype(jnp.float32)
        scores = jnp.einsum('thp,shp->hts', query_f, key_f) * inv_dim
        grad_probs = jnp.einsum('thq,shq->hts', grad_f, value_f)
        level_table = lax.optimization_barrier(jnp.sum(tok_onehot[:, None, :, :] * weight_d[:, :, None, :], -1))
        pair_weight = jnp.repeat(level_table, SPAN, axis=2).transpose(1, 0, 2) * causal[None]
        weighted_scores = (pair_weight * scores).astype(jnp.bfloat16).astype(jnp.float32)
        weighted_grads = (pair_weight * grad_probs).astype(jnp.bfloat16).astype(jnp.float32)
        value_in = jnp.einsum('hts,thq->shq', weighted_scores, grad_f)
        key_in = jnp.einsum('hts,thp->shp', weighted_grads, query_f) * inv_dim
        query_in = jnp.einsum('hts,shp->thp', weighted_grads, key_f) * inv_dim
        row_sums = (scores * grad_probs * causal[None]).reshape(HEADS, tok_count, NCH_DEV, SPAN).sum(-1)
        grad_gates = lax.optimization_barrier(jnp.sum(row_sums.transpose(1, 0, 2)[:, :, :, None] * tok_onehot[:, None, :, :], 2))
        projected = jnp.einsum('thq,lhpq->lthp', grad_f, level_d.astype(jnp.float32))
        query_cross = jnp.zeros(query_in.shape, jnp.float32)
        for slot, level in enumerate(cross_levels):
            query_cross = query_cross + weight_d[:, :, level, None] * projected[slot]
            grad_gates = grad_gates.at[:, :, level].add(lax.optimization_barrier(jnp.sum(query_f * projected[slot], -1)))
        later_f = later_d.astype(jnp.float32)
        key_cross = jnp.einsum('shq,hpq->shp', value_f, later_f)
        value_cross = jnp.einsum('shp,hpq->shq', key_f, later_f)
        return ((query_in + query_cross).astype(jnp.bfloat16), (key_in + key_cross).astype(jnp.bfloat16), (value_in + value_cross).astype(jnp.bfloat16), grad_gates)
    grad_q, grad_k, grad_v, grad_gates = lax.map(finish, (query_blk, key_blk, value_blk, grad_blk, weight_blk, level_state, later_state))
    grad_gates = grad_gates.reshape(TOKENS, HEADS, LEVELS) * allowed_tok[:, None, :]
    grad_logits = (grad_gates * gates * (1.0 - gates)).reshape(TOKENS, HEADS * LEVELS).astype(jnp.bfloat16)
    grad_weight = jnp.dot(layer_input.T, grad_logits, preferred_element_type=jnp.float32) * (1.0 / math.sqrt(TOKENS))
    return (grad_q.reshape(TOKENS, HEADS * HEAD_DIM), grad_k.reshape(TOKENS, HEADS * HEAD_DIM), grad_v.reshape(TOKENS, HEADS * HEAD_DIM), grad_weight)
```

```python
import functools
import math

import jax
import jax.numpy as jnp
from jax import lax
from jax.experimental import pallas as pl
from jax.experimental.pallas import tpu as pltpu
from jax.sharding import PartitionSpec as P

F32 = jnp.float32
BF16 = jnp.bfloat16
TOK = 512
DIM = 128
SPAN = 64
LEVELS = 8
CHIPS = 32
INV = 1.0 / DIM
VMEM_LIMIT = 24 * 1024 * 1024


def mm(left, right, left_dim=1, right_dim=0):
    return lax.dot_general(
        left, right, (((left_dim,), (right_dim,)), ((), ())), preferred_element_type=F32
    )


def aligned(index, size):
    return pl.ds(pl.multiple_of(index * size, size), size)


def call(body, out_shape, args, in_specs=None, out_specs=None, grid=(), scratch=(), cost=(10**7, 10**6)):
    whole = pl.BlockSpec(memory_space=pltpu.VMEM)
    many = isinstance(out_shape, (tuple, list))
    return pl.pallas_call(
        body,
        out_shape=out_shape,
        grid=grid,
        in_specs=in_specs or [whole] * len(args),
        out_specs=out_specs or ([whole] * len(out_shape) if many else whole),
        scratch_shapes=list(scratch),
        compiler_params=pltpu.CompilerParams(vmem_limit_bytes=VMEM_LIMIT),
        cost_estimate=pl.CostEstimate(flops=cost[0], bytes_accessed=cost[1], transcendentals=0),
    )(*args)


def shape(dims, dtype):
    return jax.ShapeDtypeStruct(dims, dtype)


def logits_body(x_ref, w_ref, o0, o1, o2, o3, scr):
    head = lax.axis_index("head")
    scr[...] = mm(w_ref[...], x_ref[...], 0, 1)
    for step, out in enumerate((o0, o1, o2, o3)):
        out[...] = scr[aligned(lax.rem(head + step, 4), 32), :]


def state_body(k_ref, v_ref, o_ref):
    o_ref[...] = mm(k_ref[...], v_ref[...], 0, 0) * INV


def allowed_mask(reach_ref):
    lane = lax.broadcasted_iota(jnp.int32, (LEVELS, TOK), 1) // SPAN
    level = lax.broadcasted_iota(jnp.int32, (LEVELS, TOK), 0)
    reach = jnp.zeros((LEVELS, TOK), jnp.int32)
    for span in range(TOK // SPAN):
        reach = jnp.where(lane == span, reach_ref[span], reach)
    return (level <= reach).astype(F32)


def level_body(q_ref, g_ref, l0, l1, l2, l3, reach_ref, gates_ref, msg_ref, keep_ref, w_scr):
    core = lax.axis_index("seq") & 1
    gates = jax.nn.sigmoid((l0[...] + l1[...]) + (l2[...] + l3[...]))
    gates_ref[...] = gates
    allowed = allowed_mask(reach_ref)
    for head in range(4):
        w_scr[8 * head : 8 * head + 8, :] = gates[8 * head : 8 * head + 8, :] * allowed
    for slot in range(4):
        kept = slot < 2
        head = 2 * core + slot if kept else 2 * (1 - core) + slot - 2
        query = q_ref[:, aligned(head, DIM)].astype(F32).T
        weight = w_scr[aligned(head, 8), :]
        gated = jnp.concatenate(
            [(weight[level : level + 1, :] * query).astype(BF16) for level in range(4, 8)], axis=0
        )
        grads = mm(gated, g_ref[:, aligned(head, DIM)]) * INV
        msg_ref[aligned(head, DIM), :] = grads[:DIM]
        for level in range(3):
            part = grads[DIM * (level + 1) : DIM * (level + 2)]
            row = 256 * level + DIM * (slot % 2)
            if kept:
                keep_ref[row : row + DIM, :] = part
            else:
                msg_ref[512 + row : 512 + row + DIM, :] = part


def mid1_body(r_ref, keep_ref, recv_ref, o_ref):
    own = [r_ref[chip] for chip in range(CHIPS)]
    pairs = [own[chip] + own[chip ^ 1] for chip in range(CHIPS)]
    zero = jnp.zeros((8, DIM), F32)
    before = [zero]
    for group in range(7):
        before.append(before[-1] + (pairs[4 * group] + pairs[4 * group + 2]))
    for chip in range(CHIPS):
        rows = [
            own[chip ^ 1] if chip & 1 else zero,
            pairs[chip ^ 2] if chip & 2 else zero,
            before[chip >> 2],
        ]
        for level in range(3):
            row = 256 * level + 8 * chip
            rows.append(keep_ref[row : row + 8, :] + recv_ref[512 + row : 512 + row + 8, :])
        o_ref[chip] = jnp.concatenate(rows, axis=0).astype(BF16)


def mid2_body(r_ref, states_ref, later_ref):
    got = [r_ref[chip].astype(F32) for chip in range(CHIPS)]
    for chip in range(0, CHIPS, 2):
        for level in range(3):
            both = [got[chip + i][8 * level : 8 * level + 8] for i in range(2)]
            row = 256 * level + 8 * chip
            states_ref[row : row + 16, :] = jnp.concatenate(both, axis=0).astype(BF16)
    zero = jnp.zeros((8, DIM), F32)
    after = [zero]
    for group in range(7, 0, -1):
        total = zero
        for chip in range(4 * group, 4 * group + 4):
            total = total + got[chip][40:48]
        after.append(after[-1] + total)
    after = after[::-1]
    for chip in range(CHIPS):
        total = after[chip >> 2]
        if not chip & 2:
            total = total + (got[chip ^ 2][32:40] + got[chip ^ 3][32:40])
        if not chip & 1:
            total = total + got[chip ^ 1][24:32]
        later_ref[chip] = total


def intra_body(q_ref, k_ref, v_ref, g_ref, gates_ref, reach_ref, dk_ref, dv_ref, dq_ref, rows_ref, p_scr, w_scr):
    weight = gates_ref[...] * allowed_mask(reach_ref)
    src = lax.broadcasted_iota(jnp.int32, (DIM, DIM), 0)
    dst = lax.broadcasted_iota(jnp.int32, (DIM, DIM), 1)
    same = (src // SPAN) == (dst // SPAN)
    mask0 = (same & (src <= dst)).astype(F32)
    mask1 = ((src // SPAN) < (dst // SPAN)).astype(F32)
    tiles = TOK // DIM
    key_t = k_ref[...].astype(F32).T.astype(BF16)
    row_parts = []
    for a in range(tiles):
        cols = slice(DIM * a, DIM * (a + 1))
        end = DIM * (a + 1)
        scores = mm(k_ref[:end, :], q_ref[cols, :], 1, 1) * INV
        probs = mm(v_ref[:end, :], g_ref[cols, :], 1, 1)
        prod = scores * probs
        sums = [None] * 4
        weights = []
        for b in range(a):
            level = (a ^ b).bit_length() + 1
            part = jnp.sum(prod[DIM * b : DIM * (b + 1)], axis=0, keepdims=True)
            sums[level] = part if sums[level] is None else sums[level] + part
            weights.append(jnp.broadcast_to(weight[level : level + 1, cols], (DIM, DIM)))
        diagonal = prod[DIM * a :]
        sums[0] = jnp.sum(diagonal * mask0, axis=0, keepdims=True)
        sums[1] = jnp.sum(diagonal * mask1, axis=0, keepdims=True)
        weights.append(weight[0:1, cols] * mask0 + weight[1:2, cols] * mask1)
        none = jnp.zeros((1, DIM), F32)
        sums = [none if part is None else part for part in sums]
        row_parts.append(jnp.concatenate(sums + [none] * 4, axis=0))
        pair = jnp.concatenate(weights, axis=0)
        p_scr[:end, cols] = (pair * scores).astype(BF16)
        weighted = (pair * probs).astype(BF16)
        w_scr[:end, cols] = weighted
        dq_ref[:, cols] = mm(key_t[:, :end], weighted) * INV
    rows_ref[...] = jnp.concatenate(row_parts, axis=1)
    for b in range(tiles):
        rows = slice(DIM * b, DIM * (b + 1))
        start = DIM * b
        dv_ref[rows, :] = mm(p_scr[rows, start:], g_ref[start:, :])
        dk_ref[rows, :] = mm(w_scr[rows, start:], q_ref[start:, :]) * INV


def cross_body(q_ref, g_ref, sib_ref, mine_ref, other_ref, gates_ref, reach_ref, dqt_ref, rows_ref, dq_ref, gl_ref):
    half = pl.program_id(0)
    core = lax.axis_index("seq") & 1
    allowed = allowed_mask(reach_ref)
    upper = (core == 1).astype(F32)
    outs = []
    for i in range(2):
        lanes = slice(DIM * i, DIM * (i + 1))
        rows = slice(DIM * i, DIM * (i + 1))
        levels = [(sib_ref[rows, :] * upper).astype(BF16)]
        for level in range(3):
            at = slice(256 * level + DIM * i, 256 * level + DIM * (i + 1))
            levels.append(jnp.where(half == core, mine_ref[at, :], other_ref[at, :]))
        projected = mm(jnp.concatenate(levels, axis=0), g_ref[:, lanes], 1, 1)
        query = q_ref[:, lanes].astype(F32).T
        gates = gates_ref[8 * i : 8 * i + 8, :]
        weight = gates * allowed
        total = dqt_ref[rows, :]
        parts = []
        for level in range(4):
            term = projected[DIM * level : DIM * (level + 1)]
            total = total + weight[4 + level : 5 + level, :] * term
            parts.append(jnp.sum(query * term, axis=0, keepdims=True))
        dq_ref[:, lanes] = total.T.astype(BF16)
        cross = jnp.concatenate([jnp.zeros((4, TOK), F32)] + parts, axis=0)
        grads = (rows_ref[8 * i : 8 * i + 8, :] + cross) * allowed
        outs.append(grads * gates * (1.0 - gates))
    gl_ref[...] = jnp.concatenate(outs, axis=0).astype(BF16)


def gradw_body(x_ref, g0, g1, g2, g3, keep_ref, send_ref, scr, full):
    head = lax.axis_index("head")
    core = lax.axis_index("seq") & 1
    for step, part in enumerate((g0, g1, g2, g3)):
        scr[aligned(lax.rem(head + 4 - step, 4), 32), :] = part[...]
    full[...] = mm(scr[...], x_ref[...]).T
    keep_ref[...] = full[aligned(core, 512), :]
    send_ref[...] = full[aligned(1 - core, 512), :]


def pack3_body(keep_ref, recv_ref, later_ref, o_ref):
    for chip in range(CHIPS):
        rows = slice(16 * chip, 16 * chip + 16)
        o_ref[chip, 0:16, :] = keep_ref[rows, :] + recv_ref[rows, :]
        o_ref[chip, 16:24, :] = later_ref[chip]


def mid3_body(scale, r_ref, sums_ref, later_ref):
    total = r_ref[0, 0:16, :]
    for chip in range(1, CHIPS):
        total = total + r_ref[chip, 0:16, :]
    total = total * scale
    for chip in range(CHIPS):
        sums_ref[chip] = total
    for chip in range(CHIPS):
        later_ref[8 * chip : 8 * chip + 8, :] = r_ref[chip, 16:24, :]


def final_body(k_ref, v_ref, sib_ref, mine_ref, other_ref, dki_ref, dvi_ref, dk_ref, dv_ref):
    half = pl.program_id(0) // 2
    core = lax.axis_index("seq") & 1
    later = jnp.where(half == core, mine_ref[...], other_ref[...])
    lower = (core == 0).astype(F32)
    later = (later + sib_ref[...] * lower).astype(BF16)
    dk_ref[...] = (dki_ref[...] + mm(v_ref[...], later, 1, 1)).astype(BF16)
    dv_ref[...] = (dvi_ref[...] + mm(k_ref[...], later, 1, 0)).astype(BF16)


def shards(layer_input, gate_weight, queries, key_vectors, value_vectors, grad_output, reach_level):
    seq_count = lax.axis_size("seq")
    core = lax.axis_index("seq") & 1
    groups = [[2 * chip + c for chip in range(CHIPS)] for c in range(2)]
    swap = [(d, d ^ 1) for d in range(seq_count)]

    def sibling(value):
        return lax.ppermute(value, "seq", swap)

    def exchange(value):
        return lax.all_to_all(value, "seq", 0, 0, axis_index_groups=groups)

    def rotate(value, step):
        return lax.ppermute(value, "head", [(h, (h + step) % 4) for h in range(4)])

    def whole():
        return pl.BlockSpec(memory_space=pltpu.VMEM)

    smem = pl.BlockSpec(memory_space=pltpu.SMEM)
    heads4 = pl.BlockSpec((TOK, DIM), lambda h: (0, h))
    rows4 = pl.BlockSpec((DIM, DIM), lambda h: (h, 0))

    states = call(
        state_body, shape((512, DIM), F32), (key_vectors, value_vectors),
        in_specs=[heads4, heads4], out_specs=rows4, grid=(4,),
    )
    sib_state = sibling(states)

    parts = call(
        logits_body, [shape((32, TOK), F32)] * 4, (layer_input, gate_weight),
        scratch=[pltpu.VMEM((DIM, TOK), F32)],
    )
    logits = [parts[0]] + [rotate(parts[step], step) for step in range(1, 4)]

    pair = lax.dynamic_slice(states + sib_state, (256 * core, 0), (256, DIM))
    got1 = exchange(pair.reshape(CHIPS, 8, DIM))

    gates, msg, keep = call(
        level_body,
        [shape((32, TOK), F32), shape((1280, DIM), F32), shape((768, DIM), F32)],
        (queries, grad_output, *logits, reach_level),
        in_specs=[whole()] * 6 + [smem],
        scratch=[pltpu.VMEM((32, TOK), F32)],
    )
    msg_in = sibling(msg)
    got2 = exchange(call(mid1_body, shape((CHIPS, 48, DIM), BF16), (got1, keep, msg_in)))

    dk_in, dv_in, dq_t, rows = call(
        intra_body,
        [shape((TOK, 512), F32), shape((TOK, 512), F32), shape((512, TOK), F32), shape((32, TOK), F32)],
        (queries, key_vectors, value_vectors, grad_output, gates, reach_level),
        in_specs=[heads4] * 4 + [pl.BlockSpec((8, TOK), lambda h: (h, 0)), smem],
        out_specs=[heads4, heads4, pl.BlockSpec((DIM, TOK), lambda h: (h, 0)), pl.BlockSpec((8, TOK), lambda h: (h, 0))],
        grid=(4,),
        scratch=[pltpu.VMEM((TOK, TOK), BF16), pltpu.VMEM((TOK, TOK), BF16)],
        cost=(2 * 10**9, 8 * 10**6),
    )

    level_half, later_slices = call(
        mid2_body, [shape((768, DIM), BF16), shape((CHIPS, 8, DIM), F32)], (got2,)
    )
    level_other = sibling(level_half)

    heads2 = pl.BlockSpec((TOK, 256), lambda h: (0, h))
    tok16 = pl.BlockSpec((16, TOK), lambda h: (h, 0))
    all768 = pl.BlockSpec((768, DIM), lambda h: (0, 0))
    grad_queries, grad_logits = call(
        cross_body,
        [shape((TOK, 512), BF16), shape((32, TOK), BF16)],
        (queries, grad_output, sib_state, level_half, level_other, gates, reach_level, dq_t, rows),
        in_specs=[
            heads2, heads2, pl.BlockSpec((256, DIM), lambda h: (h, 0)), all768, all768, tok16, smem,
            pl.BlockSpec((256, TOK), lambda h: (h, 0)), tok16,
        ],
        out_specs=[heads2, tok16],
        grid=(2,),
    )

    gl = [grad_logits] + [rotate(grad_logits, step) for step in range(1, 4)]
    w_keep, w_send = call(
        gradw_body, [shape((512, DIM), F32)] * 2, (layer_input, *gl),
        scratch=[pltpu.VMEM((DIM, TOK), BF16), pltpu.VMEM((1024, DIM), F32)],
    )
    w_in = sibling(w_send)
    got3 = exchange(call(pack3_body, shape((CHIPS, 24, DIM), F32), (w_keep, w_in, later_slices)))
    scale = 1.0 / math.sqrt(TOK * seq_count)
    sums, later_half = call(
        functools.partial(mid3_body, scale),
        [shape((CHIPS, 16, DIM), F32), shape((256, DIM), F32)], (got3,),
    )
    got4 = exchange(sums)
    later_other = sibling(later_half)

    half4 = pl.BlockSpec((DIM, DIM), lambda h: (h % 2, 0))
    grad_keys, grad_values = call(
        final_body,
        [shape((TOK, 512), BF16)] * 2,
        (key_vectors, value_vectors, msg_in, later_half, later_other, dk_in, dv_in),
        in_specs=[heads4, heads4, rows4, half4, half4, heads4, heads4],
        out_specs=[heads4, heads4],
        grid=(4,),
    )

    w_half = got4.reshape(512, DIM)
    w_other = sibling(w_half)
    low = jnp.where(core == 0, w_half, w_other)
    high = jnp.where(core == 0, w_other, w_half)
    return grad_queries, grad_keys, grad_values, jnp.concatenate([low, high], axis=0)


def solution(mesh):
    placed = (
        P("seq", "head"),
        P("head", None),
        P("seq", "head"),
        P("seq", "head"),
        P("seq", "head"),
        P("seq", "head"),
        P("seq"),
    )
    return jax.shard_map(
        shards,
        mesh=mesh,
        in_specs=placed,
        out_specs=(P("seq", "head"), P("seq", "head"), P("seq", "head"), P("head", None)),
        check_vma=False,
    )
```

```python
import functools
import math

import jax
import jax.numpy as jnp
from jax import lax
from jax.experimental import pallas as pl
from jax.experimental.pallas import tpu as pltpu
from jax.sharding import PartitionSpec as P

F32 = jnp.float32
BF16 = jnp.bfloat16
TOK = 512
DIM = 128
SPAN = 64
LEVELS = 8
CHIPS = 32
INV = 1.0 / DIM
VMEM_LIMIT = 24 * 1024 * 1024


def mm(left, right, left_dim=1, right_dim=0):
    return lax.dot_general(
        left, right, (((left_dim,), (right_dim,)), ((), ())), preferred_element_type=F32
    )


def aligned(index, size):
    return pl.ds(pl.multiple_of(index * size, size), size)


def call(
    body, out_shape, args, in_specs=None, out_specs=None, grid=(), scratch=(), cost=(10**7, 10**6), after=()
):
    whole = pl.BlockSpec(memory_space=pltpu.VMEM)
    many = isinstance(out_shape, (tuple, list))
    used = len(args)
    in_specs = list(in_specs or [whole] * used) + [pl.BlockSpec(memory_space=pl.ANY)] * len(after)
    args = (*args, *after)

    def kernel(*refs):
        body(*refs[:used], *refs[len(args) :])

    return pl.pallas_call(
        kernel,
        out_shape=out_shape,
        grid=grid,
        in_specs=in_specs,
        out_specs=out_specs or ([whole] * len(out_shape) if many else whole),
        scratch_shapes=list(scratch),
        compiler_params=pltpu.CompilerParams(vmem_limit_bytes=VMEM_LIMIT),
        cost_estimate=pl.CostEstimate(flops=cost[0], bytes_accessed=cost[1], transcendentals=0),
    )(*args)


def shape(dims, dtype):
    return jax.ShapeDtypeStruct(dims, dtype)


def logits_body(x_ref, w_ref, o0, o1, o2, o3, scr):
    head = lax.axis_index("head")
    scr[...] = mm(w_ref[...], x_ref[...], 0, 1)
    for step, out in enumerate((o0, o1, o2, o3)):
        out[...] = scr[aligned(lax.rem(head + step, 4), 32), :]


def state_body(k_ref, v_ref, o_ref):
    o_ref[...] = mm(k_ref[...], v_ref[...], 0, 0) * INV


def allowed_mask(reach_ref):
    lane = lax.broadcasted_iota(jnp.int32, (LEVELS, TOK), 1) // SPAN
    level = lax.broadcasted_iota(jnp.int32, (LEVELS, TOK), 0)
    reach = jnp.zeros((LEVELS, TOK), jnp.int32)
    for span in range(TOK // SPAN):
        reach = jnp.where(lane == span, reach_ref[span], reach)
    return (level <= reach).astype(F32)


def level_body(q_ref, g_ref, l0, l1, l2, l3, reach_ref, gates_ref, near_ref, keep_ref, send_ref, w_scr):
    core = lax.axis_index("seq") & 1
    gates = jax.nn.sigmoid((l0[...] + l1[...]) + (l2[...] + l3[...]))
    gates_ref[...] = gates
    allowed = allowed_mask(reach_ref)
    for head in range(4):
        w_scr[8 * head : 8 * head + 8, :] = gates[8 * head : 8 * head + 8, :] * allowed
    for slot in range(4):
        head = 2 * core + slot if slot < 2 else 2 * (1 - core) + slot - 2
        out = keep_ref if slot < 2 else send_ref
        query = q_ref[:, aligned(head, DIM)].astype(F32).T
        weight = w_scr[aligned(head, 8), :]
        gated = jnp.concatenate(
            [(weight[level : level + 1, :] * query).astype(BF16) for level in range(4, 8)], axis=0
        )
        grads = mm(gated, g_ref[:, aligned(head, DIM)]) * INV
        near_ref[aligned(head, DIM), :] = grads[:DIM]
        for level in range(3):
            row = 256 * level + DIM * (slot % 2)
            out[row : row + DIM, :] = grads[DIM * (level + 1) : DIM * (level + 2)]


def pack1_body(state_ref, sib_ref, keep_ref, recv_ref, o_ref):
    core = lax.axis_index("seq") & 1
    for chip in range(CHIPS):
        at = pl.ds(pl.multiple_of(256 * core + 8 * chip, 8), 8)
        rows = [state_ref[at, :] + sib_ref[at, :]]
        for level in range(3):
            row = 256 * level + 8 * chip
            rows.append(keep_ref[row : row + 8, :] + recv_ref[row : row + 8, :])
        o_ref[chip] = jnp.concatenate(rows, axis=0).astype(BF16)


def mid1_body(r_ref, o_ref):
    got = [r_ref[chip].astype(F32) for chip in range(CHIPS)]
    own = [part[0:8] for part in got]
    pairs = [own[chip] + own[chip ^ 1] for chip in range(CHIPS)]
    zero = jnp.zeros((8, DIM), F32)
    before = [zero]
    for group in range(7):
        before.append(before[-1] + (pairs[4 * group] + pairs[4 * group + 2]))
    after = [zero]
    for group in range(7, 0, -1):
        total = [got[4 * group + i][24:32] for i in range(4)]
        after.append(after[-1] + ((total[0] + total[1]) + (total[2] + total[3])))
    after = after[::-1]
    for chip in range(CHIPS):
        later = after[chip >> 2]
        if not chip & 2:
            later = later + (got[chip ^ 2][16:24] + got[chip ^ 3][16:24])
        if not chip & 1:
            later = later + got[chip ^ 1][8:16]
        rows = [
            own[chip ^ 1] if chip & 1 else zero,
            pairs[chip ^ 2] if chip & 2 else zero,
            before[chip >> 2],
            later,
        ]
        o_ref[chip] = jnp.concatenate(rows, axis=0).astype(BF16)


def mid2_body(r_ref, o_ref):
    for chip in range(0, CHIPS, 2):
        got = [r_ref[chip + i].astype(F32) for i in range(2)]
        for level in range(4):
            both = [part[8 * level : 8 * level + 8] for part in got]
            row = 256 * level + 8 * chip
            o_ref[row : row + 16, :] = jnp.concatenate(both, axis=0).astype(BF16)


def intra_body(q_ref, k_ref, v_ref, g_ref, gates_ref, reach_ref, dk_ref, dv_ref, dq_ref, rows_ref, p_scr, w_scr):
    weight = gates_ref[...] * allowed_mask(reach_ref)
    src = lax.broadcasted_iota(jnp.int32, (DIM, DIM), 0)
    dst = lax.broadcasted_iota(jnp.int32, (DIM, DIM), 1)
    same = (src // SPAN) == (dst // SPAN)
    mask0 = (same & (src <= dst)).astype(F32)
    mask1 = ((src // SPAN) < (dst // SPAN)).astype(F32)
    tiles = TOK // DIM
    key_t = k_ref[...].astype(F32).T.astype(BF16)
    row_parts = []
    for a in range(tiles):
        cols = slice(DIM * a, DIM * (a + 1))
        end = DIM * (a + 1)
        scores = mm(k_ref[:end, :], q_ref[cols, :], 1, 1) * INV
        probs = mm(v_ref[:end, :], g_ref[cols, :], 1, 1)
        prod = scores * probs
        sums = [None] * 4
        weights = []
        for b in range(a):
            level = (a ^ b).bit_length() + 1
            part = jnp.sum(prod[DIM * b : DIM * (b + 1)], axis=0, keepdims=True)
            sums[level] = part if sums[level] is None else sums[level] + part
            weights.append(jnp.broadcast_to(weight[level : level + 1, cols], (DIM, DIM)))
        diagonal = prod[DIM * a :]
        sums[0] = jnp.sum(diagonal * mask0, axis=0, keepdims=True)
        sums[1] = jnp.sum(diagonal * mask1, axis=0, keepdims=True)
        weights.append(weight[0:1, cols] * mask0 + weight[1:2, cols] * mask1)
        none = jnp.zeros((1, DIM), F32)
        sums = [none if part is None else part for part in sums]
        row_parts.append(jnp.concatenate(sums + [none] * 4, axis=0))
        pair = jnp.concatenate(weights, axis=0)
        p_scr[:end, cols] = (pair * scores).astype(BF16)
        weighted = (pair * probs).astype(BF16)
        w_scr[:end, cols] = weighted
        dq_ref[:, cols] = mm(key_t[:, :end], weighted) * INV
    rows_ref[...] = jnp.concatenate(row_parts, axis=1)
    for b in range(tiles):
        rows = slice(DIM * b, DIM * (b + 1))
        start = DIM * b
        dv_ref[rows, :] = mm(p_scr[rows, start:], g_ref[start:, :])
        dk_ref[rows, :] = mm(w_scr[rows, start:], q_ref[start:, :]) * INV


def cross_body(q_ref, g_ref, sib_ref, mine_ref, other_ref, gates_ref, reach_ref, rows_ref, dqt_ref, gl_ref):
    half = pl.program_id(0)
    core = lax.axis_index("seq") & 1
    allowed = allowed_mask(reach_ref)
    upper = (core == 1).astype(F32)
    outs = []
    for i in range(2):
        lanes = slice(DIM * i, DIM * (i + 1))
        rows = slice(DIM * i, DIM * (i + 1))
        levels = [(sib_ref[rows, :] * upper).astype(BF16)]
        for level in range(3):
            at = slice(256 * level + DIM * i, 256 * level + DIM * (i + 1))
            levels.append(jnp.where(half == core, mine_ref[at, :], other_ref[at, :]))
        projected = mm(jnp.concatenate(levels, axis=0), g_ref[:, lanes], 1, 1)
        query = q_ref[:, lanes].astype(F32).T
        gates = gates_ref[8 * i : 8 * i + 8, :]
        weight = gates * allowed
        total = None
        parts = []
        for level in range(4):
            term = projected[DIM * level : DIM * (level + 1)]
            weighted = weight[4 + level : 5 + level, :] * term
            total = weighted if total is None else total + weighted
            parts.append(jnp.sum(query * term, axis=0, keepdims=True))
        dqt_ref[rows, :] = total
        cross = jnp.concatenate([jnp.zeros((4, TOK), F32)] + parts, axis=0)
        grads = (rows_ref[8 * i : 8 * i + 8, :] + cross) * allowed
        outs.append(grads * gates * (1.0 - gates))
    gl_ref[...] = jnp.concatenate(outs, axis=0).astype(BF16)


def queries_body(in_ref, cross_ref, o_ref):
    o_ref[...] = (in_ref[...] + cross_ref[...]).T.astype(BF16)


def gradw_body(x_ref, g0, g1, g2, g3, keep_ref, send_ref, scr, full):
    head = lax.axis_index("head")
    core = lax.axis_index("seq") & 1
    for step, part in enumerate((g0, g1, g2, g3)):
        scr[aligned(lax.rem(head + 4 - step, 4), 32), :] = part[...]
    full[...] = mm(scr[...], x_ref[...]).T
    keep_ref[...] = full[aligned(core, 512), :]
    send_ref[...] = full[aligned(1 - core, 512), :]


def pack3_body(keep_ref, recv_ref, o_ref):
    for chip in range(CHIPS):
        rows = slice(16 * chip, 16 * chip + 16)
        o_ref[chip] = keep_ref[rows, :] + recv_ref[rows, :]


def mid3_body(scale, r_ref, o_ref):
    total = r_ref[0]
    for chip in range(1, CHIPS):
        total = total + r_ref[chip]
    total = (total * scale).astype(BF16)
    for chip in range(CHIPS):
        o_ref[chip] = total


def join_body(mine_ref, other_ref, o_ref):
    core = lax.axis_index("seq") & 1
    o_ref[aligned(core, 512), :] = mine_ref[...].astype(F32)
    o_ref[aligned(1 - core, 512), :] = other_ref[...].astype(F32)


def final_body(k_ref, v_ref, near_ref, mine_ref, other_ref, dki_ref, dvi_ref, dk_ref, dv_ref):
    half = pl.program_id(0) // 2
    core = lax.axis_index("seq") & 1
    later = jnp.where(half == core, mine_ref[...], other_ref[...]).astype(F32)
    lower = (core == 0).astype(F32)
    later = (later + near_ref[...] * lower).astype(BF16)
    dk_ref[...] = (dki_ref[...] + mm(v_ref[...], later, 1, 1)).astype(BF16)
    dv_ref[...] = (dvi_ref[...] + mm(k_ref[...], later, 1, 0)).astype(BF16)


def shards(layer_input, gate_weight, queries, key_vectors, value_vectors, grad_output, reach_level):
    seq_count = lax.axis_size("seq")
    groups = [[2 * chip + c for chip in range(CHIPS)] for c in range(2)]
    swap = [(d, d ^ 1) for d in range(seq_count)]

    def sibling(value):
        return lax.ppermute(value, "seq", swap)

    def exchange(value):
        return lax.all_to_all(value, "seq", 0, 0, axis_index_groups=groups)

    def rotate(value, step):
        return lax.ppermute(value, "head", [(h, (h + step) % 4) for h in range(4)])

    whole = pl.BlockSpec(memory_space=pltpu.VMEM)
    smem = pl.BlockSpec(memory_space=pltpu.SMEM)
    heads4 = pl.BlockSpec((TOK, DIM), lambda h: (0, h))
    rows4 = pl.BlockSpec((DIM, DIM), lambda h: (h, 0))
    rows4_tok = pl.BlockSpec((DIM, TOK), lambda h: (h, 0))
    gates4 = pl.BlockSpec((8, TOK), lambda h: (h, 0))

    parts = call(
        logits_body, [shape((32, TOK), F32)] * 4, (layer_input, gate_weight),
        scratch=[pltpu.VMEM((DIM, TOK), F32)],
    )
    logits = [parts[0]] + [rotate(parts[step], step) for step in range(1, 4)]
    states = call(
        state_body, shape((512, DIM), F32), (key_vectors, value_vectors),
        in_specs=[heads4, heads4], out_specs=rows4, grid=(4,), after=(parts[0],),
    )
    sib_state = sibling(states)

    gates, near, keep, send = call(
        level_body,
        [shape((32, TOK), F32), shape((512, DIM), F32), shape((768, DIM), F32), shape((768, DIM), F32)],
        (queries, grad_output, *logits, reach_level),
        in_specs=[whole] * 6 + [smem],
        scratch=[pltpu.VMEM((32, TOK), F32)],
        after=(states,),
    )

    slices = call(pack1_body, shape((CHIPS, 32, DIM), BF16), (states, sib_state, keep, sibling(send)))
    got1 = exchange(slices)
    near_in = sibling(near)
    dk_in, dv_in, dq_in, rows = call(
        intra_body,
        [shape((TOK, 512), F32), shape((TOK, 512), F32), shape((512, TOK), F32), shape((32, TOK), F32)],
        (queries, key_vectors, value_vectors, grad_output, gates, reach_level),
        in_specs=[heads4] * 4 + [gates4, smem],
        out_specs=[heads4, heads4, rows4_tok, gates4],
        grid=(4,),
        scratch=[pltpu.VMEM((TOK, TOK), BF16), pltpu.VMEM((TOK, TOK), BF16)],
        cost=(2 * 10**9, 8 * 10**6),
        after=(slices,),
    )
    got2 = exchange(call(mid1_body, shape((CHIPS, 32, DIM), BF16), (got1,), after=(rows,)))
    mine = call(mid2_body, shape((1024, DIM), BF16), (got2,))
    other = sibling(mine)

    heads2 = pl.BlockSpec((TOK, 256), lambda h: (0, h))
    tok16 = pl.BlockSpec((16, TOK), lambda h: (h, 0))
    all768 = pl.BlockSpec((768, DIM), lambda h: (0, 0))
    dq_cross, grad_logits = call(
        cross_body,
        [shape((512, TOK), F32), shape((32, TOK), BF16)],
        (queries, grad_output, sib_state, mine, other, gates, reach_level, rows),
        in_specs=[
            heads2, heads2, pl.BlockSpec((256, DIM), lambda h: (h, 0)), all768, all768, tok16, smem, tok16,
        ],
        out_specs=[pl.BlockSpec((256, TOK), lambda h: (h, 0)), tok16],
        grid=(2,),
    )

    gl = [grad_logits] + [rotate(grad_logits, step) for step in range(1, 4)]
    grad_queries = call(
        queries_body, shape((TOK, 512), BF16), (dq_in, dq_cross),
        in_specs=[rows4_tok, rows4_tok], out_specs=heads4, grid=(4,),
    )
    half4 = pl.BlockSpec((DIM, DIM), lambda h: (6 + h % 2, 0))
    grad_keys, grad_values = call(
        final_body,
        [shape((TOK, 512), BF16)] * 2,
        (key_vectors, value_vectors, near_in, mine, other, dk_in, dv_in),
        in_specs=[heads4, heads4, rows4, half4, half4, heads4, heads4],
        out_specs=[heads4, heads4],
        grid=(4,),
        after=(grad_logits,),
    )
    w_keep, w_send = call(
        gradw_body, [shape((512, DIM), F32)] * 2, (layer_input, *gl),
        scratch=[pltpu.VMEM((DIM, TOK), BF16), pltpu.VMEM((1024, DIM), F32)],
        after=(grad_queries, grad_keys),
    )
    got3 = exchange(call(pack3_body, shape((CHIPS, 16, DIM), F32), (w_keep, sibling(w_send))))
    scale = 1.0 / math.sqrt(TOK * seq_count)
    sums = call(functools.partial(mid3_body, scale), shape((CHIPS, 16, DIM), BF16), (got3,))
    w_half = exchange(sums).reshape(512, DIM)
    grad_weight = call(join_body, shape((1024, DIM), F32), (w_half, sibling(w_half)))
    return grad_queries, grad_keys, grad_values, grad_weight


def solution(mesh):
    placed = (
        P("seq", "head"),
        P("head", None),
        P("seq", "head"),
        P("seq", "head"),
        P("seq", "head"),
        P("seq", "head"),
        P("seq"),
    )
    return jax.shard_map(
        shards,
        mesh=mesh,
        in_specs=placed,
        out_specs=(P("seq", "head"), P("seq", "head"), P("seq", "head"), P("head", None)),
        check_vma=False,
    )
```

```python
import functools
import math

import jax
import jax.numpy as jnp
from jax import lax
from jax.experimental import pallas as pl
from jax.experimental.pallas import tpu as pltpu
from jax.sharding import PartitionSpec as P

F32 = jnp.float32
BF16 = jnp.bfloat16
TOK = 512
DIM = 128
SPAN = 64
LEVELS = 8
CHIPS = 32
INV = 1.0 / DIM
VMEM_LIMIT = 24 * 1024 * 1024
VMEM_ALL = 60 * 1024 * 1024


def mm(left, right, left_dim=1, right_dim=0):
    return lax.dot_general(
        left, right, (((left_dim,), (right_dim,)), ((), ())), preferred_element_type=F32
    )


def aligned(index, size):
    return pl.ds(pl.multiple_of(index * size, size), size)


def call(
    body, out_shape, args, in_specs=None, out_specs=None, grid=(), scratch=(), cost=(10**7, 10**6), after=(),
    limit=VMEM_LIMIT,
):
    whole = pl.BlockSpec(memory_space=pltpu.VMEM)
    many = isinstance(out_shape, (tuple, list))
    used = len(args)
    in_specs = list(in_specs or [whole] * used) + [pl.BlockSpec(memory_space=pl.ANY)] * len(after)
    args = (*args, *after)

    def kernel(*refs):
        body(*refs[:used], *refs[len(args) :])

    return pl.pallas_call(
        kernel,
        out_shape=out_shape,
        grid=grid,
        in_specs=in_specs,
        out_specs=out_specs or ([whole] * len(out_shape) if many else whole),
        scratch_shapes=list(scratch),
        compiler_params=pltpu.CompilerParams(vmem_limit_bytes=limit),
        cost_estimate=pl.CostEstimate(flops=cost[0], bytes_accessed=cost[1], transcendentals=0),
    )(*args)


def shape(dims, dtype):
    return jax.ShapeDtypeStruct(dims, dtype)


def logits_body(x_ref, w_ref, o0, o1, o2, o3, scr):
    head = lax.axis_index("head")
    scr[...] = mm(w_ref[...], x_ref[...], 0, 1)
    for step, out in enumerate((o0, o1, o2, o3)):
        out[...] = scr[aligned(lax.rem(head + step, 4), 32), :]


def state_body(q_ref, k_ref, v_ref, reach_ref, state_ref, qt_ref, allowed_ref):
    state_ref[...] = mm(k_ref[...], v_ref[...], 0, 0) * INV
    qt_ref[...] = q_ref[...].astype(F32).T.astype(BF16)
    lane = lax.broadcasted_iota(jnp.int32, (LEVELS, TOK), 1) // SPAN
    level = lax.broadcasted_iota(jnp.int32, (LEVELS, TOK), 0)
    reach = jnp.zeros((LEVELS, TOK), jnp.int32)
    for span in range(TOK // SPAN):
        reach = jnp.where(lane == span, reach_ref[span], reach)
    allowed_ref[...] = (level <= reach).astype(F32)


def level_grads(qt_ref, g_ref, gates_ref, allowed, head, levels):
    lanes = aligned(head, DIM)
    query = qt_ref[lanes, :].astype(F32)
    weight = gates_ref[aligned(head, 8), :] * allowed
    gated = jnp.concatenate([(weight[level : level + 1, :] * query).astype(BF16) for level in levels], axis=0)
    return mm(gated, g_ref[:, lanes]) * INV


def level_send_body(qt_ref, g_ref, l0, l1, l2, l3, allowed_ref, gates_ref, send_ref):
    core = lax.axis_index("seq") & 1
    gates_ref[...] = jax.nn.sigmoid((l0[...] + l1[...]) + (l2[...] + l3[...]))
    allowed = allowed_ref[...]
    for slot in range(2):
        grads = level_grads(qt_ref, g_ref, gates_ref, allowed, 2 * (1 - core) + slot, range(5, 8))
        for level in range(3):
            row = 256 * level + DIM * slot
            send_ref[row : row + DIM, :] = grads[DIM * level : DIM * (level + 1)].astype(BF16)


def level_keep_body(qt_ref, g_ref, gates_ref, allowed_ref, near_ref, keep_ref):
    core = lax.axis_index("seq") & 1
    allowed = allowed_ref[...]
    for slot in range(2):
        head = 2 * core + slot
        grads = level_grads(qt_ref, g_ref, gates_ref, allowed, head, range(4, 8))
        near_ref[aligned(head, DIM), :] = grads[:DIM].astype(BF16)
        for level in range(3):
            row = 256 * level + DIM * slot
            keep_ref[row : row + DIM, :] = grads[DIM * (level + 1) : DIM * (level + 2)]
        head = 2 * (1 - core) + slot
        near_ref[aligned(head, DIM), :] = level_grads(qt_ref, g_ref, gates_ref, allowed, head, (4,)).astype(BF16)


def pack1_body(state_ref, sib_ref, keep_ref, recv_ref, o_ref, scr):
    core = lax.axis_index("seq") & 1
    half = aligned(core, 256)
    scr[0:256, :] = state_ref[half, :] + sib_ref[half, :]
    scr[256:1024, :] = keep_ref[...] + recv_ref[...].astype(F32)
    for chip in range(CHIPS):
        rows = [scr[256 * level + 8 * chip : 256 * level + 8 * chip + 8, :] for level in range(4)]
        o_ref[chip] = jnp.concatenate(rows, axis=0).astype(BF16)


def mid1_body(r_ref, o_ref):
    got = [r_ref[chip].astype(F32) for chip in range(CHIPS)]
    own = [part[0:8] for part in got]
    pairs = [own[chip] + own[chip ^ 1] for chip in range(CHIPS)]
    zero = jnp.zeros((8, DIM), F32)
    before = [zero]
    for group in range(7):
        before.append(before[-1] + (pairs[4 * group] + pairs[4 * group + 2]))
    after = [zero]
    for group in range(7, 0, -1):
        total = [got[4 * group + i][24:32] for i in range(4)]
        after.append(after[-1] + ((total[0] + total[1]) + (total[2] + total[3])))
    after = after[::-1]
    for chip in range(CHIPS):
        later = after[chip >> 2]
        if not chip & 2:
            later = later + (got[chip ^ 2][16:24] + got[chip ^ 3][16:24])
        if not chip & 1:
            later = later + got[chip ^ 1][8:16]
        rows = [
            own[chip ^ 1] if chip & 1 else zero,
            pairs[chip ^ 2] if chip & 2 else zero,
            before[chip >> 2],
            later,
        ]
        o_ref[chip] = jnp.concatenate(rows, axis=0).astype(BF16)


def mid2_body(r_ref, near_ref, o_ref):
    for chip in range(0, CHIPS, 2):
        got = [r_ref[chip + i].astype(F32) for i in range(2)]
        for level in range(4):
            both = [part[8 * level : 8 * level + 8] for part in got]
            row = 256 * level + 8 * chip
            o_ref[row : row + 16, :] = jnp.concatenate(both, axis=0).astype(BF16)
    o_ref[1024:1536, :] = near_ref[...]


def causal_masks():
    src = lax.broadcasted_iota(jnp.int32, (DIM, DIM), 0)
    dst = lax.broadcasted_iota(jnp.int32, (DIM, DIM), 1)
    same = (src // SPAN) == (dst // SPAN)
    return (same & (src <= dst)).astype(F32), ((src // SPAN) < (dst // SPAN)).astype(F32)


def intra_body(
    q_ref, k_ref, v_ref, g_ref, sib_ref, gates_ref, allowed_ref, dk_ref, dv_ref, dq_ref, rows_ref, p_scr, w_scr
):
    core = lax.axis_index("seq") & 1
    weight = gates_ref[...] * allowed_ref[...]
    mask0, mask1 = causal_masks()
    tiles = TOK // DIM
    key_t = k_ref[...].astype(F32).T.astype(BF16)
    query_t = q_ref[...].astype(F32).T
    near = (sib_ref[...] * (core == 1).astype(F32)).astype(BF16)
    projected = mm(near, g_ref[...], 1, 1)
    near_row = jnp.sum(query_t * projected, axis=0, keepdims=True)
    none = jnp.zeros((1, DIM), F32)
    for a in range(tiles):
        cols = slice(DIM * a, DIM * (a + 1))
        end = DIM * (a + 1)
        scores = mm(k_ref[:end, :], q_ref[cols, :], 1, 1) * INV
        probs = mm(v_ref[:end, :], g_ref[cols, :], 1, 1)
        prod = scores * probs
        sums = [none] * 8
        sums[4] = near_row[:, cols]
        weights = []
        for b in range(a):
            level = (a ^ b).bit_length() + 1
            sums[level] = sums[level] + jnp.sum(prod[DIM * b : DIM * (b + 1)], axis=0, keepdims=True)
            weights.append(jnp.broadcast_to(weight[level : level + 1, cols], (DIM, DIM)))
        sums[0] = jnp.sum(prod[DIM * a :] * mask0, axis=0, keepdims=True)
        sums[1] = jnp.sum(prod[DIM * a :] * mask1, axis=0, keepdims=True)
        weights.append(weight[0:1, cols] * mask0 + weight[1:2, cols] * mask1)
        rows_ref[:, cols] = jnp.concatenate(sums, axis=0)
        pair = jnp.concatenate(weights, axis=0)
        p_scr[:end, cols] = (pair * scores).astype(BF16)
        weighted = (pair * probs).astype(BF16)
        w_scr[:end, cols] = weighted
        dq_ref[:, cols] = mm(key_t[:, :end], weighted) * INV + weight[4:5, cols] * projected[:, cols]
    for b in range(tiles):
        rows = slice(DIM * b, DIM * (b + 1))
        start = DIM * b
        dv_ref[rows, :] = mm(p_scr[rows, start:], g_ref[start:, :])
        dk_ref[rows, :] = mm(w_scr[rows, start:], q_ref[start:, :]) * INV


def far_projection(head, g_ref, mine_ref, other_ref):
    core = lax.axis_index("seq") & 1
    states = []
    for level in range(3):
        at = slice(256 * level + DIM * (head % 2), 256 * level + DIM * (head % 2 + 1))
        states.append(jnp.where(head // 2 == core, mine_ref[at, :], other_ref[at, :]))
    projected = mm(jnp.concatenate(states, axis=0), g_ref[:, DIM * head : DIM * (head + 1)], 1, 1)
    return [projected[DIM * level : DIM * (level + 1)] for level in range(3)]


def cross_body(qt_ref, g_ref, mine_ref, other_ref, gates_ref, allowed_ref, rows_ref, gl_ref):
    allowed = allowed_ref[...]
    outs = []
    for head in range(4):
        query = qt_ref[DIM * head : DIM * (head + 1), :].astype(F32)
        parts = [jnp.zeros((5, TOK), F32)]
        for term in far_projection(head, g_ref, mine_ref, other_ref):
            parts.append(jnp.sum(query * term, axis=0, keepdims=True))
        gates = gates_ref[8 * head : 8 * head + 8, :]
        grads = (rows_ref[8 * head : 8 * head + 8, :] + jnp.concatenate(parts, axis=0)) * allowed
        outs.append(grads * gates * (1.0 - gates))
    gl_ref[...] = jnp.concatenate(outs, axis=0).astype(BF16)


def queries_body(g_ref, mine_ref, other_ref, gates_ref, allowed_ref, in_ref, dq_hbm, token_ref, dq_ref, sems):
    allowed = allowed_ref[...]
    copies = []
    for head in range(4):
        lanes = slice(DIM * head, DIM * (head + 1))
        weight = gates_ref[8 * head : 8 * head + 8, :] * allowed
        total = in_ref[lanes, :]
        for level, term in enumerate(far_projection(head, g_ref, mine_ref, other_ref)):
            total = total + weight[5 + level : 6 + level, :] * term
        dq_ref[:, lanes] = total.T.astype(BF16)
        copies.append(pltpu.make_async_copy(dq_ref.at[:, lanes], dq_hbm.at[:, lanes], sems.at[head]))
        copies[-1].start()
    token_ref[...] = jnp.zeros_like(token_ref)
    for copy in copies:
        copy.wait()


def gradw_body(x_ref, g0, g1, g2, g3, keep_ref, send_ref, scr, full):
    head = lax.axis_index("head")
    core = lax.axis_index("seq") & 1
    for step, part in enumerate((g0, g1, g2, g3)):
        scr[aligned(lax.rem(head + 4 - step, 4), 32), :] = part[...]
    full[...] = mm(scr[...], x_ref[...]).T
    keep_ref[...] = full[aligned(core, 512), :]
    send_ref[...] = full[aligned(1 - core, 512), :]


def pack3_body(keep_ref, recv_ref, o_ref):
    for chip in range(CHIPS):
        rows = slice(16 * chip, 16 * chip + 16)
        o_ref[chip] = keep_ref[rows, :] + recv_ref[rows, :]


def mid3_body(scale, r_ref, o_ref):
    total = r_ref[0]
    for chip in range(1, CHIPS):
        total = total + r_ref[chip]
    total = (total * scale).astype(BF16)
    for chip in range(CHIPS):
        o_ref[chip] = total


def finish_body(
    k_ref, v_ref, mine_ref, other_ref, dki_ref, dvi_ref, w_mine_ref, w_other_ref,
    dk_hbm, dv_hbm, w_hbm, dk_ref, dv_ref, w_ref, sems,
):
    core = lax.axis_index("seq") & 1
    w_ref[aligned(core, 512), :] = w_mine_ref[...].astype(F32)
    w_ref[aligned(1 - core, 512), :] = w_other_ref[...].astype(F32)
    copies = [pltpu.make_async_copy(w_ref, w_hbm, sems.at[8])]
    copies[0].start()
    for head in range(4):
        lanes = slice(DIM * head, DIM * (head + 1))
        part = slice(768 + DIM * (head % 2), 768 + DIM * (head % 2 + 1))
        later = jnp.where(head // 2 == core, mine_ref[part, :], other_ref[part, :]).astype(F32)
        near = other_ref[1024 + DIM * head : 1024 + DIM * (head + 1), :].astype(F32)
        later = (later + near * (core == 0).astype(F32)).astype(BF16)
        dk_ref[:, lanes] = (dki_ref[:, lanes] + mm(v_ref[:, lanes], later, 1, 1)).astype(BF16)
        copies.append(pltpu.make_async_copy(dk_ref.at[:, lanes], dk_hbm.at[:, lanes], sems.at[head]))
        copies[-1].start()
        dv_ref[:, lanes] = (dvi_ref[:, lanes] + mm(k_ref[:, lanes], later, 1, 0)).astype(BF16)
        copies.append(pltpu.make_async_copy(dv_ref.at[:, lanes], dv_hbm.at[:, lanes], sems.at[4 + head]))
        copies[-1].start()
    for copy in copies:
        copy.wait()


def shards(layer_input, gate_weight, queries, key_vectors, value_vectors, grad_output, reach_level):
    seq_count = lax.axis_size("seq")
    groups = [[2 * chip + c for chip in range(CHIPS)] for c in range(2)]
    swap = [(d, d ^ 1) for d in range(seq_count)]

    def sibling(value):
        return lax.ppermute(value, "seq", swap)

    def exchange(value):
        return lax.all_to_all(value, "seq", 0, 0, axis_index_groups=groups)

    def rotate(value, step):
        return lax.ppermute(value, "head", [(h, (h + step) % 4) for h in range(4)])

    whole = pl.BlockSpec(memory_space=pltpu.VMEM)
    smem = pl.BlockSpec(memory_space=pltpu.SMEM)
    hbm = pl.BlockSpec(memory_space=pl.ANY)

    block = pltpu.VMEM((TOK, 512), BF16)
    heads4 = pl.BlockSpec((TOK, DIM), lambda h: (0, h))
    gates4 = pl.BlockSpec((8, TOK), lambda h: (h, 0))
    rows4_tok = pl.BlockSpec((DIM, TOK), lambda h: (h, 0))
    first8 = pl.BlockSpec((8, TOK), lambda h: (0, 0))

    parts = call(
        logits_body, [shape((32, TOK), F32)] * 4, (layer_input, gate_weight), scratch=[pltpu.VMEM((DIM, TOK), F32)]
    )
    logits = [parts[0]] + [rotate(parts[step], step) for step in range(1, 4)]
    states, queries_t, allowed = call(
        state_body,
        [shape((512, DIM), F32), shape((512, TOK), BF16), shape((LEVELS, TOK), F32)],
        (queries, key_vectors, value_vectors, reach_level),
        in_specs=[heads4] * 3 + [smem],
        out_specs=[pl.BlockSpec((DIM, DIM), lambda h: (h, 0)), rows4_tok, first8],
        grid=(4,),
        after=(parts[0],),
    )
    sib_state = sibling(states)
    gates, send = call(
        level_send_body, [shape((32, TOK), F32), shape((768, DIM), BF16)],
        (queries_t, grad_output, *logits, allowed),
        after=(states,),
    )
    near, keep = call(
        level_keep_body, [shape((512, DIM), BF16), shape((768, DIM), F32)],
        (queries_t, grad_output, gates, allowed),
    )

    slices = call(
        pack1_body, shape((CHIPS, 32, DIM), BF16), (states, sib_state, keep, sibling(send)),
        scratch=[pltpu.VMEM((1024, DIM), F32)],
    )
    got1 = exchange(slices)
    dk_in, dv_in, dq_in, rows = call(
        intra_body,
        [shape((TOK, 512), F32), shape((TOK, 512), F32), shape((512, TOK), F32), shape((32, TOK), F32)],
        (queries, key_vectors, value_vectors, grad_output, sib_state, gates, allowed),
        in_specs=[heads4] * 4
        + [pl.BlockSpec((DIM, DIM), lambda h: (h, 0)), gates4, first8],
        out_specs=[heads4, heads4, rows4_tok, gates4],
        grid=(4,),
        scratch=[pltpu.VMEM((TOK, TOK), BF16), pltpu.VMEM((TOK, TOK), BF16)],
        cost=(2 * 10**9, 8 * 10**6),
        after=(slices,),
        limit=VMEM_ALL,
    )
    got2 = exchange(call(mid1_body, shape((CHIPS, 32, DIM), BF16), (got1,), after=(rows,)))
    mine = call(mid2_body, shape((1536, DIM), BF16), (got2, near))
    other = sibling(mine)
    grad_logits = call(
        cross_body, shape((32, TOK), BF16), (queries_t, grad_output, mine, other, gates, allowed, rows)
    )

    gl = [grad_logits] + [rotate(grad_logits, step) for step in range(1, 4)]
    grad_queries, token = call(
        queries_body, [shape((TOK, 512), BF16), shape((8, DIM), F32)],
        (grad_output, mine, other, gates, allowed, dq_in),
        out_specs=[hbm, whole],
        scratch=[block, pltpu.SemaphoreType.DMA((4,))],
        after=(grad_logits,),
    )
    w_keep, w_send = call(
        gradw_body, [shape((512, DIM), F32)] * 2, (layer_input, *gl),
        scratch=[pltpu.VMEM((DIM, TOK), BF16), pltpu.VMEM((1024, DIM), F32)],
        after=(token,),
    )
    got3 = exchange(call(pack3_body, shape((CHIPS, 16, DIM), F32), (w_keep, sibling(w_send))))
    scale = 1.0 / math.sqrt(TOK * seq_count)
    sums = call(functools.partial(mid3_body, scale), shape((CHIPS, 16, DIM), BF16), (got3,))
    w_half = exchange(sums).reshape(512, DIM)
    grad_keys, grad_values, grad_weight = call(
        finish_body,
        [shape((TOK, 512), BF16)] * 2 + [shape((1024, DIM), F32)],
        (key_vectors, value_vectors, mine, other, dk_in, dv_in, w_half, sibling(w_half)),
        out_specs=[hbm] * 3,
        scratch=[block, block, pltpu.VMEM((1024, DIM), F32), pltpu.SemaphoreType.DMA((9,))],
    )
    return grad_queries, grad_keys, grad_values, grad_weight


def solution(mesh):
    placed = (
        P("seq", "head"),
        P("head", None),
        P("seq", "head"),
        P("seq", "head"),
        P("seq", "head"),
        P("seq", "head"),
        P("seq"),
    )
    return jax.shard_map(
        shards,
        mesh=mesh,
        in_specs=placed,
        out_specs=(P("seq", "head"), P("seq", "head"), P("seq", "head"), P("head", None)),
        check_vma=False,
    )
```

```python
import functools
import math

import jax
import jax.numpy as jnp
from jax import lax
from jax.experimental import pallas as pl
from jax.experimental.pallas import tpu as pltpu
from jax.sharding import PartitionSpec as P

F32 = jnp.float32
BF16 = jnp.bfloat16
TOK = 512
DIM = 128
SPAN = 64
LEVELS = 8
CHIPS = 32
INV = 1.0 / DIM
VMEM_LIMIT = 24 * 1024 * 1024
VMEM_ALL = 60 * 1024 * 1024


def mm(left, right, left_dim=1, right_dim=0):
    return lax.dot_general(
        left, right, (((left_dim,), (right_dim,)), ((), ())), preferred_element_type=F32
    )


def aligned(index, size):
    return pl.ds(pl.multiple_of(index * size, size), size)


def call(
    body, out_shape, args, in_specs=None, out_specs=None, grid=(), scratch=(), cost=(10**7, 10**6), after=(),
    limit=VMEM_LIMIT,
):
    whole = pl.BlockSpec(memory_space=pltpu.VMEM)
    many = isinstance(out_shape, (tuple, list))
    used = len(args)
    in_specs = list(in_specs or [whole] * used) + [pl.BlockSpec(memory_space=pl.ANY)] * len(after)
    args = (*args, *after)

    def kernel(*refs):
        body(*refs[:used], *refs[len(args) :])

    return pl.pallas_call(
        kernel,
        out_shape=out_shape,
        grid=grid,
        in_specs=in_specs,
        out_specs=out_specs or ([whole] * len(out_shape) if many else whole),
        scratch_shapes=list(scratch),
        compiler_params=pltpu.CompilerParams(vmem_limit_bytes=limit),
        cost_estimate=pl.CostEstimate(flops=cost[0], bytes_accessed=cost[1], transcendentals=0),
    )(*args)


def shape(dims, dtype):
    return jax.ShapeDtypeStruct(dims, dtype)


def front_body(
    x_hbm, w_hbm, q_hbm, k_hbm, v_hbm, g_hbm, reach_ref, p0, p1, p2, p3, own_hbm, leaving_hbm,
    x_ref, w_ref, part_ref, own_ref, leaving_ref, in_sems, out_sems,
):
    head = lax.axis_index("head")
    core = lax.axis_index("seq") & 1
    ins, outs = [], []

    def load(src, dst):
        ins.append(pltpu.make_async_copy(src, dst, in_sems.at[len(ins)]))
        ins[-1].start()

    def store(src, dst):
        outs.append(pltpu.make_async_copy(src, dst, out_sems.at[len(outs)]))
        outs[-1].start()

    load(w_hbm, w_ref)
    load(x_hbm, x_ref)
    for side, ref in ((1 - core, leaving_ref), (core, own_ref)):
        for i, src in enumerate((q_hbm, k_hbm, v_hbm, g_hbm)):
            load(src.at[:, aligned(side, 256)], ref.at[pl.ds(TOK * i, TOK), :])
    lane = lax.broadcasted_iota(jnp.int32, (LEVELS, TOK), 1) // SPAN
    level = lax.broadcasted_iota(jnp.int32, (LEVELS, TOK), 0)
    reach = jnp.zeros((LEVELS, TOK), jnp.int32)
    for span in range(TOK // SPAN):
        reach = jnp.where(lane == span, reach_ref[span], reach)
    allowed = (level <= reach).astype(F32)
    allowed = jnp.concatenate([allowed[:, :256], allowed[:, 256:]], axis=0).astype(BF16)
    leaving_ref[4 * TOK :, :] = allowed
    own_ref[4 * TOK :, :] = allowed
    ins[0].wait()
    ins[1].wait()
    part_ref[...] = mm(w_ref[...], x_ref[...], 0, 1)
    for step, out in enumerate((p0, p1, p2, p3)):
        store(part_ref.at[aligned(lax.rem(head + step, 4), 32), :], out)
    for copy in ins[2:6]:
        copy.wait()
    store(leaving_ref, leaving_hbm)
    for copy in ins[6:]:
        copy.wait()
    store(own_ref, own_hbm)
    for copy in outs:
        copy.wait()


def gather_body(l0, l1, l2, l3, keep_ref, send_ref):
    core = lax.axis_index("seq") & 1
    keep = aligned(core, 16)
    send = aligned(1 - core, 16)
    keep_ref[...] = (l0[keep, :] + l1[keep, :]) + (l2[keep, :] + l3[keep, :])
    send_ref[...] = (l0[send, :] + l1[send, :]) + (l2[send, :] + l3[send, :])


Q, K, V, G = (slice(TOK * i, TOK * (i + 1)) for i in range(4))


def state_body(own_ref, sib_ref, so_ref, ss_ref, qto_ref, qts_ref, ao_ref, as_ref):
    for ref, state, query_t, mask in ((own_ref, so_ref, qto_ref, ao_ref), (sib_ref, ss_ref, qts_ref, as_ref)):
        for i in range(2):
            lanes = slice(DIM * i, DIM * (i + 1))
            state[lanes, :] = mm(ref[K, lanes], ref[V, lanes], 0, 0) * INV
            query_t[lanes, :] = ref[Q, lanes].astype(F32).T.astype(BF16)
        allowed = ref[4 * TOK :, :].astype(F32)
        mask[...] = jnp.concatenate([allowed[:8], allowed[8:]], axis=1)


def span_masks():
    src = lax.broadcasted_iota(jnp.int32, (256, 256), 0)
    dst = lax.broadcasted_iota(jnp.int32, (256, 256), 1)
    near, far = src // SPAN, dst // SPAN
    return [
        ((near == far) & (src <= dst)).astype(F32),
        ((near < far) & (near // 2 == far // 2)).astype(F32),
        (near // 2 < far // 2).astype(F32),
    ]


def rows_body(own_ref, sib_ref, qto_ref, qts_ref, so_ref, ss_ref, ro_ref, rs_ref):
    core = lax.axis_index("seq") & 1
    masks = span_masks()
    none = jnp.zeros((1, 256), F32)
    for block, (ref, query_t, state, out) in enumerate(
        ((own_ref, qto_ref, ss_ref, ro_ref), (sib_ref, qts_ref, so_ref, rs_ref))
    ):
        upper = (core != block).astype(F32)
        for i in range(2):
            lanes = slice(DIM * i, DIM * (i + 1))
            near = (state[lanes, :] * upper).astype(BF16)
            projected = mm(near, ref[G, lanes], 1, 1)
            near_row = jnp.sum(query_t[lanes, :].astype(F32) * projected, axis=0, keepdims=True)
            for a in range(2):
                cols = slice(256 * a, 256 * a + 256)
                end = 256 * a + 256
                scores = mm(ref[TOK : TOK + end, lanes], ref[cols, lanes], 1, 1) * INV
                prod = scores * mm(ref[2 * TOK : 2 * TOK + end, lanes], ref[3 * TOK + 256 * a : 3 * TOK + end, lanes], 1, 1)
                diagonal = prod[256 * a :]
                sums = [jnp.sum(diagonal * mask, axis=0, keepdims=True) for mask in masks]
                sums.append(jnp.sum(prod[:256], axis=0, keepdims=True) if a else none)
                sums.append(near_row[:, cols])
                out[8 * i : 8 * i + 8, cols] = jnp.concatenate(sums + [none] * 3, axis=0)


def level_body(
    own_ref, sib_ref, qto_ref, qts_ref, ao_ref, as_ref, so_ref, ss_ref, lo_ref, ls_ref,
    go_ref, gs_ref, near_ref, o_ref, scr,
):
    core = lax.axis_index("seq") & 1
    gates = [jax.nn.sigmoid(lo_ref[...]), jax.nn.sigmoid(ls_ref[...])]
    go_ref[...] = gates[0]
    gs_ref[...] = gates[1]
    scr[0:256, :] = so_ref[...] + ss_ref[...]
    for i in range(2):
        lanes = slice(DIM * i, DIM * (i + 1))
        grads = []
        for block, (ref, query_t, mask) in enumerate(((own_ref, qto_ref, ao_ref), (sib_ref, qts_ref, as_ref))):
            query = query_t[lanes, :].astype(F32)
            weight = gates[block][8 * i : 8 * i + 8] * mask[...]
            gated = [(weight[level : level + 1, :] * query).astype(BF16) for level in range(4, 8)]
            grads.append(mm(jnp.concatenate(gated, axis=0), ref[G, lanes]))
        near_ref[lanes, :] = jnp.where(core == 1, grads[0][:DIM], grads[1][:DIM]) * INV
        total = (grads[0][DIM:] + grads[1][DIM:]) * INV
        for level in range(3):
            row = 256 * (level + 1) + DIM * i
            scr[row : row + DIM, :] = total[DIM * level : DIM * (level + 1)]
    for chip in range(CHIPS):
        rows = [scr[256 * level + 8 * chip : 256 * level + 8 * chip + 8, :] for level in range(4)]
        o_ref[chip] = jnp.concatenate(rows, axis=0).astype(BF16)


def mid1_body(r_ref, o_ref):
    got = [r_ref[chip].astype(F32) for chip in range(CHIPS)]
    own = [part[0:8] for part in got]
    pairs = [own[chip] + own[chip ^ 1] for chip in range(CHIPS)]
    zero = jnp.zeros((8, DIM), F32)
    before = [zero]
    for group in range(7):
        before.append(before[-1] + (pairs[4 * group] + pairs[4 * group + 2]))
    after = [zero]
    for group in range(7, 0, -1):
        total = [got[4 * group + i][24:32] for i in range(4)]
        after.append(after[-1] + ((total[0] + total[1]) + (total[2] + total[3])))
    after = after[::-1]
    for chip in range(CHIPS):
        later = after[chip >> 2]
        if not chip & 2:
            later = later + (got[chip ^ 2][16:24] + got[chip ^ 3][16:24])
        if not chip & 1:
            later = later + got[chip ^ 1][8:16]
        rows = [
            own[chip ^ 1] if chip & 1 else zero,
            pairs[chip ^ 2] if chip & 2 else zero,
            before[chip >> 2],
            later,
        ]
        o_ref[chip] = jnp.concatenate(rows, axis=0).astype(BF16)


def mid2_body(r_ref, o_ref):
    for chip in range(0, CHIPS, 2):
        got = [r_ref[chip + i].astype(F32) for i in range(2)]
        for level in range(4):
            both = [part[8 * level : 8 * level + 8] for part in got]
            row = 256 * level + 8 * chip
            o_ref[row : row + 16, :] = jnp.concatenate(both, axis=0).astype(BF16)


def far_projection(i, ref, mine_ref):
    lanes = slice(DIM * i, DIM * (i + 1))
    states = [mine_ref[256 * level + DIM * i : 256 * level + DIM * (i + 1), :] for level in range(3)]
    projected = mm(jnp.concatenate(states, axis=0), ref[G, lanes], 1, 1)
    return [projected[DIM * level : DIM * (level + 1)] for level in range(3)]


def cross_body(
    own_ref, sib_ref, qto_ref, qts_ref, ao_ref, as_ref, go_ref, gs_ref, ro_ref, rs_ref, mine_ref, gl_ref
):
    outs = []
    for ref, query_t, mask, gates_ref, rows_ref in (
        (own_ref, qto_ref, ao_ref, go_ref, ro_ref), (sib_ref, qts_ref, as_ref, gs_ref, rs_ref),
    ):
        for i in range(2):
            query = query_t[DIM * i : DIM * (i + 1), :].astype(F32)
            parts = [jnp.zeros((5, TOK), F32)]
            for term in far_projection(i, ref, mine_ref):
                parts.append(jnp.sum(query * term, axis=0, keepdims=True))
            rows = slice(8 * i, 8 * i + 8)
            gates = gates_ref[rows, :]
            grads = (rows_ref[rows, :] + jnp.concatenate(parts, axis=0)) * mask[...]
            outs.append(grads * gates * (1.0 - gates))
    gl_ref[...] = jnp.concatenate(outs, axis=0).astype(BF16)


def tail_body(block, blk_ref, state_ref, near_ref, mask_ref, gates_ref, mine_ref, out_ref, token_ref):
    core = lax.axis_index("seq") & 1
    masks = span_masks()
    upper = (core != block).astype(F32)
    for i in range(2):
        lanes = slice(DIM * i, DIM * (i + 1))
        query, key, value, grad = blk_ref[Q, lanes], blk_ref[K, lanes], blk_ref[V, lanes], blk_ref[G, lanes]
        weight = gates_ref[8 * i : 8 * i + 8, :] * mask_ref[...]
        key_t = key.astype(F32).T.astype(BF16)
        states = [(state_ref[lanes, :] * upper).astype(BF16)]
        for level in range(3):
            states.append(mine_ref[256 * level + DIM * i : 256 * level + DIM * (i + 1), :])
        projected = mm(jnp.concatenate(states, axis=0), grad, 1, 1)
        later = mine_ref[768 + DIM * i : 768 + DIM * (i + 1), :].astype(F32)
        later = (later + near_ref[lanes, :] * (1.0 - upper)).astype(BF16)
        dk = mm(value, later, 1, 1)
        dv = mm(key, later)
        for a in range(2):
            cols = slice(256 * a, 256 * a + 256)
            end = 256 * a + 256
            pair = sum(weight[level : level + 1, cols] * masks[level] for level in range(3))
            if a:
                pair = jnp.concatenate([jnp.broadcast_to(weight[3:4, cols], (256, 256)), pair], axis=0)
            scored = (pair * (mm(key[:end], query[cols], 1, 1) * INV)).astype(BF16)
            weighted = (pair * mm(value[:end], grad[cols], 1, 1)).astype(BF16)
            total = mm(key_t[:, :end], weighted) * INV
            for level in range(4):
                total = total + weight[4 + level : 5 + level, cols] * projected[DIM * level : DIM * (level + 1), cols]
            out_ref[cols, lanes] = total.T.astype(BF16)
            more_k = mm(weighted, query[cols]) * INV
            more_v = mm(scored, grad[cols])
            if a:
                dk, dv = dk + more_k, dv + more_v
            else:
                dk = jnp.concatenate([dk[:256] + more_k, dk[256:]], axis=0)
                dv = jnp.concatenate([dv[:256] + more_v, dv[256:]], axis=0)
        out_ref[K, lanes] = dk.astype(BF16)
        out_ref[V, lanes] = dv.astype(BF16)
    token_ref[...] = jnp.zeros_like(token_ref)


def gradw_body(xo_ref, xs_ref, g0, g1, g2, g3, o_ref, own_scr, sib_scr, full):
    head = lax.axis_index("head")
    for step, part in enumerate((g0, g1, g2, g3)):
        rows = aligned(lax.rem(head + 4 - step, 4), 16)
        own_scr[rows, :] = part[0:16, :]
        sib_scr[rows, :] = part[16:32, :]
    full[...] = mm(own_scr[...], xo_ref[...]) + mm(sib_scr[...], xs_ref[...])
    for chip in range(CHIPS):
        group, block = chip % 4, chip // 4
        o_ref[chip] = full[16 * group : 16 * group + 16, DIM * block : DIM * (block + 1)]


def mid3_body(scale, r_ref, o_ref):
    total = r_ref[0]
    for chip in range(1, CHIPS):
        total = total + r_ref[chip]
    total = (total * scale).astype(BF16)
    for chip in range(CHIPS):
        o_ref[chip] = total


def place_body(own_ref, recv_ref, dq_hbm, dk_hbm, dv_hbm, sems):
    core = lax.axis_index("seq") & 1
    copies = []
    for i, out in enumerate((dq_hbm, dk_hbm, dv_hbm)):
        rows = pl.ds(TOK * i, TOK)
        copies.append(pltpu.make_async_copy(own_ref.at[rows, :], out.at[:, aligned(core, 256)], sems.at[2 * i]))
        copies.append(pltpu.make_async_copy(recv_ref.at[rows, :], out.at[:, aligned(1 - core, 256)], sems.at[2 * i + 1]))
    for copy in copies:
        copy.start()
    for copy in copies:
        copy.wait()


def join_body(w_mine_ref, w_other_ref, w_hbm, full, w_ref, sems):
    core = lax.axis_index("seq") & 1
    copies = []
    for block in range(8):
        lanes = slice(DIM * block, DIM * (block + 1))
        for group in range(4):
            full[aligned(2 * group + core, 16), :] = w_mine_ref[4 * block + group].astype(F32)
            full[aligned(2 * group + 1 - core, 16), :] = w_other_ref[4 * block + group].astype(F32)
        w_ref[lanes, :] = full[...].T
        if block % 4 == 3:
            rows = pl.ds(512 * (block // 4), 512)
            copies.append(pltpu.make_async_copy(w_ref.at[rows, :], w_hbm.at[rows, :], sems.at[block // 4]))
            copies[-1].start()
    for copy in copies:
        copy.wait()


def shards(layer_input, gate_weight, queries, key_vectors, value_vectors, grad_output, reach_level):
    seq_count = lax.axis_size("seq")
    groups = [[2 * chip + c for chip in range(CHIPS)] for c in range(2)]
    swap = [(d, d ^ 1) for d in range(seq_count)]

    def sibling(value):
        return lax.ppermute(value, "seq", swap)

    def exchange(value):
        return lax.all_to_all(value, "seq", 0, 0, axis_index_groups=groups)

    def rotate(value, step):
        return lax.ppermute(value, "head", [(h, (h + step) % 4) for h in range(4)])

    whole = pl.BlockSpec(memory_space=pltpu.VMEM)
    smem = pl.BlockSpec(memory_space=pltpu.SMEM)
    hbm = pl.BlockSpec(memory_space=pl.ANY)

    tok16 = shape((16, TOK), F32)
    mask8 = shape((LEVELS, TOK), F32)
    half = shape((256, DIM), F32)

    *parts, own, leaving = call(
        front_body,
        [shape((32, TOK), F32)] * 4 + [shape((4 * TOK + 16, 256), BF16)] * 2,
        (layer_input, gate_weight, queries, key_vectors, value_vectors, grad_output, reach_level),
        in_specs=[hbm] * 6 + [smem],
        out_specs=[hbm] * 6,
        scratch=[
            pltpu.VMEM((TOK, 1024), BF16), pltpu.VMEM((1024, DIM), BF16), pltpu.VMEM((DIM, TOK), F32),
            pltpu.VMEM((4 * TOK + 16, 256), BF16), pltpu.VMEM((4 * TOK + 16, 256), BF16),
            pltpu.SemaphoreType.DMA((10,)), pltpu.SemaphoreType.DMA((6,)),
        ],
        limit=VMEM_ALL,
    )
    logits = [parts[0]] + [rotate(parts[step], step) for step in range(1, 4)]
    sib = sibling(leaving)
    sib_input = sibling(layer_input)
    state_own, state_sib, qt_own, qt_sib, allow_own, allow_sib = call(
        state_body, [half, half, shape((256, TOK), BF16), shape((256, TOK), BF16), mask8, mask8], (own, sib)
    )
    rows_own, rows_sib = call(
        rows_body, [tok16, tok16], (own, sib, qt_own, qt_sib, state_own, state_sib)
    )
    logits_own, logits_send = call(gather_body, [tok16, tok16], tuple(logits), after=(rows_own,))

    gates_own, gates_sib, near, slices = call(
        level_body, [tok16, tok16, half, shape((CHIPS, 32, DIM), BF16)],
        (own, sib, qt_own, qt_sib, allow_own, allow_sib, state_own, state_sib, logits_own, sibling(logits_send)),
        scratch=[pltpu.VMEM((1024, DIM), F32)],
        after=(sib_input,),
    )
    got1 = exchange(slices)

    got2 = exchange(call(mid1_body, shape((CHIPS, 32, DIM), BF16), (got1,)))
    mine = call(mid2_body, shape((1024, DIM), BF16), (got2,))
    grad_logits = call(
        cross_body, shape((32, TOK), BF16),
        (own, sib, qt_own, qt_sib, allow_own, allow_sib, gates_own, gates_sib, rows_own, rows_sib, mine),
    )

    gl = [grad_logits] + [rotate(grad_logits, step) for step in range(1, 4)]
    def tail(which, blk, state, allowed, gates, after):
        return call(
            functools.partial(tail_body, which), [shape((3 * TOK, 256), BF16), shape((8, DIM), F32)],
            (blk, state, near, allowed, gates, mine), after=after, cost=(4 * 10**9, 16 * 10**6),
        )

    out_sib, token = tail(1, sib, state_own, allow_sib, gates_sib, (grad_logits,))
    out_recv = sibling(out_sib)
    out_own, token = tail(0, own, state_sib, allow_own, gates_own, (token,))
    slices = call(
        gradw_body, shape((CHIPS, 16, DIM), F32), (layer_input, sib_input, *gl),
        scratch=[pltpu.VMEM((64, TOK), BF16), pltpu.VMEM((64, TOK), BF16), pltpu.VMEM((64, 1024), F32)],
        after=(token,),
    )
    got3 = exchange(slices)
    scale = 1.0 / math.sqrt(TOK * seq_count)
    w_half = exchange(call(functools.partial(mid3_body, scale), shape((CHIPS, 16, DIM), BF16), (got3,)))
    grads = call(
        place_body, [shape((TOK, 512), BF16)] * 3, (out_own, out_recv),
        out_specs=[hbm] * 3, scratch=[pltpu.SemaphoreType.DMA((6,))], after=(w_half,),
    )
    grad_weight = call(
        join_body, shape((1024, DIM), F32), (w_half, sibling(w_half)),
        out_specs=hbm,
        scratch=[pltpu.VMEM((DIM, DIM), F32), pltpu.VMEM((1024, DIM), F32), pltpu.SemaphoreType.DMA((2,))],
    )
    return (*grads, grad_weight)


def solution(mesh):
    placed = (
        P("seq", "head"),
        P("head", None),
        P("seq", "head"),
        P("seq", "head"),
        P("seq", "head"),
        P("seq", "head"),
        P("seq"),
    )
    return jax.shard_map(
        shards,
        mesh=mesh,
        in_specs=placed,
        out_specs=(P("seq", "head"), P("seq", "head"), P("seq", "head"), P("head", None)),
        check_vma=False,
    )
```

```python
import functools
import math

import jax
import jax.numpy as jnp
from jax import lax
from jax.experimental import pallas as pl
from jax.experimental.pallas import tpu as pltpu
from jax.sharding import PartitionSpec as P

F32 = jnp.float32
BF16 = jnp.bfloat16
TOK = 512
DIM = 128
SPAN = 64
LEVELS = 8
CHIPS = 32
INV = 1.0 / DIM
VMEM_LIMIT = 24 * 1024 * 1024
VMEM_ALL = 60 * 1024 * 1024


def mm(left, right, left_dim=1, right_dim=0):
    return lax.dot_general(
        left, right, (((left_dim,), (right_dim,)), ((), ())), preferred_element_type=F32
    )


def aligned(index, size):
    return pl.ds(pl.multiple_of(index * size, size), size)


def call(
    body, out_shape, args, in_specs=None, out_specs=None, grid=(), scratch=(), cost=(10**7, 10**6), after=(),
    limit=VMEM_LIMIT,
):
    whole = pl.BlockSpec(memory_space=pltpu.VMEM)
    many = isinstance(out_shape, (tuple, list))
    used = len(args)
    in_specs = list(in_specs or [whole] * used) + [pl.BlockSpec(memory_space=pl.ANY)] * len(after)
    args = (*args, *after)

    def kernel(*refs):
        body(*refs[:used], *refs[len(args) :])

    return pl.pallas_call(
        kernel,
        out_shape=out_shape,
        grid=grid,
        in_specs=in_specs,
        out_specs=out_specs or ([whole] * len(out_shape) if many else whole),
        scratch_shapes=list(scratch),
        compiler_params=pltpu.CompilerParams(vmem_limit_bytes=limit),
        cost_estimate=pl.CostEstimate(flops=cost[0], bytes_accessed=cost[1], transcendentals=0),
    )(*args)


def shape(dims, dtype):
    return jax.ShapeDtypeStruct(dims, dtype)


def front_body(
    x_hbm, w_hbm, q_hbm, k_hbm, v_hbm, g_hbm, reach_hbm, p0, p1, p2, p3, own_hbm, leaving_hbm,
    x_ref, w_ref, part_ref, own_ref, leaving_ref, reach_ref, in_sems, out_sems,
):
    head = lax.axis_index("head")
    core = lax.axis_index("seq") & 1
    ins, outs = [], []

    def load(src, dst):
        ins.append(pltpu.make_async_copy(src, dst, in_sems.at[len(ins)]))
        ins[-1].start()

    def store(src, dst):
        outs.append(pltpu.make_async_copy(src, dst, out_sems.at[len(outs)]))
        outs[-1].start()

    load(w_hbm, w_ref)
    load(x_hbm, x_ref)
    for side, ref in ((1 - core, leaving_ref), (core, own_ref)):
        for i, src in enumerate((q_hbm, k_hbm, v_hbm, g_hbm)):
            load(src.at[:, aligned(side, 256)], ref.at[pl.ds(TOK * i, TOK), :])
    load(reach_hbm, reach_ref)
    ins[0].wait()
    ins[1].wait()
    part_ref[...] = mm(w_ref[...], x_ref[...], 0, 1)
    for step, out in enumerate((p0, p1, p2, p3)):
        store(part_ref.at[aligned(lax.rem(head + step, 4), 32), :], out)
    ins[10].wait()
    lane = lax.broadcasted_iota(jnp.int32, (LEVELS, TOK), 1) // SPAN
    level = lax.broadcasted_iota(jnp.int32, (LEVELS, TOK), 0)
    reach = jnp.zeros((LEVELS, TOK), jnp.int32)
    for span in range(TOK // SPAN):
        reach = jnp.where(lane == span, reach_ref[span], reach)
    allowed = (level <= reach).astype(F32)
    allowed = jnp.concatenate([allowed[:, :256], allowed[:, 256:]], axis=0).astype(BF16)
    leaving_ref[4 * TOK :, :] = allowed
    own_ref[4 * TOK :, :] = allowed
    for copy in ins[2:6]:
        copy.wait()
    store(leaving_ref, leaving_hbm)
    for copy in ins[6:10]:
        copy.wait()
    store(own_ref, own_hbm)
    for copy in outs:
        copy.wait()


def gather_body(l0, l1, l2, l3, keep_ref, send_ref):
    core = lax.axis_index("seq") & 1
    keep = aligned(core, 16)
    send = aligned(1 - core, 16)
    keep_ref[...] = (l0[keep, :] + l1[keep, :]) + (l2[keep, :] + l3[keep, :])
    send_ref[...] = (l0[send, :] + l1[send, :]) + (l2[send, :] + l3[send, :])


Q, K, V, G = (slice(TOK * i, TOK * (i + 1)) for i in range(4))


def state_body(own_ref, sib_ref, so_ref, ss_ref, qto_ref, qts_ref, kto_ref, kts_ref, ao_ref, as_ref):
    for ref, state, query_t, key_t, mask in (
        (own_ref, so_ref, qto_ref, kto_ref, ao_ref), (sib_ref, ss_ref, qts_ref, kts_ref, as_ref),
    ):
        for i in range(2):
            lanes = slice(DIM * i, DIM * (i + 1))
            state[lanes, :] = mm(ref[K, lanes], ref[V, lanes], 0, 0) * INV
            query_t[lanes, :] = ref[Q, lanes].T
            key_t[lanes, :] = ref[K, lanes].T
        allowed = ref[4 * TOK :, :].astype(F32)
        mask[...] = jnp.concatenate([allowed[:8], allowed[8:]], axis=1)


def span_masks():
    src = lax.broadcasted_iota(jnp.int32, (256, 256), 0)
    dst = lax.broadcasted_iota(jnp.int32, (256, 256), 1)
    near, far = src // SPAN, dst // SPAN
    return [
        ((near == far) & (src <= dst)).astype(F32),
        ((near < far) & (near // 2 == far // 2)).astype(F32),
        (near // 2 < far // 2).astype(F32),
    ]


def rows_body(own_ref, sib_ref, qto_ref, qts_ref, so_ref, ss_ref, ro_ref, rs_ref, sco_ref, pro_ref, scs_ref, prs_ref):
    core = lax.axis_index("seq") & 1
    masks = span_masks()
    none = jnp.zeros((1, 256), F32)
    for block, (ref, query_t, state, out, score_ref, prob_ref) in enumerate((
        (own_ref, qto_ref, ss_ref, ro_ref, sco_ref, pro_ref), (sib_ref, qts_ref, so_ref, rs_ref, scs_ref, prs_ref),
    )):
        upper = (core != block).astype(F32)
        for i in range(2):
            lanes = slice(DIM * i, DIM * (i + 1))
            near = (state[lanes, :] * upper).astype(BF16)
            projected = mm(near, ref[G, lanes], 1, 1)
            near_row = jnp.sum(query_t[lanes, :].astype(F32) * projected, axis=0, keepdims=True)
            for a in range(2):
                cols = slice(256 * a, 256 * a + 256)
                end = 256 * a + 256
                scores = mm(ref[TOK : TOK + end, lanes], ref[cols, lanes], 1, 1) * INV
                probs = mm(ref[2 * TOK : 2 * TOK + end, lanes], ref[3 * TOK + 256 * a : 3 * TOK + end, lanes], 1, 1)
                kept = slice(768 * i + 256 * a, 768 * i + 256 * a + end)
                score_ref[kept, :] = scores
                prob_ref[kept, :] = probs
                prod = scores * probs
                diagonal = prod[256 * a :]
                sums = [jnp.sum(diagonal * mask, axis=0, keepdims=True) for mask in masks]
                sums.append(jnp.sum(prod[:256], axis=0, keepdims=True) if a else none)
                sums.append(near_row[:, cols])
                out[8 * i : 8 * i + 8, cols] = jnp.concatenate(sums + [none] * 3, axis=0)


def level_body(
    own_ref, sib_ref, qto_ref, qts_ref, ao_ref, as_ref, so_ref, ss_ref, lo_ref, ls_ref,
    go_ref, gs_ref, near_ref, o_ref, scr,
):
    core = lax.axis_index("seq") & 1
    gates = [jax.nn.sigmoid(lo_ref[...]), jax.nn.sigmoid(ls_ref[...])]
    go_ref[...] = gates[0]
    gs_ref[...] = gates[1]
    scr[0:256, :] = so_ref[...] + ss_ref[...]
    for i in range(2):
        lanes = slice(DIM * i, DIM * (i + 1))
        grads = []
        for block, (ref, query_t, mask) in enumerate(((own_ref, qto_ref, ao_ref), (sib_ref, qts_ref, as_ref))):
            query = query_t[lanes, :].astype(F32)
            weight = gates[block][8 * i : 8 * i + 8] * mask[...]
            gated = [(weight[level : level + 1, :] * query).astype(BF16) for level in range(4, 8)]
            grads.append(mm(jnp.concatenate(gated, axis=0), ref[G, lanes]))
        near_ref[lanes, :] = jnp.where(core == 1, grads[0][:DIM], grads[1][:DIM]) * INV
        total = (grads[0][DIM:] + grads[1][DIM:]) * INV
        for level in range(3):
            row = 256 * (level + 1) + DIM * i
            scr[row : row + DIM, :] = total[DIM * level : DIM * (level + 1)]
    for chip in range(CHIPS):
        rows = [scr[256 * level + 8 * chip : 256 * level + 8 * chip + 8, :] for level in range(4)]
        o_ref[chip] = jnp.concatenate(rows, axis=0).astype(BF16)


def mid1_body(r_ref, o_ref):
    got = [r_ref[chip].astype(F32) for chip in range(CHIPS)]
    own = [part[0:8] for part in got]
    pairs = [own[chip] + own[chip ^ 1] for chip in range(CHIPS)]
    zero = jnp.zeros((8, DIM), F32)
    before = [zero]
    for group in range(7):
        before.append(before[-1] + (pairs[4 * group] + pairs[4 * group + 2]))
    after = [zero]
    for group in range(7, 0, -1):
        total = [got[4 * group + i][24:32] for i in range(4)]
        after.append(after[-1] + ((total[0] + total[1]) + (total[2] + total[3])))
    after = after[::-1]
    for chip in range(CHIPS):
        later = after[chip >> 2]
        if not chip & 2:
            later = later + (got[chip ^ 2][16:24] + got[chip ^ 3][16:24])
        if not chip & 1:
            later = later + got[chip ^ 1][8:16]
        rows = [
            own[chip ^ 1] if chip & 1 else zero,
            pairs[chip ^ 2] if chip & 2 else zero,
            before[chip >> 2],
            later,
        ]
        o_ref[chip] = jnp.concatenate(rows, axis=0).astype(BF16)


def mid2_body(r_ref, o_ref):
    for chip in range(0, CHIPS, 2):
        got = [r_ref[chip + i].astype(F32) for i in range(2)]
        for level in range(4):
            both = [part[8 * level : 8 * level + 8] for part in got]
            row = 256 * level + 8 * chip
            o_ref[row : row + 16, :] = jnp.concatenate(both, axis=0).astype(BF16)


def far_projection(i, ref, mine_ref):
    lanes = slice(DIM * i, DIM * (i + 1))
    states = [mine_ref[256 * level + DIM * i : 256 * level + DIM * (i + 1), :] for level in range(3)]
    projected = mm(jnp.concatenate(states, axis=0), ref[G, lanes], 1, 1)
    return [projected[DIM * level : DIM * (level + 1)] for level in range(3)]


def cross_body(
    own_ref, sib_ref, qto_ref, qts_ref, ao_ref, as_ref, go_ref, gs_ref, ro_ref, rs_ref, mine_ref, gl_ref, co_ref, cs_ref
):
    outs = []
    for ref, query_t, mask, gates_ref, rows_ref, cross_ref in (
        (own_ref, qto_ref, ao_ref, go_ref, ro_ref, co_ref), (sib_ref, qts_ref, as_ref, gs_ref, rs_ref, cs_ref),
    ):
        for i in range(2):
            query = query_t[DIM * i : DIM * (i + 1), :].astype(F32)
            rows = slice(8 * i, 8 * i + 8)
            gates = gates_ref[rows, :]
            weight = gates * mask[...]
            parts = [jnp.zeros((5, TOK), F32)]
            total = None
            for level, term in enumerate(far_projection(i, ref, mine_ref)):
                parts.append(jnp.sum(query * term, axis=0, keepdims=True))
                weighted = weight[5 + level : 6 + level, :] * term
                total = weighted if total is None else total + weighted
            cross_ref[DIM * i : DIM * (i + 1), :] = total
            grads = (rows_ref[rows, :] + jnp.concatenate(parts, axis=0)) * mask[...]
            outs.append(grads * gates * (1.0 - gates))
    gl_ref[...] = jnp.concatenate(outs, axis=0).astype(BF16)


def tail_body(
    block, blk_ref, kt_ref, state_ref, near_ref, mask_ref, gates_ref, mine_ref, cross_ref, score_ref, prob_ref,
    out_ref, token_ref,
):
    core = lax.axis_index("seq") & 1
    masks = span_masks()
    upper = (core != block).astype(F32)
    for i in range(2):
        lanes = slice(DIM * i, DIM * (i + 1))
        query, key, value, grad = blk_ref[Q, lanes], blk_ref[K, lanes], blk_ref[V, lanes], blk_ref[G, lanes]
        weight = gates_ref[8 * i : 8 * i + 8, :] * mask_ref[...]
        near = mm((state_ref[lanes, :] * upper).astype(BF16), grad, 1, 1)
        later = mine_ref[768 + DIM * i : 768 + DIM * (i + 1), :].astype(F32)
        later = (later + near_ref[lanes, :] * (1.0 - upper)).astype(BF16)
        dk = mm(value, later, 1, 1)
        dv = mm(key, later)
        for a in range(2):
            cols = slice(256 * a, 256 * a + 256)
            end = 256 * a + 256
            kept = slice(768 * i + 256 * a, 768 * i + 256 * a + end)
            pair = sum(weight[level : level + 1, cols] * masks[level] for level in range(3))
            if a:
                pair = jnp.concatenate([jnp.broadcast_to(weight[3:4, cols], (256, 256)), pair], axis=0)
            scored = (pair * score_ref[kept, :]).astype(BF16)
            weighted = (pair * prob_ref[kept, :]).astype(BF16)
            total = mm(kt_ref[lanes, :end], weighted) * INV
            total = total + weight[4:5, cols] * near[:, cols] + cross_ref[lanes, cols]
            out_ref[cols, lanes] = total.astype(BF16).T
            more_k = mm(weighted, query[cols]) * INV
            more_v = mm(scored, grad[cols])
            if a:
                dk, dv = dk + more_k, dv + more_v
            else:
                dk = jnp.concatenate([dk[:256] + more_k, dk[256:]], axis=0)
                dv = jnp.concatenate([dv[:256] + more_v, dv[256:]], axis=0)
        out_ref[K, lanes] = dk.astype(BF16)
        out_ref[V, lanes] = dv.astype(BF16)
    token_ref[...] = jnp.zeros_like(token_ref)


def gradw_body(xo_ref, xs_ref, g0, g1, g2, g3, o_ref, own_scr, sib_scr, full):
    head = lax.axis_index("head")
    for step, part in enumerate((g0, g1, g2, g3)):
        rows = aligned(lax.rem(head + 4 - step, 4), 16)
        own_scr[rows, :] = part[0:16, :]
        sib_scr[rows, :] = part[16:32, :]
    full[...] = mm(own_scr[...], xo_ref[...]) + mm(sib_scr[...], xs_ref[...])
    for chip in range(CHIPS):
        group, block = chip % 4, chip // 4
        o_ref[chip] = full[16 * group : 16 * group + 16, DIM * block : DIM * (block + 1)].astype(BF16)


def mid3_body(scale, r_ref, o_ref):
    total = r_ref[0].astype(F32)
    for chip in range(1, CHIPS):
        total = total + r_ref[chip].astype(F32)
    total = (total * scale).astype(BF16)
    for chip in range(CHIPS):
        o_ref[chip] = total


def place_body(own_ref, recv_ref, dq_hbm, dk_hbm, dv_hbm, token_ref, sems):
    token_ref[...] = jnp.zeros_like(token_ref)
    core = lax.axis_index("seq") & 1
    copies = []
    for i, out in enumerate((dq_hbm, dk_hbm, dv_hbm)):
        rows = pl.ds(TOK * i, TOK)
        copies.append(pltpu.make_async_copy(own_ref.at[rows, :], out.at[:, aligned(core, 256)], sems.at[2 * i]))
        copies.append(pltpu.make_async_copy(recv_ref.at[rows, :], out.at[:, aligned(1 - core, 256)], sems.at[2 * i + 1]))
    for copy in copies:
        copy.start()
    for copy in copies:
        copy.wait()


def join_body(w_mine_ref, w_other_ref, w_hbm, full, w_ref, sems):
    core = lax.axis_index("seq") & 1
    copies = []
    for block in range(8):
        lanes = slice(DIM * block, DIM * (block + 1))
        for group in range(4):
            full[aligned(2 * group + core, 16), :] = w_mine_ref[4 * block + group].astype(F32)
            full[aligned(2 * group + 1 - core, 16), :] = w_other_ref[4 * block + group].astype(F32)
        w_ref[lanes, :] = full[...].T
        if block % 4 == 3:
            rows = pl.ds(512 * (block // 4), 512)
            copies.append(pltpu.make_async_copy(w_ref.at[rows, :], w_hbm.at[rows, :], sems.at[block // 4]))
            copies[-1].start()
    for copy in copies:
        copy.wait()


def shards(layer_input, gate_weight, queries, key_vectors, value_vectors, grad_output, reach_level):
    seq_count = lax.axis_size("seq")
    groups = [[2 * chip + c for chip in range(CHIPS)] for c in range(2)]
    swap = [(d, d ^ 1) for d in range(seq_count)]

    def sibling(value):
        return lax.ppermute(value, "seq", swap)

    def exchange(value):
        return lax.all_to_all(value, "seq", 0, 0, axis_index_groups=groups)

    def rotate(value, step):
        return lax.ppermute(value, "head", [(h, (h + step) % 4) for h in range(4)])

    whole = pl.BlockSpec(memory_space=pltpu.VMEM)
    hbm = pl.BlockSpec(memory_space=pl.ANY)

    tok16 = shape((16, TOK), F32)
    mask8 = shape((LEVELS, TOK), F32)
    half = shape((256, DIM), F32)

    *parts, own, leaving = call(
        front_body,
        [shape((32, TOK), F32)] * 4 + [shape((4 * TOK + 16, 256), BF16)] * 2,
        (layer_input, gate_weight, queries, key_vectors, value_vectors, grad_output, reach_level),
        in_specs=[hbm] * 7,
        out_specs=[hbm] * 6,
        scratch=[
            pltpu.VMEM((TOK, 1024), BF16), pltpu.VMEM((1024, DIM), BF16), pltpu.VMEM((DIM, TOK), F32),
            pltpu.VMEM((4 * TOK + 16, 256), BF16), pltpu.VMEM((4 * TOK + 16, 256), BF16),
            pltpu.SMEM((LEVELS,), jnp.int32), pltpu.SemaphoreType.DMA((11,)), pltpu.SemaphoreType.DMA((6,)),
        ],
        limit=VMEM_ALL,
    )
    logits = [parts[0]] + [rotate(parts[step], step) for step in range(1, 4)]
    sib = sibling(leaving)
    sib_input = sibling(layer_input)
    state_own, state_sib, qt_own, qt_sib, kt_own, kt_sib, allow_own, allow_sib = call(
        state_body, [half, half] + [shape((256, TOK), BF16)] * 4 + [mask8, mask8], (own, sib)
    )
    pairs = shape((1536, 256), F32)
    rows_own, rows_sib, sc_own, pr_own, sc_sib, pr_sib = call(
        rows_body, [tok16, tok16] + [pairs] * 4, (own, sib, qt_own, qt_sib, state_own, state_sib)
    )
    logits_own, logits_send = call(gather_body, [tok16, tok16], tuple(logits), after=(rows_own,))

    gates_own, gates_sib, near, slices = call(
        level_body, [tok16, tok16, half, shape((CHIPS, 32, DIM), BF16)],
        (own, sib, qt_own, qt_sib, allow_own, allow_sib, state_own, state_sib, logits_own, sibling(logits_send)),
        scratch=[pltpu.VMEM((1024, DIM), F32)],
        after=(sib_input,),
    )
    got1 = exchange(slices)

    got2 = exchange(call(mid1_body, shape((CHIPS, 32, DIM), BF16), (got1,)))
    mine = call(mid2_body, shape((1024, DIM), BF16), (got2,))
    tok256 = shape((256, TOK), F32)
    grad_logits, cross_own, cross_sib = call(
        cross_body, [shape((32, TOK), BF16), tok256, tok256],
        (own, sib, qt_own, qt_sib, allow_own, allow_sib, gates_own, gates_sib, rows_own, rows_sib, mine),
    )

    gl = [grad_logits] + [rotate(grad_logits, step) for step in range(1, 4)]
    def tail(which, blk, key_t, state, allowed, gates, cross, scores, probs, after):
        return call(
            functools.partial(tail_body, which), [shape((3 * TOK, 256), BF16), shape((8, DIM), F32)],
            (blk, key_t, state, near, allowed, gates, mine, cross, scores, probs), after=after, cost=(4 * 10**9, 16 * 10**6),
        )

    out_sib, token = tail(1, sib, kt_sib, state_own, allow_sib, gates_sib, cross_sib, sc_sib, pr_sib, (grad_logits,))
    out_recv = sibling(out_sib)
    out_own, token = tail(0, own, kt_own, state_sib, allow_own, gates_own, cross_own, sc_own, pr_own, (token,))
    slices = call(
        gradw_body, shape((CHIPS, 16, DIM), BF16), (layer_input, sib_input, *gl),
        scratch=[pltpu.VMEM((64, TOK), BF16), pltpu.VMEM((64, TOK), BF16), pltpu.VMEM((64, 1024), F32)],
        after=(token,),
    )
    got3 = exchange(slices)
    scale = 1.0 / math.sqrt(TOK * seq_count)
    w_half = exchange(call(functools.partial(mid3_body, scale), shape((CHIPS, 16, DIM), BF16), (got3,)))
    *grads, token = call(
        place_body, [shape((TOK, 512), BF16)] * 3 + [shape((8, DIM), F32)], (out_own, out_recv),
        out_specs=[hbm] * 3 + [whole], scratch=[pltpu.SemaphoreType.DMA((6,))], after=(w_half,),
    )
    grad_weight = call(
        join_body, shape((1024, DIM), F32), (w_half, sibling(w_half)),
        out_specs=hbm,
        after=(token,),
        scratch=[pltpu.VMEM((DIM, DIM), F32), pltpu.VMEM((1024, DIM), F32), pltpu.SemaphoreType.DMA((2,))],
    )
    return (*grads, grad_weight)


def solution(mesh):
    placed = (
        P("seq", "head"),
        P("head", None),
        P("seq", "head"),
        P("seq", "head"),
        P("seq", "head"),
        P("seq", "head"),
        P("seq"),
    )
    return jax.shard_map(
        shards,
        mesh=mesh,
        in_specs=placed,
        out_specs=(P("seq", "head"), P("seq", "head"), P("seq", "head"), P("head", None)),
        check_vma=False,
    )
```

```python
import functools
import math

import jax
import jax.numpy as jnp
from jax import lax
from jax.experimental import pallas as pl
from jax.experimental.pallas import tpu as pltpu
from jax.sharding import PartitionSpec as P

F32 = jnp.float32
BF16 = jnp.bfloat16
TOK = 512
DIM = 128
SPAN = 64
LEVELS = 8
CHIPS = 32
INV = 1.0 / DIM
VMEM_LIMIT = 24 * 1024 * 1024
VMEM_ALL = 60 * 1024 * 1024


def mm(left, right, left_dim=1, right_dim=0):
    return lax.dot_general(
        left, right, (((left_dim,), (right_dim,)), ((), ())), preferred_element_type=F32
    )


def aligned(index, size):
    return pl.ds(pl.multiple_of(index * size, size), size)


def call(
    body, out_shape, args, in_specs=None, out_specs=None, grid=(), scratch=(), cost=(10**7, 10**6), after=(),
    limit=VMEM_LIMIT,
):
    whole = pl.BlockSpec(memory_space=pltpu.VMEM)
    many = isinstance(out_shape, (tuple, list))
    used = len(args)
    in_specs = list(in_specs or [whole] * used) + [pl.BlockSpec(memory_space=pl.ANY)] * len(after)
    args = (*args, *after)

    def kernel(*refs):
        body(*refs[:used], *refs[len(args) :])

    return pl.pallas_call(
        kernel,
        out_shape=out_shape,
        grid=grid,
        in_specs=in_specs,
        out_specs=out_specs or ([whole] * len(out_shape) if many else whole),
        scratch_shapes=list(scratch),
        compiler_params=pltpu.CompilerParams(vmem_limit_bytes=limit),
        cost_estimate=pl.CostEstimate(flops=cost[0], bytes_accessed=cost[1], transcendentals=0),
    )(*args)


def shape(dims, dtype):
    return jax.ShapeDtypeStruct(dims, dtype)


def front_body(
    x_hbm, w_hbm, q_hbm, k_hbm, v_hbm, g_hbm, reach_hbm, p0, p1, p2, p3, own_hbm, leaving_hbm,
    x_ref, w_ref, part_ref, own_ref, leaving_ref, reach_ref, in_sems, out_sems,
):
    head = lax.axis_index("head")
    core = lax.axis_index("seq") & 1
    ins, outs = [], []

    def load(src, dst):
        ins.append(pltpu.make_async_copy(src, dst, in_sems.at[len(ins)]))
        ins[-1].start()

    def store(src, dst):
        outs.append(pltpu.make_async_copy(src, dst, out_sems.at[len(outs)]))
        outs[-1].start()

    load(w_hbm, w_ref)
    load(x_hbm, x_ref)
    for side, ref in ((1 - core, leaving_ref), (core, own_ref)):
        for i, src in enumerate((q_hbm, k_hbm, v_hbm, g_hbm)):
            load(src.at[:, aligned(side, 256)], ref.at[pl.ds(TOK * i, TOK), :])
    load(reach_hbm, reach_ref)
    ins[0].wait()
    ins[1].wait()
    part_ref[...] = mm(w_ref[...], x_ref[...], 0, 1)
    for step, out in enumerate((p0, p1, p2, p3)):
        store(part_ref.at[aligned(lax.rem(head + step, 4), 32), :], out)
    ins[10].wait()
    lane = lax.broadcasted_iota(jnp.int32, (LEVELS, TOK), 1) // SPAN
    level = lax.broadcasted_iota(jnp.int32, (LEVELS, TOK), 0)
    reach = jnp.zeros((LEVELS, TOK), jnp.int32)
    for span in range(TOK // SPAN):
        reach = jnp.where(lane == span, reach_ref[span], reach)
    allowed = (level <= reach).astype(F32)
    allowed = jnp.concatenate([allowed[:, :256], allowed[:, 256:]], axis=0).astype(BF16)
    leaving_ref[4 * TOK :, :] = allowed
    own_ref[4 * TOK :, :] = allowed
    for copy in ins[2:6]:
        copy.wait()
    store(leaving_ref, leaving_hbm)
    for copy in ins[6:10]:
        copy.wait()
    store(own_ref, own_hbm)
    for copy in outs:
        copy.wait()


def gather_body(l0, l1, l2, l3, keep_ref, send_ref):
    core = lax.axis_index("seq") & 1
    keep = aligned(core, 16)
    send = aligned(1 - core, 16)
    keep_ref[...] = (l0[keep, :] + l1[keep, :]) + (l2[keep, :] + l3[keep, :])
    send_ref[...] = (l0[send, :] + l1[send, :]) + (l2[send, :] + l3[send, :])


Q, K, V, G = (slice(TOK * i, TOK * (i + 1)) for i in range(4))


def state_body(own_ref, sib_ref, so_ref, ss_ref, qto_ref, qts_ref, kto_ref, kts_ref, ao_ref, as_ref, pair_ref):
    for ref, state, query_t, key_t, mask in (
        (own_ref, so_ref, qto_ref, kto_ref, ao_ref), (sib_ref, ss_ref, qts_ref, kts_ref, as_ref),
    ):
        for i in range(2):
            lanes = slice(DIM * i, DIM * (i + 1))
            state[lanes, :] = mm(ref[K, lanes], ref[V, lanes], 0, 0) * INV
            query_t[lanes, :] = ref[Q, lanes].T
            key_t[lanes, :] = ref[K, lanes].T
        allowed = ref[4 * TOK :, :].astype(F32)
        mask[...] = jnp.concatenate([allowed[:8], allowed[8:]], axis=1)
    pair_ref[...] = (so_ref[...] + ss_ref[...]).astype(BF16)


def span_masks():
    src = lax.broadcasted_iota(jnp.int32, (256, 256), 0)
    dst = lax.broadcasted_iota(jnp.int32, (256, 256), 1)
    near, far = src // SPAN, dst // SPAN
    return [
        ((near == far) & (src <= dst)).astype(F32),
        ((near < far) & (near // 2 == far // 2)).astype(F32),
        (near // 2 < far // 2).astype(F32),
    ]


def rows_body(own_ref, sib_ref, qto_ref, qts_ref, so_ref, ss_ref, ro_ref, rs_ref, sco_ref, pro_ref, scs_ref, prs_ref):
    core = lax.axis_index("seq") & 1
    masks = span_masks()
    none = jnp.zeros((1, 256), F32)
    for block, (ref, query_t, state, out, score_ref, prob_ref) in enumerate((
        (own_ref, qto_ref, ss_ref, ro_ref, sco_ref, pro_ref), (sib_ref, qts_ref, so_ref, rs_ref, scs_ref, prs_ref),
    )):
        upper = (core != block).astype(F32)
        for i in range(2):
            lanes = slice(DIM * i, DIM * (i + 1))
            near = (state[lanes, :] * upper).astype(BF16)
            projected = mm(near, ref[G, lanes], 1, 1)
            near_row = jnp.sum(query_t[lanes, :].astype(F32) * projected, axis=0, keepdims=True)
            for a in range(2):
                cols = slice(256 * a, 256 * a + 256)
                end = 256 * a + 256
                scores = mm(ref[TOK : TOK + end, lanes], ref[cols, lanes], 1, 1) * INV
                probs = mm(ref[2 * TOK : 2 * TOK + end, lanes], ref[3 * TOK + 256 * a : 3 * TOK + end, lanes], 1, 1)
                kept = slice(768 * i + 256 * a, 768 * i + 256 * a + end)
                score_ref[kept, :] = scores
                prob_ref[kept, :] = probs
                prod = scores * probs
                diagonal = prod[256 * a :]
                sums = [jnp.sum(diagonal * mask, axis=0, keepdims=True) for mask in masks]
                sums.append(jnp.sum(prod[:256], axis=0, keepdims=True) if a else none)
                sums.append(near_row[:, cols])
                out[8 * i : 8 * i + 8, cols] = jnp.concatenate(sums + [none] * 3, axis=0)


def level_body(
    own_ref, sib_ref, qto_ref, qts_ref, ao_ref, as_ref, so_ref, ss_ref, lo_ref, ls_ref,
    go_ref, gs_ref, near_ref, o_ref, scr,
):
    core = lax.axis_index("seq") & 1
    gates = [jax.nn.sigmoid(lo_ref[...]), jax.nn.sigmoid(ls_ref[...])]
    go_ref[...] = gates[0]
    gs_ref[...] = gates[1]
    scr[0:256, :] = so_ref[...] + ss_ref[...]
    for i in range(2):
        lanes = slice(DIM * i, DIM * (i + 1))
        grads = []
        for block, (ref, query_t, mask) in enumerate(((own_ref, qto_ref, ao_ref), (sib_ref, qts_ref, as_ref))):
            query = query_t[lanes, :].astype(F32)
            weight = gates[block][8 * i : 8 * i + 8] * mask[...]
            gated = [(weight[level : level + 1, :] * query).astype(BF16) for level in range(4, 8)]
            grads.append(mm(jnp.concatenate(gated, axis=0), ref[G, lanes]))
        near_ref[lanes, :] = jnp.where(core == 1, grads[0][:DIM], grads[1][:DIM]) * INV
        total = (grads[0][DIM:] + grads[1][DIM:]) * INV
        for level in range(3):
            row = 256 * (level + 1) + DIM * i
            scr[row : row + DIM, :] = total[DIM * level : DIM * (level + 1)]
    for chip in range(CHIPS):
        rows = [scr[256 * level + 8 * chip : 256 * level + 8 * chip + 8, :] for level in range(4)]
        o_ref[chip] = jnp.concatenate(rows, axis=0).astype(BF16)


def mid1_body(r_ref, o_ref):
    got = [r_ref[chip].astype(F32) for chip in range(CHIPS)]
    own = [part[0:8] for part in got]
    pairs = [own[chip] + own[chip ^ 1] for chip in range(CHIPS)]
    zero = jnp.zeros((8, DIM), F32)
    before = [zero]
    for group in range(7):
        before.append(before[-1] + (pairs[4 * group] + pairs[4 * group + 2]))
    after = [zero]
    for group in range(7, 0, -1):
        total = [got[4 * group + i][24:32] for i in range(4)]
        after.append(after[-1] + ((total[0] + total[1]) + (total[2] + total[3])))
    after = after[::-1]
    for chip in range(CHIPS):
        later = after[chip >> 2]
        if not chip & 2:
            later = later + (got[chip ^ 2][16:24] + got[chip ^ 3][16:24])
        if not chip & 1:
            later = later + got[chip ^ 1][8:16]
        rows = [pairs[chip ^ 2] if chip & 2 else zero, before[chip >> 2], later]
        o_ref[chip] = jnp.concatenate(rows, axis=0).astype(BF16)


def mid2_body(r_ref, o_ref):
    for chip in range(0, CHIPS, 2):
        got = [r_ref[chip + i].astype(F32) for i in range(2)]
        for level in range(3):
            both = [part[8 * level : 8 * level + 8] for part in got]
            row = 256 * level + 8 * chip
            o_ref[row : row + 16, :] = jnp.concatenate(both, axis=0).astype(BF16)


def far_projection(i, ref, next_ref, mine_ref):
    lanes = slice(DIM * i, DIM * (i + 1))
    states = [next_ref[lanes, :]]
    states += [mine_ref[256 * level + DIM * i : 256 * level + DIM * (i + 1), :] for level in range(2)]
    projected = mm(jnp.concatenate(states, axis=0), ref[G, lanes], 1, 1)
    return [projected[DIM * level : DIM * (level + 1)] for level in range(3)]


def cross_body(
    own_ref, sib_ref, qto_ref, qts_ref, ao_ref, as_ref, go_ref, gs_ref, ro_ref, rs_ref, next_ref, mine_ref, gl_ref, co_ref, cs_ref
):
    outs = []
    for ref, query_t, mask, gates_ref, rows_ref, cross_ref in (
        (own_ref, qto_ref, ao_ref, go_ref, ro_ref, co_ref), (sib_ref, qts_ref, as_ref, gs_ref, rs_ref, cs_ref),
    ):
        for i in range(2):
            query = query_t[DIM * i : DIM * (i + 1), :].astype(F32)
            rows = slice(8 * i, 8 * i + 8)
            gates = gates_ref[rows, :]
            weight = gates * mask[...]
            parts = [jnp.zeros((5, TOK), F32)]
            total = None
            for level, term in enumerate(far_projection(i, ref, next_ref, mine_ref)):
                parts.append(jnp.sum(query * term, axis=0, keepdims=True))
                weighted = weight[5 + level : 6 + level, :] * term
                total = weighted if total is None else total + weighted
            cross_ref[DIM * i : DIM * (i + 1), :] = total
            grads = (rows_ref[rows, :] + jnp.concatenate(parts, axis=0)) * mask[...]
            outs.append(grads * gates * (1.0 - gates))
    gl_ref[...] = jnp.concatenate(outs, axis=0).astype(BF16)


def tail_body(
    block, blk_ref, kt_ref, state_ref, near_ref, mask_ref, gates_ref, mine_ref, cross_ref, score_ref, prob_ref,
    out_ref, token_ref,
):
    core = lax.axis_index("seq") & 1
    masks = span_masks()
    upper = (core != block).astype(F32)
    for i in range(2):
        lanes = slice(DIM * i, DIM * (i + 1))
        query, key, value, grad = blk_ref[Q, lanes], blk_ref[K, lanes], blk_ref[V, lanes], blk_ref[G, lanes]
        weight = gates_ref[8 * i : 8 * i + 8, :] * mask_ref[...]
        near = mm((state_ref[lanes, :] * upper).astype(BF16), grad, 1, 1)
        later = mine_ref[512 + DIM * i : 512 + DIM * (i + 1), :].astype(F32)
        later = (later + near_ref[lanes, :] * (1.0 - upper)).astype(BF16)
        dk = mm(value, later, 1, 1)
        dv = mm(key, later)
        for a in range(2):
            cols = slice(256 * a, 256 * a + 256)
            end = 256 * a + 256
            kept = slice(768 * i + 256 * a, 768 * i + 256 * a + end)
            pair = sum(weight[level : level + 1, cols] * masks[level] for level in range(3))
            if a:
                pair = jnp.concatenate([jnp.broadcast_to(weight[3:4, cols], (256, 256)), pair], axis=0)
            scored = (pair * score_ref[kept, :]).astype(BF16)
            weighted = (pair * prob_ref[kept, :]).astype(BF16)
            total = mm(kt_ref[lanes, :end], weighted) * INV
            total = total + weight[4:5, cols] * near[:, cols] + cross_ref[lanes, cols]
            out_ref[cols, lanes] = total.astype(BF16).T
            more_k = mm(weighted, query[cols]) * INV
            more_v = mm(scored, grad[cols])
            if a:
                dk, dv = dk + more_k, dv + more_v
            else:
                dk = jnp.concatenate([dk[:256] + more_k, dk[256:]], axis=0)
                dv = jnp.concatenate([dv[:256] + more_v, dv[256:]], axis=0)
        out_ref[K, lanes] = dk.astype(BF16)
        out_ref[V, lanes] = dv.astype(BF16)
    token_ref[...] = jnp.zeros_like(token_ref)


def gradw_body(xo_ref, xs_ref, g0, g1, g2, g3, o_ref, own_scr, sib_scr, full):
    head = lax.axis_index("head")
    for step, part in enumerate((g0, g1, g2, g3)):
        rows = aligned(lax.rem(head + 4 - step, 4), 16)
        own_scr[rows, :] = part[0:16, :]
        sib_scr[rows, :] = part[16:32, :]
    full[...] = mm(own_scr[...], xo_ref[...]) + mm(sib_scr[...], xs_ref[...])
    for chip in range(CHIPS):
        group, block = chip % 4, chip // 4
        o_ref[chip] = full[16 * group : 16 * group + 16, DIM * block : DIM * (block + 1)].astype(BF16)


def mid3_body(scale, r_ref, o_ref):
    total = r_ref[0].astype(F32)
    for chip in range(1, CHIPS):
        total = total + r_ref[chip].astype(F32)
    total = (total * scale).astype(BF16)
    for chip in range(CHIPS):
        o_ref[chip] = total


def place_body(own_ref, recv_ref, dq_hbm, dk_hbm, dv_hbm, token_ref, sems):
    token_ref[...] = jnp.zeros_like(token_ref)
    core = lax.axis_index("seq") & 1
    copies = []
    for i, out in enumerate((dq_hbm, dk_hbm, dv_hbm)):
        rows = pl.ds(TOK * i, TOK)
        copies.append(pltpu.make_async_copy(own_ref.at[rows, :], out.at[:, aligned(core, 256)], sems.at[2 * i]))
        copies.append(pltpu.make_async_copy(recv_ref.at[rows, :], out.at[:, aligned(1 - core, 256)], sems.at[2 * i + 1]))
    for copy in copies:
        copy.start()
    for copy in copies:
        copy.wait()


def join_body(w_mine_ref, w_other_ref, w_hbm, full, w_ref, sems):
    core = lax.axis_index("seq") & 1
    copies = []
    for block in range(8):
        lanes = slice(DIM * block, DIM * (block + 1))
        for group in range(4):
            full[aligned(2 * group + core, 16), :] = w_mine_ref[4 * block + group].astype(F32)
            full[aligned(2 * group + 1 - core, 16), :] = w_other_ref[4 * block + group].astype(F32)
        w_ref[lanes, :] = full[...].T
        if block % 4 == 3:
            rows = pl.ds(512 * (block // 4), 512)
            copies.append(pltpu.make_async_copy(w_ref.at[rows, :], w_hbm.at[rows, :], sems.at[block // 4]))
            copies[-1].start()
    for copy in copies:
        copy.wait()


def shards(layer_input, gate_weight, queries, key_vectors, value_vectors, grad_output, reach_level):
    seq_count = lax.axis_size("seq")
    groups = [[2 * chip + c for chip in range(CHIPS)] for c in range(2)]
    swap = [(d, d ^ 1) for d in range(seq_count)]

    def sibling(value):
        return lax.ppermute(value, "seq", swap)

    def exchange(value):
        return lax.all_to_all(value, "seq", 0, 0, axis_index_groups=groups)

    def rotate(value, step):
        return lax.ppermute(value, "head", [(h, (h + step) % 4) for h in range(4)])

    whole = pl.BlockSpec(memory_space=pltpu.VMEM)
    hbm = pl.BlockSpec(memory_space=pl.ANY)

    tok16 = shape((16, TOK), F32)
    mask8 = shape((LEVELS, TOK), F32)
    half = shape((256, DIM), F32)

    *parts, own, leaving = call(
        front_body,
        [shape((32, TOK), F32)] * 4 + [shape((4 * TOK + 16, 256), BF16)] * 2,
        (layer_input, gate_weight, queries, key_vectors, value_vectors, grad_output, reach_level),
        in_specs=[hbm] * 7,
        out_specs=[hbm] * 6,
        scratch=[
            pltpu.VMEM((TOK, 1024), BF16), pltpu.VMEM((1024, DIM), BF16), pltpu.VMEM((DIM, TOK), F32),
            pltpu.VMEM((4 * TOK + 16, 256), BF16), pltpu.VMEM((4 * TOK + 16, 256), BF16),
            pltpu.SMEM((LEVELS,), jnp.int32), pltpu.SemaphoreType.DMA((11,)), pltpu.SemaphoreType.DMA((6,)),
        ],
        limit=VMEM_ALL,
    )
    logits = [parts[0]] + [rotate(parts[step], step) for step in range(1, 4)]
    sib = sibling(leaving)
    sib_input = sibling(layer_input)
    state_own, state_sib, qt_own, qt_sib, kt_own, kt_sib, allow_own, allow_sib, pair_state = call(
        state_body, [half, half] + [shape((256, TOK), BF16)] * 4 + [mask8, mask8, shape((256, DIM), BF16)],
        (own, sib),
    )
    next_state = lax.ppermute(pair_state, "seq", [(d, d ^ 2) for d in range(seq_count) if not d & 2])
    pairs = shape((1536, 256), F32)
    rows_own, rows_sib, sc_own, pr_own, sc_sib, pr_sib = call(
        rows_body, [tok16, tok16] + [pairs] * 4, (own, sib, qt_own, qt_sib, state_own, state_sib)
    )
    logits_own, logits_send = call(gather_body, [tok16, tok16], tuple(logits))

    gates_own, gates_sib, near, slices = call(
        level_body, [tok16, tok16, half, shape((CHIPS, 32, DIM), BF16)],
        (own, sib, qt_own, qt_sib, allow_own, allow_sib, state_own, state_sib, logits_own, sibling(logits_send)),
        scratch=[pltpu.VMEM((1024, DIM), F32)],
        after=(sib_input, next_state, rows_own),
    )
    got1 = exchange(slices)

    got2 = exchange(call(mid1_body, shape((CHIPS, 24, DIM), BF16), (got1,)))
    mine = call(mid2_body, shape((768, DIM), BF16), (got2,))
    tok256 = shape((256, TOK), F32)
    grad_logits, cross_own, cross_sib = call(
        cross_body, [shape((32, TOK), BF16), tok256, tok256],
        (own, sib, qt_own, qt_sib, allow_own, allow_sib, gates_own, gates_sib, rows_own, rows_sib, next_state, mine),
    )

    gl = [grad_logits] + [rotate(grad_logits, step) for step in range(1, 4)]
    def tail(which, blk, key_t, state, allowed, gates, cross, scores, probs, after):
        return call(
            functools.partial(tail_body, which), [shape((3 * TOK, 256), BF16), shape((8, DIM), F32)],
            (blk, key_t, state, near, allowed, gates, mine, cross, scores, probs), after=after, cost=(4 * 10**9, 16 * 10**6),
        )

    out_sib, token = tail(1, sib, kt_sib, state_own, allow_sib, gates_sib, cross_sib, sc_sib, pr_sib, (grad_logits,))
    out_recv = sibling(out_sib)
    out_own, token = tail(0, own, kt_own, state_sib, allow_own, gates_own, cross_own, sc_own, pr_own, (token,))
    slices = call(
        gradw_body, shape((CHIPS, 16, DIM), BF16), (layer_input, sib_input, *gl),
        scratch=[pltpu.VMEM((64, TOK), BF16), pltpu.VMEM((64, TOK), BF16), pltpu.VMEM((64, 1024), F32)],
        after=(token,),
    )
    got3 = exchange(slices)
    scale = 1.0 / math.sqrt(TOK * seq_count)
    w_half = exchange(call(functools.partial(mid3_body, scale), shape((CHIPS, 16, DIM), BF16), (got3,)))
    *grads, token = call(
        place_body, [shape((TOK, 512), BF16)] * 3 + [shape((8, DIM), F32)], (out_own, out_recv),
        out_specs=[hbm] * 3 + [whole], scratch=[pltpu.SemaphoreType.DMA((6,))], after=(w_half,),
    )
    grad_weight = call(
        join_body, shape((1024, DIM), F32), (w_half, sibling(w_half)),
        out_specs=hbm,
        after=(token,),
        scratch=[pltpu.VMEM((DIM, DIM), F32), pltpu.VMEM((1024, DIM), F32), pltpu.SemaphoreType.DMA((2,))],
    )
    return (*grads, grad_weight)


def solution(mesh):
    placed = (
        P("seq", "head"),
        P("head", None),
        P("seq", "head"),
        P("seq", "head"),
        P("seq", "head"),
        P("seq", "head"),
        P("seq"),
    )
    return jax.shard_map(
        shards,
        mesh=mesh,
        in_specs=placed,
        out_specs=(P("seq", "head"), P("seq", "head"), P("seq", "head"), P("head", None)),
        check_vma=False,
    )
```

```python
import functools
import math

import jax
import jax.numpy as jnp
from jax import lax
from jax.experimental import pallas as pl
from jax.experimental.pallas import tpu as pltpu
from jax.sharding import PartitionSpec as P

F32 = jnp.float32
BF16 = jnp.bfloat16
TOK = 512
DIM = 128
SPAN = 64
LEVELS = 8
CHIPS = 32
INV = 1.0 / DIM
VMEM_LIMIT = 24 * 1024 * 1024
VMEM_ALL = 60 * 1024 * 1024


def mm(left, right, left_dim=1, right_dim=0):
    return lax.dot_general(
        left, right, (((left_dim,), (right_dim,)), ((), ())), preferred_element_type=F32
    )


def aligned(index, size):
    return pl.ds(pl.multiple_of(index * size, size), size)


def call(
    body, out_shape, args, in_specs=None, out_specs=None, grid=(), scratch=(), cost=(10**7, 10**6), after=(),
    limit=VMEM_LIMIT,
):
    whole = pl.BlockSpec(memory_space=pltpu.VMEM)
    many = isinstance(out_shape, (tuple, list))
    used = len(args)
    in_specs = list(in_specs or [whole] * used) + [pl.BlockSpec(memory_space=pl.ANY)] * len(after)
    args = (*args, *after)

    def kernel(*refs):
        body(*refs[:used], *refs[len(args) :])

    return pl.pallas_call(
        kernel,
        out_shape=out_shape,
        grid=grid,
        in_specs=in_specs,
        out_specs=out_specs or ([whole] * len(out_shape) if many else whole),
        scratch_shapes=list(scratch),
        compiler_params=pltpu.CompilerParams(vmem_limit_bytes=limit),
        cost_estimate=pl.CostEstimate(flops=cost[0], bytes_accessed=cost[1], transcendentals=0),
    )(*args)


def shape(dims, dtype):
    return jax.ShapeDtypeStruct(dims, dtype)


def front_body(
    x_hbm, w_hbm, q_hbm, k_hbm, v_hbm, g_hbm, reach_hbm, p0, p1, p2, p3, own_hbm, leaving_hbm,
    x_ref, w_ref, part_ref, own_ref, leaving_ref, reach_ref, in_sems, out_sems,
):
    head = lax.axis_index("head")
    core = lax.axis_index("seq") & 1
    ins, outs = [], []

    def load(src, dst):
        ins.append(pltpu.make_async_copy(src, dst, in_sems.at[len(ins)]))
        ins[-1].start()

    def store(src, dst):
        outs.append(pltpu.make_async_copy(src, dst, out_sems.at[len(outs)]))
        outs[-1].start()

    load(w_hbm, w_ref)
    load(x_hbm, x_ref)
    for side, ref in ((1 - core, leaving_ref), (core, own_ref)):
        for i, src in enumerate((q_hbm, k_hbm, v_hbm, g_hbm)):
            load(src.at[:, aligned(side, 256)], ref.at[pl.ds(TOK * i, TOK), :])
    load(reach_hbm, reach_ref)
    ins[0].wait()
    ins[1].wait()
    part_ref[...] = mm(w_ref[...], x_ref[...], 0, 1)
    for step, out in enumerate((p0, p1, p2, p3)):
        store(part_ref.at[aligned(lax.rem(head + step, 4), 32), :], out)
    ins[10].wait()
    lane = lax.broadcasted_iota(jnp.int32, (LEVELS, TOK), 1) // SPAN
    level = lax.broadcasted_iota(jnp.int32, (LEVELS, TOK), 0)
    reach = jnp.zeros((LEVELS, TOK), jnp.int32)
    for span in range(TOK // SPAN):
        reach = jnp.where(lane == span, reach_ref[span], reach)
    allowed = (level <= reach).astype(F32)
    allowed = jnp.concatenate([allowed[:, :256], allowed[:, 256:]], axis=0).astype(BF16)
    leaving_ref[4 * TOK :, :] = allowed
    own_ref[4 * TOK :, :] = allowed
    for copy in ins[2:6]:
        copy.wait()
    store(leaving_ref, leaving_hbm)
    for copy in ins[6:10]:
        copy.wait()
    store(own_ref, own_hbm)
    for copy in outs:
        copy.wait()


def gather_body(l0, l1, l2, l3, keep_ref, send_ref):
    core = lax.axis_index("seq") & 1
    keep = aligned(core, 16)
    send = aligned(1 - core, 16)
    keep_ref[...] = (l0[keep, :] + l1[keep, :]) + (l2[keep, :] + l3[keep, :])
    send_ref[...] = (l0[send, :] + l1[send, :]) + (l2[send, :] + l3[send, :])


Q, K, V, G = (slice(TOK * i, TOK * (i + 1)) for i in range(4))


def state_body(own_ref, sib_ref, so_ref, ss_ref, qto_ref, qts_ref, kto_ref, kts_ref, ao_ref, as_ref, pair_ref):
    for ref, state, query_t, key_t, mask in (
        (own_ref, so_ref, qto_ref, kto_ref, ao_ref), (sib_ref, ss_ref, qts_ref, kts_ref, as_ref),
    ):
        for i in range(2):
            lanes = slice(DIM * i, DIM * (i + 1))
            state[lanes, :] = mm(ref[K, lanes], ref[V, lanes], 0, 0) * INV
            query_t[lanes, :] = ref[Q, lanes].T
            key_t[lanes, :] = ref[K, lanes].T
        allowed = ref[4 * TOK :, :].astype(F32)
        mask[...] = jnp.concatenate([allowed[:8], allowed[8:]], axis=1)
    pair_ref[...] = (so_ref[...] + ss_ref[...]).astype(BF16)


def span_masks():
    src = lax.broadcasted_iota(jnp.int32, (256, 256), 0)
    dst = lax.broadcasted_iota(jnp.int32, (256, 256), 1)
    near, far = src // SPAN, dst // SPAN
    return [
        ((near == far) & (src <= dst)).astype(F32),
        ((near < far) & (near // 2 == far // 2)).astype(F32),
        (near // 2 < far // 2).astype(F32),
    ]


def rows_body(own_ref, sib_ref, qto_ref, qts_ref, so_ref, ss_ref, ro_ref, rs_ref, sco_ref, pro_ref, scs_ref, prs_ref):
    core = lax.axis_index("seq") & 1
    masks = span_masks()
    none = jnp.zeros((1, 256), F32)
    for block, (ref, query_t, state, out, score_ref, prob_ref) in enumerate((
        (own_ref, qto_ref, ss_ref, ro_ref, sco_ref, pro_ref), (sib_ref, qts_ref, so_ref, rs_ref, scs_ref, prs_ref),
    )):
        upper = (core != block).astype(F32)
        for i in range(2):
            lanes = slice(DIM * i, DIM * (i + 1))
            near = (state[lanes, :] * upper).astype(BF16)
            projected = mm(near, ref[G, lanes], 1, 1)
            near_row = jnp.sum(query_t[lanes, :].astype(F32) * projected, axis=0, keepdims=True)
            for a in range(2):
                cols = slice(256 * a, 256 * a + 256)
                end = 256 * a + 256
                scores = mm(ref[TOK : TOK + end, lanes], ref[cols, lanes], 1, 1) * INV
                probs = mm(ref[2 * TOK : 2 * TOK + end, lanes], ref[3 * TOK + 256 * a : 3 * TOK + end, lanes], 1, 1)
                kept = slice(768 * i + 256 * a, 768 * i + 256 * a + end)
                score_ref[kept, :] = scores
                prob_ref[kept, :] = probs
                prod = scores * probs
                diagonal = prod[256 * a :]
                sums = [jnp.sum(diagonal * mask, axis=0, keepdims=True) for mask in masks]
                sums.append(jnp.sum(prod[:256], axis=0, keepdims=True) if a else none)
                sums.append(near_row[:, cols])
                out[8 * i : 8 * i + 8, cols] = jnp.concatenate(sums + [none] * 3, axis=0)


def level_body(
    own_ref, sib_ref, qto_ref, qts_ref, ao_ref, as_ref, so_ref, ss_ref, lo_ref, ls_ref,
    go_ref, gs_ref, near_ref, o_ref, scr,
):
    core = lax.axis_index("seq") & 1
    gates = [jax.nn.sigmoid(lo_ref[...]), jax.nn.sigmoid(ls_ref[...])]
    go_ref[...] = gates[0]
    gs_ref[...] = gates[1]
    scr[0:256, :] = so_ref[...] + ss_ref[...]
    for i in range(2):
        lanes = slice(DIM * i, DIM * (i + 1))
        grads = []
        for block, (ref, query_t, mask) in enumerate(((own_ref, qto_ref, ao_ref), (sib_ref, qts_ref, as_ref))):
            query = query_t[lanes, :].astype(F32)
            weight = gates[block][8 * i : 8 * i + 8] * mask[...]
            gated = [(weight[level : level + 1, :] * query).astype(BF16) for level in range(4, 8)]
            grads.append(mm(jnp.concatenate(gated, axis=0), ref[G, lanes]))
        near_ref[lanes, :] = jnp.where(core == 1, grads[0][:DIM], grads[1][:DIM]) * INV
        total = (grads[0][DIM:] + grads[1][DIM:]) * INV
        for level in range(3):
            row = 256 * (level + 1) + DIM * i
            scr[row : row + DIM, :] = total[DIM * level : DIM * (level + 1)]
    for chip in range(CHIPS):
        rows = [scr[256 * level + 8 * chip : 256 * level + 8 * chip + 8, :] for level in range(4)]
        o_ref[chip] = jnp.concatenate(rows, axis=0).astype(BF16)


def mid1_body(r_ref, o_ref):
    got = [r_ref[chip].astype(F32) for chip in range(CHIPS)]
    own = [part[0:8] for part in got]
    pairs = [own[chip] + own[chip ^ 1] for chip in range(CHIPS)]
    zero = jnp.zeros((8, DIM), F32)
    before = [zero]
    for group in range(7):
        before.append(before[-1] + (pairs[4 * group] + pairs[4 * group + 2]))
    after = [zero]
    for group in range(7, 0, -1):
        total = [got[4 * group + i][24:32] for i in range(4)]
        after.append(after[-1] + ((total[0] + total[1]) + (total[2] + total[3])))
    after = after[::-1]
    for chip in range(CHIPS):
        later = after[chip >> 2]
        if not chip & 2:
            later = later + (got[chip ^ 2][16:24] + got[chip ^ 3][16:24])
        if not chip & 1:
            later = later + got[chip ^ 1][8:16]
        rows = [pairs[chip ^ 2] if chip & 2 else zero, before[chip >> 2], later]
        o_ref[chip] = jnp.concatenate(rows, axis=0).astype(BF16)


def mid2_body(r_ref, o_ref):
    for chip in range(0, CHIPS, 2):
        got = [r_ref[chip + i].astype(F32) for i in range(2)]
        for level in range(3):
            both = [part[8 * level : 8 * level + 8] for part in got]
            row = 256 * level + 8 * chip
            o_ref[row : row + 16, :] = jnp.concatenate(both, axis=0).astype(BF16)


def far_projection(i, ref, next_ref, mine_ref):
    lanes = slice(DIM * i, DIM * (i + 1))
    states = [next_ref[lanes, :]]
    states += [mine_ref[256 * level + DIM * i : 256 * level + DIM * (i + 1), :] for level in range(2)]
    projected = mm(jnp.concatenate(states, axis=0), ref[G, lanes], 1, 1)
    return [projected[DIM * level : DIM * (level + 1)] for level in range(3)]


def cross_body(
    own_ref, sib_ref, qto_ref, qts_ref, ao_ref, as_ref, go_ref, gs_ref, ro_ref, rs_ref, next_ref, mine_ref, gl_ref, co_ref, cs_ref
):
    outs = []
    for ref, query_t, mask, gates_ref, rows_ref, cross_ref in (
        (own_ref, qto_ref, ao_ref, go_ref, ro_ref, co_ref), (sib_ref, qts_ref, as_ref, gs_ref, rs_ref, cs_ref),
    ):
        for i in range(2):
            query = query_t[DIM * i : DIM * (i + 1), :].astype(F32)
            rows = slice(8 * i, 8 * i + 8)
            gates = gates_ref[rows, :]
            weight = gates * mask[...]
            parts = [jnp.zeros((5, TOK), F32)]
            total = None
            for level, term in enumerate(far_projection(i, ref, next_ref, mine_ref)):
                parts.append(jnp.sum(query * term, axis=0, keepdims=True))
                weighted = weight[5 + level : 6 + level, :] * term
                total = weighted if total is None else total + weighted
            cross_ref[DIM * i : DIM * (i + 1), :] = total
            grads = (rows_ref[rows, :] + jnp.concatenate(parts, axis=0)) * mask[...]
            outs.append(grads * gates * (1.0 - gates))
    gl_ref[...] = jnp.concatenate(outs, axis=0).astype(BF16)


def tail_body(
    block, blk_ref, kt_ref, state_ref, near_ref, mask_ref, gates_ref, mine_ref, cross_ref, score_ref, prob_ref,
    out_ref, token_ref,
):
    core = lax.axis_index("seq") & 1
    masks = span_masks()
    upper = (core != block).astype(F32)
    for i in range(2):
        lanes = slice(DIM * i, DIM * (i + 1))
        query, key, value, grad = blk_ref[Q, lanes], blk_ref[K, lanes], blk_ref[V, lanes], blk_ref[G, lanes]
        weight = gates_ref[8 * i : 8 * i + 8, :] * mask_ref[...]
        near = mm((state_ref[lanes, :] * upper).astype(BF16), grad, 1, 1)
        later = mine_ref[512 + DIM * i : 512 + DIM * (i + 1), :].astype(F32)
        later = (later + near_ref[lanes, :] * (1.0 - upper)).astype(BF16)
        dk = mm(value, later, 1, 1)
        dv = mm(key, later)
        for a in range(2):
            cols = slice(256 * a, 256 * a + 256)
            end = 256 * a + 256
            kept = slice(768 * i + 256 * a, 768 * i + 256 * a + end)
            pair = sum(weight[level : level + 1, cols] * masks[level] for level in range(3))
            if a:
                pair = jnp.concatenate([jnp.broadcast_to(weight[3:4, cols], (256, 256)), pair], axis=0)
            scored = (pair * score_ref[kept, :]).astype(BF16)
            weighted = (pair * prob_ref[kept, :]).astype(BF16)
            total = mm(kt_ref[lanes, :end], weighted) * INV
            total = total + weight[4:5, cols] * near[:, cols] + cross_ref[lanes, cols]
            out_ref[cols, lanes] = total.astype(BF16).T
            more_k = mm(weighted, query[cols]) * INV
            more_v = mm(scored, grad[cols])
            if a:
                dk, dv = dk + more_k, dv + more_v
            else:
                dk = jnp.concatenate([dk[:256] + more_k, dk[256:]], axis=0)
                dv = jnp.concatenate([dv[:256] + more_v, dv[256:]], axis=0)
        out_ref[K, lanes] = dk.astype(BF16)
        out_ref[V, lanes] = dv.astype(BF16)
    token_ref[...] = jnp.zeros_like(token_ref)


def gradw_body(xo_ref, xs_ref, g0, g1, g2, g3, o0, o1, o2, o3, own_scr, sib_scr, full):
    head = lax.axis_index("head")
    for step, part in enumerate((g0, g1, g2, g3)):
        rows = aligned(lax.rem(head + 4 - step, 4), 16)
        own_scr[rows, :] = part[0:16, :]
        sib_scr[rows, :] = part[16:32, :]
    full[...] = mm(own_scr[...], xo_ref[...]) + mm(sib_scr[...], xs_ref[...])
    place = (lax.axis_index("seq") // 2) % 4
    for step, out in enumerate((o0, o1, o2, o3)):
        start = 256 * lax.rem(place + step, 4)
        for block in range(2):
            part = full[:, pl.ds(pl.multiple_of(start + DIM * block, DIM), DIM)]
            out[64 * block : 64 * block + 64, :] = part.astype(out.dtype)


def sum_x_body(own_ref, r1, r2, r3, o_ref):
    total = (own_ref[...] + r1[...].astype(F32)) + (r2[...].astype(F32) + r3[...].astype(F32))
    total = total.astype(BF16)
    for place in range(8):
        o_ref[place] = total


def sum_z_body(scale, r_ref, o_ref):
    total = r_ref[0].astype(F32)
    for place in range(1, 8):
        total = total + r_ref[place].astype(F32)
    o_ref[...] = (total * scale).astype(BF16)


def both_body(mine_ref, other_ref, o_ref):
    core = lax.axis_index("seq") & 1
    o_ref[aligned(core, DIM), :] = mine_ref[...]
    o_ref[aligned(1 - core, DIM), :] = other_ref[...]


def place_body(own_ref, recv_ref, dq_hbm, dk_hbm, dv_hbm, token_ref, sems):
    token_ref[...] = jnp.zeros_like(token_ref)
    core = lax.axis_index("seq") & 1
    copies = []
    for i, out in enumerate((dq_hbm, dk_hbm, dv_hbm)):
        rows = pl.ds(TOK * i, TOK)
        copies.append(pltpu.make_async_copy(own_ref.at[rows, :], out.at[:, aligned(core, 256)], sems.at[2 * i]))
        copies.append(pltpu.make_async_copy(recv_ref.at[rows, :], out.at[:, aligned(1 - core, 256)], sems.at[2 * i + 1]))
    for copy in copies:
        copy.start()
    for copy in copies:
        copy.wait()


def join_body(r0, r1, r2, r3, w_hbm, w_ref, sems):
    place = (lax.axis_index("seq") // 2) % 4
    copies = []
    for step, ref in enumerate((r0, r1, r2, r3)):
        data = ref[...].astype(F32)
        for block in range(2):
            parts = [
                data[DIM * half + 64 * block + 16 * group : DIM * half + 64 * block + 16 * group + 16]
                for group in range(4)
                for half in range(2)
            ]
            at = 2 * step + block
            w_ref[DIM * at : DIM * (at + 1), :] = jnp.concatenate(parts, axis=0).T
        rows = aligned(lax.rem(place + 4 - step, 4), 256)
        copies.append(
            pltpu.make_async_copy(w_ref.at[pl.ds(256 * step, 256), :], w_hbm.at[rows, :], sems.at[step])
        )
        copies[-1].start()
    for copy in copies:
        copy.wait()


def shards(layer_input, gate_weight, queries, key_vectors, value_vectors, grad_output, reach_level):
    seq_count = lax.axis_size("seq")
    groups = [[2 * chip + c for chip in range(CHIPS)] for c in range(2)]
    swap = [(d, d ^ 1) for d in range(seq_count)]

    def sibling(value):
        return lax.ppermute(value, "seq", swap)

    def exchange(value):
        return lax.all_to_all(value, "seq", 0, 0, axis_index_groups=groups)

    def rotate_x(value, step):
        pairs = [(d, d // 8 * 8 + (d + 2 * step) % 8) for d in range(seq_count)]
        return lax.ppermute(value, "seq", pairs)

    def rotate(value, step):
        return lax.ppermute(value, "head", [(h, (h + step) % 4) for h in range(4)])

    whole = pl.BlockSpec(memory_space=pltpu.VMEM)
    hbm = pl.BlockSpec(memory_space=pl.ANY)

    tok16 = shape((16, TOK), F32)
    mask8 = shape((LEVELS, TOK), F32)
    half = shape((256, DIM), F32)

    *parts, own, leaving = call(
        front_body,
        [shape((32, TOK), F32)] * 4 + [shape((4 * TOK + 16, 256), BF16)] * 2,
        (layer_input, gate_weight, queries, key_vectors, value_vectors, grad_output, reach_level),
        in_specs=[hbm] * 7,
        out_specs=[hbm] * 6,
        scratch=[
            pltpu.VMEM((TOK, 1024), BF16), pltpu.VMEM((1024, DIM), BF16), pltpu.VMEM((DIM, TOK), F32),
            pltpu.VMEM((4 * TOK + 16, 256), BF16), pltpu.VMEM((4 * TOK + 16, 256), BF16),
            pltpu.SMEM((LEVELS,), jnp.int32), pltpu.SemaphoreType.DMA((11,)), pltpu.SemaphoreType.DMA((6,)),
        ],
        limit=VMEM_ALL,
    )
    logits = [parts[0]] + [rotate(parts[step], step) for step in range(1, 4)]
    sib = sibling(leaving)
    sib_input = sibling(layer_input)
    state_own, state_sib, qt_own, qt_sib, kt_own, kt_sib, allow_own, allow_sib, pair_state = call(
        state_body, [half, half] + [shape((256, TOK), BF16)] * 4 + [mask8, mask8, shape((256, DIM), BF16)],
        (own, sib),
    )
    next_state = lax.ppermute(pair_state, "seq", [(d, d ^ 2) for d in range(seq_count) if not d & 2])
    pairs = shape((1536, 256), F32)
    rows_own, rows_sib, sc_own, pr_own, sc_sib, pr_sib = call(
        rows_body, [tok16, tok16] + [pairs] * 4, (own, sib, qt_own, qt_sib, state_own, state_sib)
    )
    logits_own, logits_send = call(gather_body, [tok16, tok16], tuple(logits))

    gates_own, gates_sib, near, slices = call(
        level_body, [tok16, tok16, half, shape((CHIPS, 32, DIM), BF16)],
        (own, sib, qt_own, qt_sib, allow_own, allow_sib, state_own, state_sib, logits_own, sibling(logits_send)),
        scratch=[pltpu.VMEM((1024, DIM), F32)],
        after=(sib_input, next_state, rows_own),
    )
    got1 = exchange(slices)

    got2 = exchange(call(mid1_body, shape((CHIPS, 24, DIM), BF16), (got1,)))
    mine = call(mid2_body, shape((768, DIM), BF16), (got2,))
    tok256 = shape((256, TOK), F32)
    grad_logits, cross_own, cross_sib = call(
        cross_body, [shape((32, TOK), BF16), tok256, tok256],
        (own, sib, qt_own, qt_sib, allow_own, allow_sib, gates_own, gates_sib, rows_own, rows_sib, next_state, mine),
    )

    gl = [grad_logits] + [rotate(grad_logits, step) for step in range(1, 4)]
    def tail(which, blk, key_t, state, allowed, gates, cross, scores, probs, after):
        return call(
            functools.partial(tail_body, which), [shape((3 * TOK, 256), BF16), shape((8, DIM), F32)],
            (blk, key_t, state, near, allowed, gates, mine, cross, scores, probs), after=after, cost=(4 * 10**9, 16 * 10**6),
        )

    out_sib, token = tail(1, sib, kt_sib, state_own, allow_sib, gates_sib, cross_sib, sc_sib, pr_sib, (grad_logits,))
    out_recv = sibling(out_sib)
    out_own, token = tail(0, own, kt_own, state_sib, allow_own, gates_own, cross_own, sc_own, pr_own, (token,))
    quarter = shape((DIM, DIM), BF16)
    sums = call(
        gradw_body, [shape((DIM, DIM), F32)] + [quarter] * 3, (layer_input, sib_input, *gl),
        scratch=[pltpu.VMEM((64, TOK), BF16), pltpu.VMEM((64, TOK), BF16), pltpu.VMEM((64, 1024), F32)],
        after=(token,),
    )
    got3 = [sums[0]] + [rotate_x(sums[step], step) for step in range(1, 4)]
    spread = call(sum_x_body, shape((8, DIM, DIM), BF16), tuple(got3))
    columns = [[8 * z + place for z in range(8)] for place in range(8)]
    got4 = lax.all_to_all(spread, "seq", 0, 0, axis_index_groups=columns)
    scale = 1.0 / math.sqrt(TOK * seq_count)
    mine_sum = call(functools.partial(sum_z_body, scale), quarter, (got4,))
    other_sum = sibling(mine_sum)
    *grads, token = call(
        place_body, [shape((TOK, 512), BF16)] * 3 + [shape((8, DIM), F32)], (out_own, out_recv),
        out_specs=[hbm] * 3 + [whole], scratch=[pltpu.SemaphoreType.DMA((6,))], after=(mine_sum,),
    )
    both = call(both_body, shape((256, DIM), BF16), (mine_sum, other_sum))
    got5 = [both] + [rotate_x(both, step) for step in range(1, 4)]
    grad_weight = call(
        join_body, shape((1024, DIM), F32), tuple(got5),
        out_specs=hbm,
        after=(token,),
        scratch=[pltpu.VMEM((1024, DIM), F32), pltpu.SemaphoreType.DMA((4,))],
    )
    return (*grads, grad_weight)


def solution(mesh):
    placed = (
        P("seq", "head"),
        P("head", None),
        P("seq", "head"),
        P("seq", "head"),
        P("seq", "head"),
        P("seq", "head"),
        P("seq"),
    )
    return jax.shard_map(
        shards,
        mesh=mesh,
        in_specs=placed,
        out_specs=(P("seq", "head"), P("seq", "head"), P("seq", "head"), P("head", None)),
        check_vma=False,
    )
```

```python
import functools
import math

import jax
import jax.numpy as jnp
from jax import lax
from jax.experimental import pallas as pl
from jax.experimental.pallas import tpu as pltpu
from jax.sharding import PartitionSpec as P

F32 = jnp.float32
BF16 = jnp.bfloat16
TOK = 512
DIM = 128
SPAN = 64
LEVELS = 8
INV = 1.0 / DIM
VMEM_LIMIT = 24 * 1024 * 1024
VMEM_ALL = 60 * 1024 * 1024


def mm(left, right, left_dim=1, right_dim=0):
    return lax.dot_general(
        left, right, (((left_dim,), (right_dim,)), ((), ())), preferred_element_type=F32
    )


def aligned(index, size):
    return pl.ds(pl.multiple_of(index * size, size), size)


def call(
    body, out_shape, args, in_specs=None, out_specs=None, grid=(), scratch=(), cost=(10**7, 10**6), after=(),
    limit=VMEM_LIMIT,
):
    whole = pl.BlockSpec(memory_space=pltpu.VMEM)
    many = isinstance(out_shape, (tuple, list))
    used = len(args)
    in_specs = list(in_specs or [whole] * used) + [pl.BlockSpec(memory_space=pl.ANY)] * len(after)
    args = (*args, *after)

    def kernel(*refs):
        body(*refs[:used], *refs[len(args) :])

    return pl.pallas_call(
        kernel,
        out_shape=out_shape,
        grid=grid,
        in_specs=in_specs,
        out_specs=out_specs or ([whole] * len(out_shape) if many else whole),
        scratch_shapes=list(scratch),
        compiler_params=pltpu.CompilerParams(vmem_limit_bytes=limit),
        cost_estimate=pl.CostEstimate(flops=cost[0], bytes_accessed=cost[1], transcendentals=0),
    )(*args)


def shape(dims, dtype):
    return jax.ShapeDtypeStruct(dims, dtype)


def front_body(
    x_hbm, w_hbm, q_hbm, k_hbm, v_hbm, g_hbm, reach_hbm, p0, p1, p2, p3, own_hbm, leaving_hbm,
    x_ref, w_ref, part_ref, own_ref, leaving_ref, reach_ref, in_sems, out_sems,
):
    head = lax.axis_index("head")
    core = lax.axis_index("seq") & 1
    ins, outs = [], []

    def load(src, dst):
        ins.append(pltpu.make_async_copy(src, dst, in_sems.at[len(ins)]))
        ins[-1].start()

    def store(src, dst):
        outs.append(pltpu.make_async_copy(src, dst, out_sems.at[len(outs)]))
        outs[-1].start()

    load(w_hbm, w_ref)
    load(x_hbm, x_ref)
    for side, ref in ((1 - core, leaving_ref), (core, own_ref)):
        for i, src in enumerate((q_hbm, k_hbm, v_hbm, g_hbm)):
            load(src.at[:, aligned(side, 256)], ref.at[pl.ds(TOK * i, TOK), :])
    load(reach_hbm, reach_ref)
    ins[0].wait()
    ins[1].wait()
    part_ref[...] = mm(w_ref[...], x_ref[...], 0, 1)
    for step, out in enumerate((p0, p1, p2, p3)):
        store(part_ref.at[aligned(lax.rem(head + step, 4), 32), :], out)
    ins[10].wait()
    lane = lax.broadcasted_iota(jnp.int32, (LEVELS, TOK), 1) // SPAN
    level = lax.broadcasted_iota(jnp.int32, (LEVELS, TOK), 0)
    reach = jnp.zeros((LEVELS, TOK), jnp.int32)
    for span in range(TOK // SPAN):
        reach = jnp.where(lane == span, reach_ref[span], reach)
    allowed = (level <= reach).astype(F32)
    allowed = jnp.concatenate([allowed[:, :256], allowed[:, 256:]], axis=0).astype(BF16)
    leaving_ref[4 * TOK :, :] = allowed
    own_ref[4 * TOK :, :] = allowed
    for copy in ins[2:6]:
        copy.wait()
    store(leaving_ref, leaving_hbm)
    for copy in ins[6:10]:
        copy.wait()
    store(own_ref, own_hbm)
    for copy in outs:
        copy.wait()


def gather_body(l0, l1, l2, l3, keep_ref, send_ref):
    core = lax.axis_index("seq") & 1
    keep = aligned(core, 16)
    send = aligned(1 - core, 16)
    keep_ref[...] = (l0[keep, :] + l1[keep, :]) + (l2[keep, :] + l3[keep, :])
    send_ref[...] = (l0[send, :] + l1[send, :]) + (l2[send, :] + l3[send, :])


Q, K, V, G = (slice(TOK * i, TOK * (i + 1)) for i in range(4))


def state_body(own_ref, sib_ref, so_ref, ss_ref, qto_ref, qts_ref, kto_ref, kts_ref, ao_ref, as_ref):
    for ref, state, query_t, key_t, mask in (
        (own_ref, so_ref, qto_ref, kto_ref, ao_ref), (sib_ref, ss_ref, qts_ref, kts_ref, as_ref),
    ):
        for i in range(2):
            lanes = slice(DIM * i, DIM * (i + 1))
            state[lanes, :] = mm(ref[K, lanes], ref[V, lanes], 0, 0) * INV
            query_t[lanes, :] = ref[Q, lanes].T
            key_t[lanes, :] = ref[K, lanes].T
        allowed = ref[4 * TOK :, :].astype(F32)
        mask[...] = jnp.concatenate([allowed[:8], allowed[8:]], axis=1)


def span_masks():
    src = lax.broadcasted_iota(jnp.int32, (256, 256), 0)
    dst = lax.broadcasted_iota(jnp.int32, (256, 256), 1)
    near, far = src // SPAN, dst // SPAN
    return [
        ((near == far) & (src <= dst)).astype(F32),
        ((near < far) & (near // 2 == far // 2)).astype(F32),
        (near // 2 < far // 2).astype(F32),
    ]


def rows_body(own_ref, sib_ref, qto_ref, qts_ref, so_ref, ss_ref, ro_ref, rs_ref, sco_ref, pro_ref, scs_ref, prs_ref):
    core = lax.axis_index("seq") & 1
    masks = span_masks()
    none = jnp.zeros((1, 256), F32)
    for block, (ref, query_t, state, out, score_ref, prob_ref) in enumerate((
        (own_ref, qto_ref, ss_ref, ro_ref, sco_ref, pro_ref), (sib_ref, qts_ref, so_ref, rs_ref, scs_ref, prs_ref),
    )):
        upper = (core != block).astype(F32)
        for i in range(2):
            lanes = slice(DIM * i, DIM * (i + 1))
            near = (state[lanes, :] * upper).astype(BF16)
            projected = mm(near, ref[G, lanes], 1, 1)
            near_row = jnp.sum(query_t[lanes, :].astype(F32) * projected, axis=0, keepdims=True)
            for a in range(2):
                cols = slice(256 * a, 256 * a + 256)
                end = 256 * a + 256
                scores = mm(ref[TOK : TOK + end, lanes], ref[cols, lanes], 1, 1) * INV
                probs = mm(ref[2 * TOK : 2 * TOK + end, lanes], ref[3 * TOK + 256 * a : 3 * TOK + end, lanes], 1, 1)
                kept = slice(768 * i + 256 * a, 768 * i + 256 * a + end)
                score_ref[kept, :] = scores
                prob_ref[kept, :] = probs
                prod = scores * probs
                diagonal = prod[256 * a :]
                sums = [jnp.sum(diagonal * mask, axis=0, keepdims=True) for mask in masks]
                sums.append(jnp.sum(prod[:256], axis=0, keepdims=True) if a else none)
                sums.append(near_row[:, cols])
                out[8 * i : 8 * i + 8, cols] = jnp.concatenate(sums + [none] * 3, axis=0)


def level_body(
    own_ref, sib_ref, qto_ref, qts_ref, ao_ref, as_ref, so_ref, ss_ref, lo_ref, ls_ref,
    go_ref, gs_ref, near_ref, own_slice_ref, m1_ref, m2_ref, m3_ref, scr,
):
    core = lax.axis_index("seq") & 1
    gates = [jax.nn.sigmoid(lo_ref[...]), jax.nn.sigmoid(ls_ref[...])]
    go_ref[...] = gates[0]
    gs_ref[...] = gates[1]
    scr[0:256, :] = so_ref[...] + ss_ref[...]
    for i in range(2):
        lanes = slice(DIM * i, DIM * (i + 1))
        grads = []
        for block, (ref, query_t, mask) in enumerate(((own_ref, qto_ref, ao_ref), (sib_ref, qts_ref, as_ref))):
            query = query_t[lanes, :].astype(F32)
            weight = gates[block][8 * i : 8 * i + 8] * mask[...]
            gated = [(weight[level : level + 1, :] * query).astype(BF16) for level in range(4, 8)]
            grads.append(mm(jnp.concatenate(gated, axis=0), ref[G, lanes]))
        near_ref[lanes, :] = jnp.where(core == 1, grads[0][:DIM], grads[1][:DIM]) * INV
        total = (grads[0][DIM:] + grads[1][DIM:]) * INV
        for level in range(3):
            row = 256 * (level + 1) + DIM * i
            scr[row : row + DIM, :] = total[DIM * level : DIM * (level + 1)]
    place = (lax.axis_index("seq") // 2) % 4
    own_slice_ref[0:64, :] = scr[aligned(place, 64), :]
    own_slice_ref[64:128, :] = scr[pl.ds(pl.multiple_of(768 + 64 * place, 64), 64), :]
    for mask, out in ((1, m1_ref), (2, m2_ref), (3, m3_ref)):
        later = (place >> (mask >> 1)) & 1
        start = later * (256 if mask == 1 else 512)
        out[0:256, :] = scr[pl.ds(pl.multiple_of(start, 256), 256), :].astype(BF16)
        peer = 64 * (place ^ mask)
        for part in range(2):
            rows = scr[pl.ds(pl.multiple_of(768 * part + peer, 64), 64), :]
            out[256 + 64 * part : 320 + 64 * part, :] = rows.astype(BF16)


def along_x_body(own_ref, m1_ref, m2_ref, m3_ref, spread_ref, states_ref, later_ref):
    place = (lax.axis_index("seq") // 2) % 4
    got = [m1_ref[...].astype(F32), m2_ref[...].astype(F32), m3_ref[...].astype(F32)]
    level5, level6 = got[0][:256], got[1][:256] + got[2][:256]
    upper5 = (place & 1).astype(F32)
    upper6 = (place >> 1).astype(F32)
    states_ref[0:256, :] = (level5 * upper5).astype(BF16)
    states_ref[256:512, :] = (level6 * upper6).astype(BF16)
    later_ref[...] = level5 * (1.0 - upper5) + level6 * (1.0 - upper6)
    total = own_ref[...] + got[0][256:] + (got[1][256:] + got[2][256:])
    here = lax.axis_index("seq") // 8
    for group in range(8):
        spread_ref[7 - group] = jnp.where(group > here, total[:64], total[64:]).astype(BF16)


def along_z_body(r_ref, o_ref):
    here = lax.axis_index("seq") // 8
    before = jnp.zeros((64, DIM), F32)
    after = jnp.zeros((64, DIM), F32)
    for group in range(8):
        part = r_ref[7 - group].astype(F32)
        before = before + part * (here > group).astype(F32)
        after = after + part * (here < group).astype(F32)
    o_ref[...] = jnp.concatenate([before, after], axis=0).astype(BF16)


def far_body(own_ref, r1, r2, r3, states_ref, near_ref, mine_ref, later_ref):
    place = (lax.axis_index("seq") // 2) % 4
    mine_ref[0:512, :] = states_ref[...]
    for mask, ref in enumerate((own_ref, r1, r2, r3)):
        peer = 64 * (place ^ mask)
        mine_ref[pl.ds(pl.multiple_of(512 + peer, 64), 64), :] = ref[0:64, :]
        rows = pl.ds(pl.multiple_of(peer, 64), 64)
        later_ref[rows, :] = near_ref[rows, :] + ref[64:128, :].astype(F32)


def far_projection(i, ref, mine_ref):
    lanes = slice(DIM * i, DIM * (i + 1))
    states = [mine_ref[256 * level + DIM * i : 256 * level + DIM * (i + 1), :] for level in range(3)]
    projected = mm(jnp.concatenate(states, axis=0), ref[G, lanes], 1, 1)
    return [projected[DIM * level : DIM * (level + 1)] for level in range(3)]


def cross_body(
    own_ref, sib_ref, qto_ref, qts_ref, ao_ref, as_ref, go_ref, gs_ref, ro_ref, rs_ref, mine_ref, gl_ref, co_ref, cs_ref
):
    outs = []
    for ref, query_t, mask, gates_ref, rows_ref, cross_ref in (
        (own_ref, qto_ref, ao_ref, go_ref, ro_ref, co_ref), (sib_ref, qts_ref, as_ref, gs_ref, rs_ref, cs_ref),
    ):
        for i in range(2):
            query = query_t[DIM * i : DIM * (i + 1), :].astype(F32)
            rows = slice(8 * i, 8 * i + 8)
            gates = gates_ref[rows, :]
            weight = gates * mask[...]
            parts = [jnp.zeros((5, TOK), F32)]
            total = None
            for level, term in enumerate(far_projection(i, ref, mine_ref)):
                parts.append(jnp.sum(query * term, axis=0, keepdims=True))
                weighted = weight[5 + level : 6 + level, :] * term
                total = weighted if total is None else total + weighted
            cross_ref[DIM * i : DIM * (i + 1), :] = total
            grads = (rows_ref[rows, :] + jnp.concatenate(parts, axis=0)) * mask[...]
            outs.append(grads * gates * (1.0 - gates))
    gl_ref[...] = jnp.concatenate(outs, axis=0).astype(BF16)


def tail_body(
    block, blk_ref, kt_ref, state_ref, near_ref, mask_ref, gates_ref, later_ref, cross_ref, score_ref, prob_ref,
    out_ref, token_ref,
):
    core = lax.axis_index("seq") & 1
    masks = span_masks()
    upper = (core != block).astype(F32)
    for i in range(2):
        lanes = slice(DIM * i, DIM * (i + 1))
        query, key, value, grad = blk_ref[Q, lanes], blk_ref[K, lanes], blk_ref[V, lanes], blk_ref[G, lanes]
        weight = gates_ref[8 * i : 8 * i + 8, :] * mask_ref[...]
        near = mm((state_ref[lanes, :] * upper).astype(BF16), grad, 1, 1)
        later = (later_ref[lanes, :] + near_ref[lanes, :] * (1.0 - upper)).astype(BF16)
        dk = mm(value, later, 1, 1)
        dv = mm(key, later)
        for a in range(2):
            cols = slice(256 * a, 256 * a + 256)
            end = 256 * a + 256
            kept = slice(768 * i + 256 * a, 768 * i + 256 * a + end)
            pair = sum(weight[level : level + 1, cols] * masks[level] for level in range(3))
            if a:
                pair = jnp.concatenate([jnp.broadcast_to(weight[3:4, cols], (256, 256)), pair], axis=0)
            scored = (pair * score_ref[kept, :]).astype(BF16)
            weighted = (pair * prob_ref[kept, :]).astype(BF16)
            total = mm(kt_ref[lanes, :end], weighted) * INV
            total = total + weight[4:5, cols] * near[:, cols] + cross_ref[lanes, cols]
            out_ref[cols, lanes] = total.astype(BF16).T
            more_k = mm(weighted, query[cols]) * INV
            more_v = mm(scored, grad[cols])
            if a:
                dk, dv = dk + more_k, dv + more_v
            else:
                dk = jnp.concatenate([dk[:256] + more_k, dk[256:]], axis=0)
                dv = jnp.concatenate([dv[:256] + more_v, dv[256:]], axis=0)
        out_ref[K, lanes] = dk.astype(BF16)
        out_ref[V, lanes] = dv.astype(BF16)
    token_ref[...] = jnp.zeros_like(token_ref)


def gradw_body(xo_ref, xs_ref, g0, g1, g2, g3, o0, o1, o2, o3, own_scr, sib_scr, full):
    head = lax.axis_index("head")
    for step, part in enumerate((g0, g1, g2, g3)):
        rows = aligned(lax.rem(head + 4 - step, 4), 16)
        own_scr[rows, :] = part[0:16, :]
        sib_scr[rows, :] = part[16:32, :]
    full[...] = mm(own_scr[...], xo_ref[...]) + mm(sib_scr[...], xs_ref[...])
    place = (lax.axis_index("seq") // 2) % 4
    for step, out in enumerate((o0, o1, o2, o3)):
        start = 256 * lax.rem(place + step, 4)
        for block in range(2):
            part = full[:, pl.ds(pl.multiple_of(start + DIM * block, DIM), DIM)]
            out[64 * block : 64 * block + 64, :] = part.astype(out.dtype)


def sum_x_body(own_ref, r1, r2, r3, o_ref):
    total = (own_ref[...] + r1[...].astype(F32)) + (r2[...].astype(F32) + r3[...].astype(F32))
    total = total.astype(BF16)
    for place in range(8):
        o_ref[place] = total


def sum_z_body(scale, r_ref, o_ref):
    total = r_ref[0].astype(F32)
    for place in range(1, 8):
        total = total + r_ref[place].astype(F32)
    o_ref[...] = (total * scale).astype(BF16)


def both_body(mine_ref, other_ref, o_ref):
    core = lax.axis_index("seq") & 1
    o_ref[aligned(core, DIM), :] = mine_ref[...]
    o_ref[aligned(1 - core, DIM), :] = other_ref[...]


def place_body(own_ref, recv_ref, dq_hbm, dk_hbm, dv_hbm, token_ref, sems):
    token_ref[...] = jnp.zeros_like(token_ref)
    core = lax.axis_index("seq") & 1
    copies = []
    for i, out in enumerate((dq_hbm, dk_hbm, dv_hbm)):
        rows = pl.ds(TOK * i, TOK)
        copies.append(pltpu.make_async_copy(own_ref.at[rows, :], out.at[:, aligned(core, 256)], sems.at[2 * i]))
        copies.append(pltpu.make_async_copy(recv_ref.at[rows, :], out.at[:, aligned(1 - core, 256)], sems.at[2 * i + 1]))
    for copy in copies:
        copy.start()
    for copy in copies:
        copy.wait()


def join_body(r0, r1, r2, r3, w_hbm, w_ref, sems):
    place = (lax.axis_index("seq") // 2) % 4
    copies = []
    for step, ref in enumerate((r0, r1, r2, r3)):
        data = ref[...].astype(F32)
        for block in range(2):
            parts = [
                data[DIM * half + 64 * block + 16 * group : DIM * half + 64 * block + 16 * group + 16]
                for group in range(4)
                for half in range(2)
            ]
            at = 2 * step + block
            w_ref[DIM * at : DIM * (at + 1), :] = jnp.concatenate(parts, axis=0).T
        rows = aligned(lax.rem(place + 4 - step, 4), 256)
        copies.append(
            pltpu.make_async_copy(w_ref.at[pl.ds(256 * step, 256), :], w_hbm.at[rows, :], sems.at[step])
        )
        copies[-1].start()
    for copy in copies:
        copy.wait()


def shards(layer_input, gate_weight, queries, key_vectors, value_vectors, grad_output, reach_level):
    seq_count = lax.axis_size("seq")
    columns = [[8 * z + place for z in reversed(range(8))] for place in range(8)]
    swap = [(d, d ^ 1) for d in range(seq_count)]

    def sibling(value):
        return lax.ppermute(value, "seq", swap)

    def swap_x(value, mask):
        return lax.ppermute(value, "seq", [(d, d ^ (2 * mask)) for d in range(seq_count)])

    def rotate_x(value, step):
        pairs = [(d, d // 8 * 8 + (d + 2 * step) % 8) for d in range(seq_count)]
        return lax.ppermute(value, "seq", pairs)

    def rotate(value, step):
        return lax.ppermute(value, "head", [(h, (h + step) % 4) for h in range(4)])

    whole = pl.BlockSpec(memory_space=pltpu.VMEM)
    hbm = pl.BlockSpec(memory_space=pl.ANY)

    tok16 = shape((16, TOK), F32)
    mask8 = shape((LEVELS, TOK), F32)
    half = shape((256, DIM), F32)

    *parts, own, leaving = call(
        front_body,
        [shape((32, TOK), F32)] * 4 + [shape((4 * TOK + 16, 256), BF16)] * 2,
        (layer_input, gate_weight, queries, key_vectors, value_vectors, grad_output, reach_level),
        in_specs=[hbm] * 7,
        out_specs=[hbm] * 6,
        scratch=[
            pltpu.VMEM((TOK, 1024), BF16), pltpu.VMEM((1024, DIM), BF16), pltpu.VMEM((DIM, TOK), F32),
            pltpu.VMEM((4 * TOK + 16, 256), BF16), pltpu.VMEM((4 * TOK + 16, 256), BF16),
            pltpu.SMEM((LEVELS,), jnp.int32), pltpu.SemaphoreType.DMA((11,)), pltpu.SemaphoreType.DMA((6,)),
        ],
        limit=VMEM_ALL,
    )
    logits = [parts[0]] + [rotate(parts[step], step) for step in range(1, 4)]
    sib = sibling(leaving)
    sib_input = sibling(layer_input)
    state_own, state_sib, qt_own, qt_sib, kt_own, kt_sib, allow_own, allow_sib = call(
        state_body, [half, half] + [shape((256, TOK), BF16)] * 4 + [mask8, mask8],
        (own, sib),
    )
    pairs = shape((1536, 256), F32)
    rows_own, rows_sib, sc_own, pr_own, sc_sib, pr_sib = call(
        rows_body, [tok16, tok16] + [pairs] * 4, (own, sib, qt_own, qt_sib, state_own, state_sib)
    )
    logits_own, logits_send = call(gather_body, [tok16, tok16], tuple(logits), after=(rows_own,))

    message = shape((384, DIM), BF16)
    eighth = shape((DIM, DIM), BF16)
    gates_own, gates_sib, near, own_slice, *messages = call(
        level_body, [tok16, tok16, half, shape((DIM, DIM), F32), message, message, message],
        (own, sib, qt_own, qt_sib, allow_own, allow_sib, state_own, state_sib, logits_own, sibling(logits_send)),
        scratch=[pltpu.VMEM((1024, DIM), F32)],
        after=(sib_input, rows_own),
    )
    spread, close_states, close_later = call(
        along_x_body, [shape((8, 64, DIM), BF16), shape((512, DIM), BF16), half],
        (own_slice, *(swap_x(messages[mask - 1], mask) for mask in (1, 2, 3))),
    )
    got = call(along_z_body, eighth, (lax.all_to_all(spread, "seq", 0, 0, axis_index_groups=columns),))
    mine, later = call(
        far_body, [shape((768, DIM), BF16), half],
        (got, *(swap_x(got, mask) for mask in (1, 2, 3)), close_states, close_later),
    )
    tok256 = shape((256, TOK), F32)
    grad_logits, cross_own, cross_sib = call(
        cross_body, [shape((32, TOK), BF16), tok256, tok256],
        (own, sib, qt_own, qt_sib, allow_own, allow_sib, gates_own, gates_sib, rows_own, rows_sib, mine),
    )

    gl = [grad_logits] + [rotate(grad_logits, step) for step in range(1, 4)]
    def tail(which, blk, key_t, state, allowed, gates, cross, scores, probs, after):
        return call(
            functools.partial(tail_body, which), [shape((3 * TOK, 256), BF16), shape((8, DIM), F32)],
            (blk, key_t, state, near, allowed, gates, later, cross, scores, probs), after=after, cost=(4 * 10**9, 16 * 10**6),
        )

    out_sib, token = tail(1, sib, kt_sib, state_own, allow_sib, gates_sib, cross_sib, sc_sib, pr_sib, (grad_logits,))
    out_recv = sibling(out_sib)
    out_own, token = tail(0, own, kt_own, state_sib, allow_own, gates_own, cross_own, sc_own, pr_own, (token,))
    quarter = shape((DIM, DIM), BF16)
    sums = call(
        gradw_body, [shape((DIM, DIM), F32)] + [quarter] * 3, (layer_input, sib_input, *gl),
        scratch=[pltpu.VMEM((64, TOK), BF16), pltpu.VMEM((64, TOK), BF16), pltpu.VMEM((64, 1024), F32)],
        after=(token,),
    )
    got3 = [sums[0]] + [rotate_x(sums[step], step) for step in range(1, 4)]
    spread = call(sum_x_body, shape((8, DIM, DIM), BF16), tuple(got3))
    got4 = lax.all_to_all(spread, "seq", 0, 0, axis_index_groups=columns)
    scale = 1.0 / math.sqrt(TOK * seq_count)
    mine_sum = call(functools.partial(sum_z_body, scale), quarter, (got4,))
    other_sum = sibling(mine_sum)
    *grads, token = call(
        place_body, [shape((TOK, 512), BF16)] * 3 + [shape((8, DIM), F32)], (out_own, out_recv),
        out_specs=[hbm] * 3 + [whole], scratch=[pltpu.SemaphoreType.DMA((6,))], after=(mine_sum,),
    )
    both = call(both_body, shape((256, DIM), BF16), (mine_sum, other_sum))
    got5 = [both] + [rotate_x(both, step) for step in range(1, 4)]
    grad_weight = call(
        join_body, shape((1024, DIM), F32), tuple(got5),
        out_specs=hbm,
        after=(token,),
        scratch=[pltpu.VMEM((1024, DIM), F32), pltpu.SemaphoreType.DMA((4,))],
    )
    return (*grads, grad_weight)


def solution(mesh):
    placed = (
        P("seq", "head"),
        P("head", None),
        P("seq", "head"),
        P("seq", "head"),
        P("seq", "head"),
        P("seq", "head"),
        P("seq"),
    )
    return jax.shard_map(
        shards,
        mesh=mesh,
        in_specs=placed,
        out_specs=(P("seq", "head"), P("seq", "head"), P("seq", "head"), P("head", None)),
        check_vma=False,
    )
```

```python
import functools
import math

import jax
import jax.numpy as jnp
from jax import lax
from jax.experimental import pallas as pl
from jax.experimental.pallas import tpu as pltpu
from jax.sharding import PartitionSpec as P

F32 = jnp.float32
BF16 = jnp.bfloat16
TOK = 512
DIM = 128
SPAN = 64
LEVELS = 8
INV = 1.0 / DIM
VMEM_LIMIT = 24 * 1024 * 1024
VMEM_ALL = 60 * 1024 * 1024


def mm(left, right, left_dim=1, right_dim=0):
    return lax.dot_general(
        left, right, (((left_dim,), (right_dim,)), ((), ())), preferred_element_type=F32
    )


def aligned(index, size):
    return pl.ds(pl.multiple_of(index * size, size), size)


def call(
    body, out_shape, args, in_specs=None, out_specs=None, grid=(), scratch=(), cost=(10**7, 10**6), after=(),
    limit=VMEM_LIMIT, aliases=None,
):
    whole = pl.BlockSpec(memory_space=pltpu.VMEM)
    many = isinstance(out_shape, (tuple, list))
    used = len(args)
    in_specs = list(in_specs or [whole] * used) + [pl.BlockSpec(memory_space=pl.ANY)] * len(after)
    args = (*args, *after)

    def kernel(*refs):
        body(*refs[:used], *refs[len(args) :])

    return pl.pallas_call(
        kernel,
        out_shape=out_shape,
        grid=grid,
        in_specs=in_specs,
        input_output_aliases=aliases or {},
        out_specs=out_specs or ([whole] * len(out_shape) if many else whole),
        scratch_shapes=list(scratch),
        compiler_params=pltpu.CompilerParams(vmem_limit_bytes=limit),
        cost_estimate=pl.CostEstimate(flops=cost[0], bytes_accessed=cost[1], transcendentals=0),
    )(*args)


def shape(dims, dtype):
    return jax.ShapeDtypeStruct(dims, dtype)


def front_body(
    x_hbm, w_hbm, q_hbm, k_hbm, v_hbm, g_hbm, reach_hbm, p0, p1, p2, p3, own_hbm, leaving_hbm,
    x_ref, w_ref, part_ref, own_ref, leaving_ref, reach_ref, in_sems, out_sems,
):
    head = lax.axis_index("head")
    core = lax.axis_index("seq") & 1
    ins, outs = [], []

    def load(src, dst):
        ins.append(pltpu.make_async_copy(src, dst, in_sems.at[len(ins)]))
        ins[-1].start()

    def store(src, dst):
        outs.append(pltpu.make_async_copy(src, dst, out_sems.at[len(outs)]))
        outs[-1].start()

    load(w_hbm, w_ref)
    load(x_hbm, x_ref)
    for side, ref in ((1 - core, leaving_ref), (core, own_ref)):
        for i, src in enumerate((q_hbm, k_hbm, v_hbm, g_hbm)):
            load(src.at[:, aligned(side, 256)], ref.at[pl.ds(TOK * i, TOK), :])
    load(reach_hbm, reach_ref)
    ins[0].wait()
    ins[1].wait()
    part_ref[...] = mm(w_ref[...], x_ref[...], 0, 1)
    for step, out in enumerate((p0, p1, p2, p3)):
        store(part_ref.at[aligned(lax.rem(head + step, 4), 32), :], out)
    ins[10].wait()
    lane = lax.broadcasted_iota(jnp.int32, (LEVELS, TOK), 1) // SPAN
    level = lax.broadcasted_iota(jnp.int32, (LEVELS, TOK), 0)
    reach = jnp.zeros((LEVELS, TOK), jnp.int32)
    for span in range(TOK // SPAN):
        reach = jnp.where(lane == span, reach_ref[span], reach)
    allowed = (level <= reach).astype(F32)
    allowed = jnp.concatenate([allowed[:, :256], allowed[:, 256:]], axis=0).astype(BF16)
    leaving_ref[4 * TOK :, :] = allowed
    own_ref[4 * TOK :, :] = allowed
    for copy in ins[2:6]:
        copy.wait()
    store(leaving_ref, leaving_hbm)
    for copy in ins[6:10]:
        copy.wait()
    store(own_ref, own_hbm)
    for copy in outs:
        copy.wait()


def gather_body(l0, l1, l2, l3, keep_ref, send_ref):
    core = lax.axis_index("seq") & 1
    keep = aligned(core, 16)
    send = aligned(1 - core, 16)
    keep_ref[...] = (l0[keep, :] + l1[keep, :]) + (l2[keep, :] + l3[keep, :])
    send_ref[...] = (l0[send, :] + l1[send, :]) + (l2[send, :] + l3[send, :])


Q, K, V, G = (slice(TOK * i, TOK * (i + 1)) for i in range(4))


def state_body(own_ref, sib_ref, so_ref, ss_ref, qto_ref, qts_ref, kto_ref, kts_ref, ao_ref, as_ref):
    for ref, state, query_t, key_t, mask in (
        (own_ref, so_ref, qto_ref, kto_ref, ao_ref), (sib_ref, ss_ref, qts_ref, kts_ref, as_ref),
    ):
        for i in range(2):
            lanes = slice(DIM * i, DIM * (i + 1))
            state[lanes, :] = mm(ref[K, lanes], ref[V, lanes], 0, 0) * INV
            query_t[lanes, :] = ref[Q, lanes].T
            key_t[lanes, :] = ref[K, lanes].T
        allowed = ref[4 * TOK :, :].astype(F32)
        mask[...] = jnp.concatenate([allowed[:8], allowed[8:]], axis=1)


def span_masks():
    src = lax.broadcasted_iota(jnp.int32, (256, 256), 0)
    dst = lax.broadcasted_iota(jnp.int32, (256, 256), 1)
    near, far = src // SPAN, dst // SPAN
    return [
        ((near == far) & (src <= dst)).astype(F32),
        ((near < far) & (near // 2 == far // 2)).astype(F32),
        (near // 2 < far // 2).astype(F32),
    ]


def rows_body(own_ref, sib_ref, qto_ref, qts_ref, so_ref, ss_ref, ro_ref, rs_ref, sco_ref, pro_ref, scs_ref, prs_ref):
    core = lax.axis_index("seq") & 1
    masks = span_masks()
    none = jnp.zeros((1, 256), F32)
    for block, (ref, query_t, state, out, score_ref, prob_ref) in enumerate((
        (own_ref, qto_ref, ss_ref, ro_ref, sco_ref, pro_ref), (sib_ref, qts_ref, so_ref, rs_ref, scs_ref, prs_ref),
    )):
        upper = (core != block).astype(F32)
        for i in range(2):
            lanes = slice(DIM * i, DIM * (i + 1))
            near = (state[lanes, :] * upper).astype(BF16)
            projected = mm(near, ref[G, lanes], 1, 1)
            near_row = jnp.sum(query_t[lanes, :].astype(F32) * projected, axis=0, keepdims=True)
            for a in range(2):
                cols = slice(256 * a, 256 * a + 256)
                end = 256 * a + 256
                scores = mm(ref[TOK : TOK + end, lanes], ref[cols, lanes], 1, 1) * INV
                probs = mm(ref[2 * TOK : 2 * TOK + end, lanes], ref[3 * TOK + 256 * a : 3 * TOK + end, lanes], 1, 1)
                kept = slice(768 * i + 256 * a, 768 * i + 256 * a + end)
                score_ref[kept, :] = scores
                prob_ref[kept, :] = probs
                prod = scores * probs
                diagonal = prod[256 * a :]
                sums = [jnp.sum(diagonal * mask, axis=0, keepdims=True) for mask in masks]
                sums.append(jnp.sum(prod[:256], axis=0, keepdims=True) if a else none)
                sums.append(near_row[:, cols])
                out[8 * i : 8 * i + 8, cols] = jnp.concatenate(sums + [none] * 3, axis=0)


def level_body(
    own_ref, sib_ref, qto_ref, qts_ref, ao_ref, as_ref, so_ref, ss_ref, lo_ref, ls_ref,
    go_ref, gs_ref, near_ref, own_slice_ref, m1_ref, m2_ref, m3_ref, scr,
):
    core = lax.axis_index("seq") & 1
    gates = [jax.nn.sigmoid(lo_ref[...]), jax.nn.sigmoid(ls_ref[...])]
    go_ref[...] = gates[0]
    gs_ref[...] = gates[1]
    scr[0:256, :] = so_ref[...] + ss_ref[...]
    for i in range(2):
        lanes = slice(DIM * i, DIM * (i + 1))
        grads = []
        for block, (ref, query_t, mask) in enumerate(((own_ref, qto_ref, ao_ref), (sib_ref, qts_ref, as_ref))):
            query = query_t[lanes, :].astype(F32)
            weight = gates[block][8 * i : 8 * i + 8] * mask[...]
            gated = [(weight[level : level + 1, :] * query).astype(BF16) for level in range(4, 8)]
            grads.append(mm(jnp.concatenate(gated, axis=0), ref[G, lanes]))
        near_ref[lanes, :] = jnp.where(core == 1, grads[0][:DIM], grads[1][:DIM]) * INV
        total = (grads[0][DIM:] + grads[1][DIM:]) * INV
        for level in range(3):
            row = 256 * (level + 1) + DIM * i
            scr[row : row + DIM, :] = total[DIM * level : DIM * (level + 1)]
    place = (lax.axis_index("seq") // 2) % 4
    own_slice_ref[0:64, :] = scr[aligned(place, 64), :]
    own_slice_ref[64:128, :] = scr[pl.ds(pl.multiple_of(768 + 64 * place, 64), 64), :]
    for step, out in ((1, m1_ref), (2, m2_ref), (3, m3_ref)):
        peer = lax.rem(place + step, 4)
        gradient = jnp.where((place ^ peer) == 1, 256, 512)
        start = jnp.where(peer < place, gradient, 0)
        out[0:256, :] = scr[pl.ds(pl.multiple_of(start, 256), 256), :].astype(BF16)
        for part in range(2):
            rows = scr[pl.ds(pl.multiple_of(768 * part + 64 * peer, 64), 64), :]
            out[256 + 64 * part : 320 + 64 * part, :] = rows.astype(BF16)


def along_x_body(own_ref, m1_ref, m2_ref, m3_ref, spread_ref, states_ref, later_ref):
    place = (lax.axis_index("seq") // 2) % 4
    got = [m1_ref[...].astype(F32), m2_ref[...].astype(F32), m3_ref[...].astype(F32)]
    states = [jnp.zeros((256, DIM), F32)] * 2
    later = jnp.zeros((256, DIM), F32)
    for step in range(1, 4):
        source = lax.rem(place + 4 - step, 4)
        part = got[step - 1][:256]
        earlier = (source < place).astype(F32)
        level5 = ((place ^ source) == 1).astype(F32)
        states = [states[0] + part * (earlier * level5), states[1] + part * (earlier * (1.0 - level5))]
        later = later + part * (1.0 - earlier)
    states_ref[0:256, :] = states[0].astype(BF16)
    states_ref[256:512, :] = states[1].astype(BF16)
    later_ref[...] = later
    total = own_ref[...] + got[0][256:] + (got[1][256:] + got[2][256:])
    here = lax.axis_index("seq") // 8
    for group in range(8):
        spread_ref[7 - group] = jnp.where(group > here, total[:64], total[64:]).astype(BF16)


def along_z_body(r_ref, o_ref):
    here = lax.axis_index("seq") // 8
    before = jnp.zeros((64, DIM), F32)
    after = jnp.zeros((64, DIM), F32)
    for group in range(8):
        part = r_ref[7 - group].astype(F32)
        before = before + part * (here > group).astype(F32)
        after = after + part * (here < group).astype(F32)
    o_ref[...] = jnp.concatenate([before, after], axis=0).astype(BF16)


def far_body(own_ref, r1, r2, r3, states_ref, near_ref, mine_ref, later_ref):
    place = (lax.axis_index("seq") // 2) % 4
    mine_ref[0:512, :] = states_ref[...]
    for step, ref in enumerate((own_ref, r1, r2, r3)):
        peer = 64 * lax.rem(place + 4 - step, 4)
        mine_ref[pl.ds(pl.multiple_of(512 + peer, 64), 64), :] = ref[0:64, :]
        rows = pl.ds(pl.multiple_of(peer, 64), 64)
        later_ref[rows, :] = near_ref[rows, :] + ref[64:128, :].astype(F32)


def far_projection(i, ref, mine_ref):
    lanes = slice(DIM * i, DIM * (i + 1))
    states = [mine_ref[256 * level + DIM * i : 256 * level + DIM * (i + 1), :] for level in range(3)]
    projected = mm(jnp.concatenate(states, axis=0), ref[G, lanes], 1, 1)
    return [projected[DIM * level : DIM * (level + 1)] for level in range(3)]


def cross_body(
    own_ref, sib_ref, qto_ref, qts_ref, ao_ref, as_ref, go_ref, gs_ref, ro_ref, rs_ref, mine_ref, gl_ref, co_ref, cs_ref
):
    outs = []
    for ref, query_t, mask, gates_ref, rows_ref, cross_ref in (
        (own_ref, qto_ref, ao_ref, go_ref, ro_ref, co_ref), (sib_ref, qts_ref, as_ref, gs_ref, rs_ref, cs_ref),
    ):
        for i in range(2):
            query = query_t[DIM * i : DIM * (i + 1), :].astype(F32)
            rows = slice(8 * i, 8 * i + 8)
            gates = gates_ref[rows, :]
            weight = gates * mask[...]
            parts = [jnp.zeros((5, TOK), F32)]
            total = None
            for level, term in enumerate(far_projection(i, ref, mine_ref)):
                parts.append(jnp.sum(query * term, axis=0, keepdims=True))
                weighted = weight[5 + level : 6 + level, :] * term
                total = weighted if total is None else total + weighted
            cross_ref[DIM * i : DIM * (i + 1), :] = total
            grads = (rows_ref[rows, :] + jnp.concatenate(parts, axis=0)) * mask[...]
            outs.append(grads * gates * (1.0 - gates))
    gl_ref[...] = jnp.concatenate(outs, axis=0).astype(BF16)


def tail_body(
    block, blk_ref, kt_ref, state_ref, near_ref, mask_ref, gates_ref, later_ref, cross_ref, score_ref, prob_ref,
    out_ref, token_ref,
):
    core = lax.axis_index("seq") & 1
    masks = span_masks()
    upper = (core != block).astype(F32)
    for i in range(2):
        lanes = slice(DIM * i, DIM * (i + 1))
        query, key, value, grad = blk_ref[Q, lanes], blk_ref[K, lanes], blk_ref[V, lanes], blk_ref[G, lanes]
        weight = gates_ref[8 * i : 8 * i + 8, :] * mask_ref[...]
        near = mm((state_ref[lanes, :] * upper).astype(BF16), grad, 1, 1)
        later = (later_ref[lanes, :] + near_ref[lanes, :] * (1.0 - upper)).astype(BF16)
        dk = mm(value, later, 1, 1)
        dv = mm(key, later)
        for a in range(2):
            cols = slice(256 * a, 256 * a + 256)
            end = 256 * a + 256
            kept = slice(768 * i + 256 * a, 768 * i + 256 * a + end)
            pair = sum(weight[level : level + 1, cols] * masks[level] for level in range(3))
            if a:
                pair = jnp.concatenate([jnp.broadcast_to(weight[3:4, cols], (256, 256)), pair], axis=0)
            scored = (pair * score_ref[kept, :]).astype(BF16)
            weighted = (pair * prob_ref[kept, :]).astype(BF16)
            total = mm(kt_ref[lanes, :end], weighted) * INV
            total = total + weight[4:5, cols] * near[:, cols] + cross_ref[lanes, cols]
            out_ref[cols, lanes] = total.astype(BF16).T
            more_k = mm(weighted, query[cols]) * INV
            more_v = mm(scored, grad[cols])
            if a:
                dk, dv = dk + more_k, dv + more_v
            else:
                dk = jnp.concatenate([dk[:256] + more_k, dk[256:]], axis=0)
                dv = jnp.concatenate([dv[:256] + more_v, dv[256:]], axis=0)
        out_ref[K, lanes] = dk.astype(BF16)
        out_ref[V, lanes] = dv.astype(BF16)
    token_ref[...] = jnp.zeros_like(token_ref)


def gradw_body(xo_ref, xs_ref, g0, g1, g2, g3, o0, o1, o2, o3, own_scr, sib_scr, full):
    head = lax.axis_index("head")
    for step, part in enumerate((g0, g1, g2, g3)):
        rows = aligned(lax.rem(head + 4 - step, 4), 16)
        own_scr[rows, :] = part[0:16, :]
        sib_scr[rows, :] = part[16:32, :]
    full[...] = mm(own_scr[...], xo_ref[...]) + mm(sib_scr[...], xs_ref[...])
    place = (lax.axis_index("seq") // 2) % 4
    for step, out in enumerate((o0, o1, o2, o3)):
        start = 256 * lax.rem(place + step, 4)
        for block in range(2):
            part = full[:, pl.ds(pl.multiple_of(start + DIM * block, DIM), DIM)]
            out[64 * block : 64 * block + 64, :] = part.astype(out.dtype)


def sum_x_body(own_ref, r1, r2, r3, o_ref):
    total = (own_ref[...] + r1[...].astype(F32)) + (r2[...].astype(F32) + r3[...].astype(F32))
    total = total.astype(BF16)
    for place in range(8):
        o_ref[place] = total


def sum_z_body(scale, r_ref, o_ref):
    total = r_ref[0].astype(F32)
    for place in range(1, 8):
        total = total + r_ref[place].astype(F32)
    o_ref[...] = (total * scale).astype(BF16)


def both_body(mine_ref, other_ref, held_ref, o_ref, passed_ref):
    core = lax.axis_index("seq") & 1
    o_ref[aligned(core, DIM), :] = mine_ref[...]
    o_ref[aligned(1 - core, DIM), :] = other_ref[...]


def place_body(own_ref, recv_ref, dq_hbm, dk_hbm, dv_hbm, token_ref, sems):
    token_ref[...] = jnp.zeros_like(token_ref)
    core = lax.axis_index("seq") & 1
    copies = []
    for i, out in enumerate((dq_hbm, dk_hbm, dv_hbm)):
        rows = pl.ds(TOK * i, TOK)
        copies.append(pltpu.make_async_copy(own_ref.at[rows, :], out.at[:, aligned(core, 256)], sems.at[2 * i]))
        copies.append(pltpu.make_async_copy(recv_ref.at[rows, :], out.at[:, aligned(1 - core, 256)], sems.at[2 * i + 1]))
    for copy in copies:
        copy.start()
    for copy in copies:
        copy.wait()


def join_body(r0, r1, r2, r3, w_hbm, w_ref, sems):
    place = (lax.axis_index("seq") // 2) % 4
    copies = []
    for step, ref in enumerate((r0, r1, r2, r3)):
        data = ref[...].astype(F32)
        for block in range(2):
            parts = [
                data[DIM * half + 64 * block + 16 * group : DIM * half + 64 * block + 16 * group + 16]
                for group in range(4)
                for half in range(2)
            ]
            at = 2 * step + block
            w_ref[DIM * at : DIM * (at + 1), :] = jnp.concatenate(parts, axis=0).T
        rows = aligned(lax.rem(place + 4 - step, 4), 256)
        copies.append(
            pltpu.make_async_copy(w_ref.at[pl.ds(256 * step, 256), :], w_hbm.at[rows, :], sems.at[step])
        )
        copies[-1].start()
    for copy in copies:
        copy.wait()


def shards(layer_input, gate_weight, queries, key_vectors, value_vectors, grad_output, reach_level):
    seq_count = lax.axis_size("seq")
    columns = [[8 * z + place for z in reversed(range(8))] for place in range(8)]
    swap = [(d, d ^ 1) for d in range(seq_count)]

    def sibling(value):
        return lax.ppermute(value, "seq", swap)

    def rotate_x(value, step):
        pairs = [(d, d // 8 * 8 + (d + 2 * step) % 8) for d in range(seq_count)]
        return lax.ppermute(value, "seq", pairs)

    def rotate(value, step):
        return lax.ppermute(value, "head", [(h, (h + step) % 4) for h in range(4)])

    whole = pl.BlockSpec(memory_space=pltpu.VMEM)
    hbm = pl.BlockSpec(memory_space=pl.ANY)

    tok16 = shape((16, TOK), F32)
    mask8 = shape((LEVELS, TOK), F32)
    half = shape((256, DIM), F32)

    *parts, own, leaving = call(
        front_body,
        [shape((32, TOK), F32)] * 4 + [shape((4 * TOK + 16, 256), BF16)] * 2,
        (layer_input, gate_weight, queries, key_vectors, value_vectors, grad_output, reach_level),
        in_specs=[hbm] * 7,
        out_specs=[hbm] * 6,
        scratch=[
            pltpu.VMEM((TOK, 1024), BF16), pltpu.VMEM((1024, DIM), BF16), pltpu.VMEM((DIM, TOK), F32),
            pltpu.VMEM((4 * TOK + 16, 256), BF16), pltpu.VMEM((4 * TOK + 16, 256), BF16),
            pltpu.SMEM((LEVELS,), jnp.int32), pltpu.SemaphoreType.DMA((11,)), pltpu.SemaphoreType.DMA((6,)),
        ],
        limit=VMEM_ALL,
    )
    logits = [parts[0]] + [rotate(parts[step], step) for step in range(1, 4)]
    sib = sibling(leaving)
    sib_input = sibling(layer_input)
    state_own, state_sib, qt_own, qt_sib, kt_own, kt_sib, allow_own, allow_sib = call(
        state_body, [half, half] + [shape((256, TOK), BF16)] * 4 + [mask8, mask8],
        (own, sib),
    )
    pairs = shape((1536, 256), F32)
    rows_own, rows_sib, sc_own, pr_own, sc_sib, pr_sib = call(
        rows_body, [tok16, tok16] + [pairs] * 4, (own, sib, qt_own, qt_sib, state_own, state_sib)
    )
    logits_own, logits_send = call(gather_body, [tok16, tok16], tuple(logits), after=(rows_own,))

    message = shape((384, DIM), BF16)
    eighth = shape((DIM, DIM), BF16)
    gates_own, gates_sib, near, own_slice, *messages = call(
        level_body, [tok16, tok16, half, shape((DIM, DIM), F32), message, message, message],
        (own, sib, qt_own, qt_sib, allow_own, allow_sib, state_own, state_sib, logits_own, sibling(logits_send)),
        scratch=[pltpu.VMEM((1024, DIM), F32)],
        after=(sib_input, rows_own),
    )
    spread, close_states, close_later = call(
        along_x_body, [shape((8, 64, DIM), BF16), shape((512, DIM), BF16), half],
        (own_slice, *(rotate_x(messages[step - 1], step) for step in (1, 2, 3))),
    )
    got = call(along_z_body, eighth, (lax.all_to_all(spread, "seq", 0, 0, axis_index_groups=columns),))
    mine, later = call(
        far_body, [shape((768, DIM), BF16), half],
        (got, *(rotate_x(got, step) for step in (1, 2, 3)), close_states, close_later),
    )
    tok256 = shape((256, TOK), F32)
    grad_logits, cross_own, cross_sib = call(
        cross_body, [shape((32, TOK), BF16), tok256, tok256],
        (own, sib, qt_own, qt_sib, allow_own, allow_sib, gates_own, gates_sib, rows_own, rows_sib, mine),
    )

    gl = [grad_logits] + [rotate(grad_logits, step) for step in range(1, 4)]
    def tail(which, blk, key_t, state, allowed, gates, cross, scores, probs, after):
        return call(
            functools.partial(tail_body, which), [shape((3 * TOK, 256), BF16), shape((8, DIM), F32)],
            (blk, key_t, state, near, allowed, gates, later, cross, scores, probs), after=after, cost=(4 * 10**9, 16 * 10**6),
        )

    out_sib, token = tail(1, sib, kt_sib, state_own, allow_sib, gates_sib, cross_sib, sc_sib, pr_sib, (grad_logits,))
    out_own, token = tail(0, own, kt_own, state_sib, allow_own, gates_own, cross_own, sc_own, pr_own, (token,))
    quarter = shape((DIM, DIM), BF16)
    sums = call(
        gradw_body, [shape((DIM, DIM), F32)] + [quarter] * 3, (layer_input, sib_input, *gl),
        scratch=[pltpu.VMEM((64, TOK), BF16), pltpu.VMEM((64, TOK), BF16), pltpu.VMEM((64, 1024), F32)],
        after=(token,),
    )
    got3 = [sums[0]] + [rotate_x(sums[step], step) for step in range(1, 4)]
    spread = call(sum_x_body, shape((8, DIM, DIM), BF16), tuple(got3))
    got4 = lax.all_to_all(spread, "seq", 0, 0, axis_index_groups=columns)
    scale = 1.0 / math.sqrt(TOK * seq_count)
    mine_sum = call(functools.partial(sum_z_body, scale), quarter, (got4,))
    other_sum = sibling(mine_sum)
    both, out_sib = call(
        both_body, [shape((256, DIM), BF16), shape((3 * TOK, 256), BF16)], (mine_sum, other_sum, out_sib),
        in_specs=[whole, whole, hbm], out_specs=[whole, hbm], aliases={2: 1},
    )
    out_recv = sibling(out_sib)
    *grads, token = call(
        place_body, [shape((TOK, 512), BF16)] * 3 + [shape((8, DIM), F32)], (out_own, out_recv),
        out_specs=[hbm] * 3 + [whole], scratch=[pltpu.SemaphoreType.DMA((6,))], after=(both,),
    )
    got5 = [both] + [rotate_x(both, step) for step in range(1, 4)]
    grad_weight = call(
        join_body, shape((1024, DIM), F32), tuple(got5),
        out_specs=hbm,
        after=(token,),
        scratch=[pltpu.VMEM((1024, DIM), F32), pltpu.SemaphoreType.DMA((4,))],
    )
    return (*grads, grad_weight)


def solution(mesh):
    placed = (
        P("seq", "head"),
        P("head", None),
        P("seq", "head"),
        P("seq", "head"),
        P("seq", "head"),
        P("seq", "head"),
        P("seq"),
    )
    return jax.shard_map(
        shards,
        mesh=mesh,
        in_specs=placed,
        out_specs=(P("seq", "head"), P("seq", "head"), P("seq", "head"), P("head", None)),
        check_vma=False,
    )
```

```python
import functools
import math

import jax
import jax.numpy as jnp
from jax import lax
from jax.experimental import pallas as pl
from jax.experimental.pallas import tpu as pltpu
from jax.sharding import PartitionSpec as P

F32 = jnp.float32
BF16 = jnp.bfloat16
TOK = 512
DIM = 128
SPAN = 64
LEVELS = 8
ORDER = [5, 4, 6, 3, 2, 7, 0, 1]
INV = 1.0 / DIM
VMEM_LIMIT = 24 * 1024 * 1024
VMEM_ALL = 60 * 1024 * 1024


def mm(left, right, left_dim=1, right_dim=0):
    return lax.dot_general(
        left, right, (((left_dim,), (right_dim,)), ((), ())), preferred_element_type=F32
    )


def aligned(index, size):
    return pl.ds(pl.multiple_of(index * size, size), size)


def call(
    body, out_shape, args, in_specs=None, out_specs=None, grid=(), scratch=(), cost=(10**7, 10**6), after=(),
    limit=VMEM_LIMIT, aliases=None,
):
    whole = pl.BlockSpec(memory_space=pltpu.VMEM)
    many = isinstance(out_shape, (tuple, list))
    used = len(args)
    in_specs = list(in_specs or [whole] * used) + [pl.BlockSpec(memory_space=pl.ANY)] * len(after)
    args = (*args, *after)

    def kernel(*refs):
        body(*refs[:used], *refs[len(args) :])

    return pl.pallas_call(
        kernel,
        out_shape=out_shape,
        grid=grid,
        in_specs=in_specs,
        input_output_aliases=aliases or {},
        out_specs=out_specs or ([whole] * len(out_shape) if many else whole),
        scratch_shapes=list(scratch),
        compiler_params=pltpu.CompilerParams(vmem_limit_bytes=limit),
        cost_estimate=pl.CostEstimate(flops=cost[0], bytes_accessed=cost[1], transcendentals=0),
    )(*args)


def shape(dims, dtype):
    return jax.ShapeDtypeStruct(dims, dtype)


def front_body(
    x_hbm, w_hbm, q_hbm, k_hbm, v_hbm, g_hbm, reach_hbm, p0, p1, p2, p3, own_hbm, leaving_hbm,
    x_ref, w_ref, part_ref, own_ref, leaving_ref, reach_ref, in_sems, out_sems,
):
    head = lax.axis_index("head")
    core = lax.axis_index("seq") & 1
    ins, outs = [], []

    def load(src, dst):
        ins.append(pltpu.make_async_copy(src, dst, in_sems.at[len(ins)]))
        ins[-1].start()

    def store(src, dst):
        outs.append(pltpu.make_async_copy(src, dst, out_sems.at[len(outs)]))
        outs[-1].start()

    load(w_hbm, w_ref)
    load(x_hbm, x_ref)
    for side, ref in ((1 - core, leaving_ref), (core, own_ref)):
        for i, src in enumerate((q_hbm, k_hbm, v_hbm, g_hbm)):
            load(src.at[:, aligned(side, 256)], ref.at[pl.ds(TOK * i, TOK), :])
    load(reach_hbm, reach_ref)
    ins[0].wait()
    ins[1].wait()
    part_ref[...] = mm(w_ref[...], x_ref[...], 0, 1)
    for step, out in enumerate((p0, p1, p2, p3)):
        store(part_ref.at[aligned(lax.rem(head + step, 4), 32), :], out)
    ins[10].wait()
    lane = lax.broadcasted_iota(jnp.int32, (LEVELS, TOK), 1) // SPAN
    level = lax.broadcasted_iota(jnp.int32, (LEVELS, TOK), 0)
    reach = jnp.zeros((LEVELS, TOK), jnp.int32)
    for span in range(TOK // SPAN):
        reach = jnp.where(lane == span, reach_ref[span], reach)
    allowed = (level <= reach).astype(F32)
    allowed = jnp.concatenate([allowed[:, :256], allowed[:, 256:]], axis=0).astype(BF16)
    leaving_ref[4 * TOK :, :] = allowed
    own_ref[4 * TOK :, :] = allowed
    for copy in ins[2:6]:
        copy.wait()
    store(leaving_ref, leaving_hbm)
    for copy in ins[6:10]:
        copy.wait()
    store(own_ref, own_hbm)
    for copy in outs:
        copy.wait()


def gather_body(l0, l1, l2, l3, keep_ref, send_ref):
    core = lax.axis_index("seq") & 1
    keep = aligned(core, 16)
    send = aligned(1 - core, 16)
    keep_ref[...] = (l0[keep, :] + l1[keep, :]) + (l2[keep, :] + l3[keep, :])
    send_ref[...] = (l0[send, :] + l1[send, :]) + (l2[send, :] + l3[send, :])


Q, K, V, G = (slice(TOK * i, TOK * (i + 1)) for i in range(4))


def state_body(own_ref, sib_ref, so_ref, ss_ref, qto_ref, qts_ref, kto_ref, kts_ref, ao_ref, as_ref):
    for ref, state, query_t, key_t, mask in (
        (own_ref, so_ref, qto_ref, kto_ref, ao_ref), (sib_ref, ss_ref, qts_ref, kts_ref, as_ref),
    ):
        for i in range(2):
            lanes = slice(DIM * i, DIM * (i + 1))
            state[lanes, :] = mm(ref[K, lanes], ref[V, lanes], 0, 0) * INV
            query_t[lanes, :] = ref[Q, lanes].T
            key_t[lanes, :] = ref[K, lanes].T
        allowed = ref[4 * TOK :, :].astype(F32)
        mask[...] = jnp.concatenate([allowed[:8], allowed[8:]], axis=1)


def span_masks():
    src = lax.broadcasted_iota(jnp.int32, (256, 256), 0)
    dst = lax.broadcasted_iota(jnp.int32, (256, 256), 1)
    near, far = src // SPAN, dst // SPAN
    return [
        ((near == far) & (src <= dst)).astype(F32),
        ((near < far) & (near // 2 == far // 2)).astype(F32),
        (near // 2 < far // 2).astype(F32),
    ]


def rows_body(own_ref, sib_ref, qto_ref, qts_ref, so_ref, ss_ref, ro_ref, rs_ref, sco_ref, pro_ref, scs_ref, prs_ref):
    core = lax.axis_index("seq") & 1
    masks = span_masks()
    none = jnp.zeros((1, 256), F32)
    for block, (ref, query_t, state, out, score_ref, prob_ref) in enumerate((
        (own_ref, qto_ref, ss_ref, ro_ref, sco_ref, pro_ref), (sib_ref, qts_ref, so_ref, rs_ref, scs_ref, prs_ref),
    )):
        upper = (core != block).astype(F32)
        for i in range(2):
            lanes = slice(DIM * i, DIM * (i + 1))
            near = (state[lanes, :] * upper).astype(BF16)
            projected = mm(near, ref[G, lanes], 1, 1)
            near_row = jnp.sum(query_t[lanes, :].astype(F32) * projected, axis=0, keepdims=True)
            for a in range(2):
                cols = slice(256 * a, 256 * a + 256)
                end = 256 * a + 256
                scores = mm(ref[TOK : TOK + end, lanes], ref[cols, lanes], 1, 1) * INV
                probs = mm(ref[2 * TOK : 2 * TOK + end, lanes], ref[3 * TOK + 256 * a : 3 * TOK + end, lanes], 1, 1)
                kept = slice(768 * i + 256 * a, 768 * i + 256 * a + end)
                score_ref[kept, :] = scores
                prob_ref[kept, :] = probs
                prod = scores * probs
                diagonal = prod[256 * a :]
                sums = [jnp.sum(diagonal * mask, axis=0, keepdims=True) for mask in masks]
                sums.append(jnp.sum(prod[:256], axis=0, keepdims=True) if a else none)
                sums.append(near_row[:, cols])
                out[8 * i : 8 * i + 8, cols] = jnp.concatenate(sums + [none] * 3, axis=0)


def level_body(
    own_ref, sib_ref, qto_ref, qts_ref, ao_ref, as_ref, so_ref, ss_ref, lo_ref, ls_ref,
    go_ref, gs_ref, near_ref, own_slice_ref, m1_ref, m2_ref, m3_ref, scr,
):
    core = lax.axis_index("seq") & 1
    gates = [jax.nn.sigmoid(lo_ref[...]), jax.nn.sigmoid(ls_ref[...])]
    go_ref[...] = gates[0]
    gs_ref[...] = gates[1]
    scr[0:256, :] = so_ref[...] + ss_ref[...]
    for i in range(2):
        lanes = slice(DIM * i, DIM * (i + 1))
        grads = []
        for block, (ref, query_t, mask) in enumerate(((own_ref, qto_ref, ao_ref), (sib_ref, qts_ref, as_ref))):
            query = query_t[lanes, :].astype(F32)
            weight = gates[block][8 * i : 8 * i + 8] * mask[...]
            gated = [(weight[level : level + 1, :] * query).astype(BF16) for level in range(4, 8)]
            grads.append(mm(jnp.concatenate(gated, axis=0), ref[G, lanes]))
        near_ref[lanes, :] = jnp.where(core == 1, grads[0][:DIM], grads[1][:DIM]) * INV
        total = (grads[0][DIM:] + grads[1][DIM:]) * INV
        for level in range(3):
            row = 256 * (level + 1) + DIM * i
            scr[row : row + DIM, :] = total[DIM * level : DIM * (level + 1)]
    place = (lax.axis_index("seq") // 2) % 4
    own_slice_ref[0:64, :] = scr[aligned(place, 64), :]
    own_slice_ref[64:128, :] = scr[pl.ds(pl.multiple_of(768 + 64 * place, 64), 64), :]
    for step, out in ((1, m1_ref), (2, m2_ref), (3, m3_ref)):
        peer = lax.rem(place + step, 4)
        gradient = jnp.where((place ^ peer) == 1, 256, 512)
        start = jnp.where(peer < place, gradient, 0)
        out[0:256, :] = scr[pl.ds(pl.multiple_of(start, 256), 256), :].astype(BF16)
        for part in range(2):
            rows = scr[pl.ds(pl.multiple_of(768 * part + 64 * peer, 64), 64), :]
            out[256 + 64 * part : 320 + 64 * part, :] = rows.astype(BF16)


def along_x_body(own_ref, m1_ref, m2_ref, m3_ref, spread_ref, states_ref, later_ref):
    place = (lax.axis_index("seq") // 2) % 4
    got = [m1_ref[...].astype(F32), m2_ref[...].astype(F32), m3_ref[...].astype(F32)]
    states = [jnp.zeros((256, DIM), F32)] * 2
    later = jnp.zeros((256, DIM), F32)
    for step in range(1, 4):
        source = lax.rem(place + 4 - step, 4)
        part = got[step - 1][:256]
        earlier = (source < place).astype(F32)
        level5 = ((place ^ source) == 1).astype(F32)
        states = [states[0] + part * (earlier * level5), states[1] + part * (earlier * (1.0 - level5))]
        later = later + part * (1.0 - earlier)
    states_ref[0:256, :] = states[0].astype(BF16)
    states_ref[256:512, :] = states[1].astype(BF16)
    later_ref[...] = later
    total = own_ref[...] + got[0][256:] + (got[1][256:] + got[2][256:])
    here = lax.axis_index("seq") // 8
    for group in range(8):
        spread_ref[ORDER.index(group)] = jnp.where(group > here, total[:64], total[64:]).astype(BF16)


def along_z_body(r_ref, o_ref):
    here = lax.axis_index("seq") // 8
    before = jnp.zeros((64, DIM), F32)
    after = jnp.zeros((64, DIM), F32)
    for group in range(8):
        part = r_ref[ORDER.index(group)].astype(F32)
        before = before + part * (here > group).astype(F32)
        after = after + part * (here < group).astype(F32)
    o_ref[...] = jnp.concatenate([before, after], axis=0).astype(BF16)


def far_body(own_ref, r1, r2, r3, states_ref, near_ref, mine_ref, later_ref):
    place = (lax.axis_index("seq") // 2) % 4
    mine_ref[0:512, :] = states_ref[...]
    for step, ref in enumerate((own_ref, r1, r2, r3)):
        peer = 64 * lax.rem(place + 4 - step, 4)
        mine_ref[pl.ds(pl.multiple_of(512 + peer, 64), 64), :] = ref[0:64, :]
        rows = pl.ds(pl.multiple_of(peer, 64), 64)
        later_ref[rows, :] = near_ref[rows, :] + ref[64:128, :].astype(F32)


def far_projection(i, ref, mine_ref):
    lanes = slice(DIM * i, DIM * (i + 1))
    states = [mine_ref[256 * level + DIM * i : 256 * level + DIM * (i + 1), :] for level in range(3)]
    projected = mm(jnp.concatenate(states, axis=0), ref[G, lanes], 1, 1)
    return [projected[DIM * level : DIM * (level + 1)] for level in range(3)]


def cross_body(
    own_ref, sib_ref, qto_ref, qts_ref, ao_ref, as_ref, go_ref, gs_ref, ro_ref, rs_ref, mine_ref, gl_ref, co_ref, cs_ref
):
    outs = []
    for ref, query_t, mask, gates_ref, rows_ref, cross_ref in (
        (own_ref, qto_ref, ao_ref, go_ref, ro_ref, co_ref), (sib_ref, qts_ref, as_ref, gs_ref, rs_ref, cs_ref),
    ):
        for i in range(2):
            query = query_t[DIM * i : DIM * (i + 1), :].astype(F32)
            rows = slice(8 * i, 8 * i + 8)
            gates = gates_ref[rows, :]
            weight = gates * mask[...]
            parts = [jnp.zeros((5, TOK), F32)]
            total = None
            for level, term in enumerate(far_projection(i, ref, mine_ref)):
                parts.append(jnp.sum(query * term, axis=0, keepdims=True))
                weighted = weight[5 + level : 6 + level, :] * term
                total = weighted if total is None else total + weighted
            cross_ref[DIM * i : DIM * (i + 1), :] = total
            grads = (rows_ref[rows, :] + jnp.concatenate(parts, axis=0)) * mask[...]
            outs.append(grads * gates * (1.0 - gates))
    gl_ref[...] = jnp.concatenate(outs, axis=0).astype(BF16)


def tail_body(
    block, blk_ref, kt_ref, state_ref, near_ref, mask_ref, gates_ref, later_ref, cross_ref, score_ref, prob_ref,
    out_ref, token_ref,
):
    core = lax.axis_index("seq") & 1
    masks = span_masks()
    upper = (core != block).astype(F32)
    for i in range(2):
        lanes = slice(DIM * i, DIM * (i + 1))
        query, key, value, grad = blk_ref[Q, lanes], blk_ref[K, lanes], blk_ref[V, lanes], blk_ref[G, lanes]
        weight = gates_ref[8 * i : 8 * i + 8, :] * mask_ref[...]
        near = mm((state_ref[lanes, :] * upper).astype(BF16), grad, 1, 1)
        later = (later_ref[lanes, :] + near_ref[lanes, :] * (1.0 - upper)).astype(BF16)
        dk = mm(value, later, 1, 1)
        dv = mm(key, later)
        for a in range(2):
            cols = slice(256 * a, 256 * a + 256)
            end = 256 * a + 256
            kept = slice(768 * i + 256 * a, 768 * i + 256 * a + end)
            pair = sum(weight[level : level + 1, cols] * masks[level] for level in range(3))
            if a:
                pair = jnp.concatenate([jnp.broadcast_to(weight[3:4, cols], (256, 256)), pair], axis=0)
            scored = (pair * score_ref[kept, :]).astype(BF16)
            weighted = (pair * prob_ref[kept, :]).astype(BF16)
            total = mm(kt_ref[lanes, :end], weighted) * INV
            total = total + weight[4:5, cols] * near[:, cols] + cross_ref[lanes, cols]
            out_ref[cols, lanes] = total.astype(BF16).T
            more_k = mm(weighted, query[cols]) * INV
            more_v = mm(scored, grad[cols])
            if a:
                dk, dv = dk + more_k, dv + more_v
            else:
                dk = jnp.concatenate([dk[:256] + more_k, dk[256:]], axis=0)
                dv = jnp.concatenate([dv[:256] + more_v, dv[256:]], axis=0)
        out_ref[K, lanes] = dk.astype(BF16)
        out_ref[V, lanes] = dv.astype(BF16)
    token_ref[...] = jnp.zeros_like(token_ref)


def gradw_body(xo_ref, xs_ref, g0, g1, g2, g3, o0, o1, o2, o3, own_scr, sib_scr, full):
    head = lax.axis_index("head")
    for step, part in enumerate((g0, g1, g2, g3)):
        rows = aligned(lax.rem(head + 4 - step, 4), 16)
        own_scr[rows, :] = part[0:16, :]
        sib_scr[rows, :] = part[16:32, :]
    full[...] = mm(own_scr[...], xo_ref[...]) + mm(sib_scr[...], xs_ref[...])
    place = (lax.axis_index("seq") // 2) % 4
    for step, out in enumerate((o0, o1, o2, o3)):
        start = 256 * lax.rem(place + step, 4)
        for block in range(2):
            part = full[:, pl.ds(pl.multiple_of(start + DIM * block, DIM), DIM)]
            out[64 * block : 64 * block + 64, :] = part.astype(out.dtype)


def sum_x_body(own_ref, r1, r2, r3, o_ref):
    total = (own_ref[...] + r1[...].astype(F32)) + (r2[...].astype(F32) + r3[...].astype(F32))
    total = total.astype(BF16)
    for place in range(8):
        o_ref[place] = total


def sum_z_body(scale, r_ref, o_ref):
    total = r_ref[0].astype(F32)
    for place in range(1, 8):
        total = total + r_ref[place].astype(F32)
    o_ref[...] = (total * scale).astype(BF16)


def both_body(mine_ref, other_ref, held_ref, o_ref, passed_ref):
    core = lax.axis_index("seq") & 1
    o_ref[aligned(core, DIM), :] = mine_ref[...]
    o_ref[aligned(1 - core, DIM), :] = other_ref[...]


def place_body(own_ref, recv_ref, dq_hbm, dk_hbm, dv_hbm, token_ref, sems):
    token_ref[...] = jnp.zeros_like(token_ref)
    core = lax.axis_index("seq") & 1
    copies = []
    for i, out in enumerate((dq_hbm, dk_hbm, dv_hbm)):
        rows = pl.ds(TOK * i, TOK)
        copies.append(pltpu.make_async_copy(own_ref.at[rows, :], out.at[:, aligned(core, 256)], sems.at[2 * i]))
        copies.append(pltpu.make_async_copy(recv_ref.at[rows, :], out.at[:, aligned(1 - core, 256)], sems.at[2 * i + 1]))
    for copy in copies:
        copy.start()
    for copy in copies:
        copy.wait()


def join_body(r0, r1, r2, r3, w_hbm, w_ref, sems):
    place = (lax.axis_index("seq") // 2) % 4
    copies = []
    for step, ref in enumerate((r0, r1, r2, r3)):
        data = ref[...].astype(F32)
        for block in range(2):
            parts = [
                data[DIM * half + 64 * block + 16 * group : DIM * half + 64 * block + 16 * group + 16]
                for group in range(4)
                for half in range(2)
            ]
            at = 2 * step + block
            w_ref[DIM * at : DIM * (at + 1), :] = jnp.concatenate(parts, axis=0).T
        rows = aligned(lax.rem(place + 4 - step, 4), 256)
        copies.append(
            pltpu.make_async_copy(w_ref.at[pl.ds(256 * step, 256), :], w_hbm.at[rows, :], sems.at[step])
        )
        copies[-1].start()
    for copy in copies:
        copy.wait()


def shards(layer_input, gate_weight, queries, key_vectors, value_vectors, grad_output, reach_level):
    seq_count = lax.axis_size("seq")
    columns = [[8 * z + place for z in ORDER] for place in range(8)]
    swap = [(d, d ^ 1) for d in range(seq_count)]

    def sibling(value):
        return lax.ppermute(value, "seq", swap)

    def rotate_x(value, step):
        pairs = [(d, d // 8 * 8 + (d + 2 * step) % 8) for d in range(seq_count)]
        return lax.ppermute(value, "seq", pairs)

    def rotate(value, step):
        return lax.ppermute(value, "head", [(h, (h + step) % 4) for h in range(4)])

    whole = pl.BlockSpec(memory_space=pltpu.VMEM)
    hbm = pl.BlockSpec(memory_space=pl.ANY)

    tok16 = shape((16, TOK), F32)
    mask8 = shape((LEVELS, TOK), F32)
    half = shape((256, DIM), F32)

    *parts, own, leaving = call(
        front_body,
        [shape((32, TOK), F32)] * 4 + [shape((4 * TOK + 16, 256), BF16)] * 2,
        (layer_input, gate_weight, queries, key_vectors, value_vectors, grad_output, reach_level),
        in_specs=[hbm] * 7,
        out_specs=[hbm] * 6,
        scratch=[
            pltpu.VMEM((TOK, 1024), BF16), pltpu.VMEM((1024, DIM), BF16), pltpu.VMEM((DIM, TOK), F32),
            pltpu.VMEM((4 * TOK + 16, 256), BF16), pltpu.VMEM((4 * TOK + 16, 256), BF16),
            pltpu.SMEM((LEVELS,), jnp.int32), pltpu.SemaphoreType.DMA((11,)), pltpu.SemaphoreType.DMA((6,)),
        ],
        limit=VMEM_ALL,
    )
    logits = [parts[0]] + [rotate(parts[step], step) for step in range(1, 4)]
    sib = sibling(leaving)
    sib_input = sibling(layer_input)
    state_own, state_sib, qt_own, qt_sib, kt_own, kt_sib, allow_own, allow_sib = call(
        state_body, [half, half] + [shape((256, TOK), BF16)] * 4 + [mask8, mask8],
        (own, sib),
    )
    pairs = shape((1536, 256), F32)
    rows_own, rows_sib, sc_own, pr_own, sc_sib, pr_sib = call(
        rows_body, [tok16, tok16] + [pairs] * 4, (own, sib, qt_own, qt_sib, state_own, state_sib)
    )
    logits_own, logits_send = call(gather_body, [tok16, tok16], tuple(logits), after=(rows_own,))

    message = shape((384, DIM), BF16)
    eighth = shape((DIM, DIM), BF16)
    gates_own, gates_sib, near, own_slice, *messages = call(
        level_body, [tok16, tok16, half, shape((DIM, DIM), F32), message, message, message],
        (own, sib, qt_own, qt_sib, allow_own, allow_sib, state_own, state_sib, logits_own, sibling(logits_send)),
        scratch=[pltpu.VMEM((1024, DIM), F32)],
        after=(sib_input, rows_own),
    )
    spread, close_states, close_later = call(
        along_x_body, [shape((8, 64, DIM), BF16), shape((512, DIM), BF16), half],
        (own_slice, *(rotate_x(messages[step - 1], step) for step in (1, 2, 3))),
    )
    got = call(along_z_body, eighth, (lax.all_to_all(spread, "seq", 0, 0, axis_index_groups=columns),))
    mine, later = call(
        far_body, [shape((768, DIM), BF16), half],
        (got, *(rotate_x(got, step) for step in (1, 2, 3)), close_states, close_later),
    )
    tok256 = shape((256, TOK), F32)
    grad_logits, cross_own, cross_sib = call(
        cross_body, [shape((32, TOK), BF16), tok256, tok256],
        (own, sib, qt_own, qt_sib, allow_own, allow_sib, gates_own, gates_sib, rows_own, rows_sib, mine),
    )

    gl = [grad_logits] + [rotate(grad_logits, step) for step in range(1, 4)]
    def tail(which, blk, key_t, state, allowed, gates, cross, scores, probs, after):
        return call(
            functools.partial(tail_body, which), [shape((3 * TOK, 256), BF16), shape((8, DIM), F32)],
            (blk, key_t, state, near, allowed, gates, later, cross, scores, probs), after=after, cost=(4 * 10**9, 16 * 10**6),
        )

    out_sib, token = tail(1, sib, kt_sib, state_own, allow_sib, gates_sib, cross_sib, sc_sib, pr_sib, (grad_logits,))
    out_own, token = tail(0, own, kt_own, state_sib, allow_own, gates_own, cross_own, sc_own, pr_own, (token,))
    quarter = shape((DIM, DIM), BF16)
    sums = call(
        gradw_body, [shape((DIM, DIM), F32)] + [quarter] * 3, (layer_input, sib_input, *gl),
        scratch=[pltpu.VMEM((64, TOK), BF16), pltpu.VMEM((64, TOK), BF16), pltpu.VMEM((64, 1024), F32)],
        after=(token,),
    )
    got3 = [sums[0]] + [rotate_x(sums[step], step) for step in range(1, 4)]
    spread = call(sum_x_body, shape((8, DIM, DIM), BF16), tuple(got3))
    got4 = lax.all_to_all(spread, "seq", 0, 0, axis_index_groups=columns)
    scale = 1.0 / math.sqrt(TOK * seq_count)
    mine_sum = call(functools.partial(sum_z_body, scale), quarter, (got4,))
    other_sum = sibling(mine_sum)
    both, out_sib = call(
        both_body, [shape((256, DIM), BF16), shape((3 * TOK, 256), BF16)], (mine_sum, other_sum, out_sib),
        in_specs=[whole, whole, hbm], out_specs=[whole, hbm], aliases={2: 1},
    )
    out_recv = sibling(out_sib)
    *grads, token = call(
        place_body, [shape((TOK, 512), BF16)] * 3 + [shape((8, DIM), F32)], (out_own, out_recv),
        out_specs=[hbm] * 3 + [whole], scratch=[pltpu.SemaphoreType.DMA((6,))], after=(both,),
    )
    got5 = [both] + [rotate_x(both, step) for step in range(1, 4)]
    grad_weight = call(
        join_body, shape((1024, DIM), F32), tuple(got5),
        out_specs=hbm,
        after=(token,),
        scratch=[pltpu.VMEM((1024, DIM), F32), pltpu.SemaphoreType.DMA((4,))],
    )
    return (*grads, grad_weight)


def solution(mesh):
    placed = (
        P("seq", "head"),
        P("head", None),
        P("seq", "head"),
        P("seq", "head"),
        P("seq", "head"),
        P("seq", "head"),
        P("seq"),
    )
    return jax.shard_map(
        shards,
        mesh=mesh,
        in_specs=placed,
        out_specs=(P("seq", "head"), P("seq", "head"), P("seq", "head"), P("head", None)),
        check_vma=False,
    )
```

```python
import functools
import math

import jax
import jax.numpy as jnp
from jax import lax
from jax.experimental import pallas as pl
from jax.experimental.pallas import tpu as pltpu
from jax.sharding import PartitionSpec as P

F32 = jnp.float32
BF16 = jnp.bfloat16
TOK = 512
DIM = 128
SPAN = 64
LEVELS = 8
ORDER = [5, 4, 6, 3, 2, 7, 0, 1]
INV = 1.0 / DIM
VMEM_LIMIT = 24 * 1024 * 1024
VMEM_ALL = 60 * 1024 * 1024


def mm(left, right, left_dim=1, right_dim=0):
    return lax.dot_general(
        left, right, (((left_dim,), (right_dim,)), ((), ())), preferred_element_type=F32
    )


def aligned(index, size):
    return pl.ds(pl.multiple_of(index * size, size), size)


def call(
    body, out_shape, args, in_specs=None, out_specs=None, grid=(), scratch=(), cost=(10**7, 10**6), after=(),
    limit=VMEM_LIMIT, aliases=None,
):
    whole = pl.BlockSpec(memory_space=pltpu.VMEM)
    many = isinstance(out_shape, (tuple, list))
    used = len(args)
    in_specs = list(in_specs or [whole] * used) + [pl.BlockSpec(memory_space=pl.ANY)] * len(after)
    args = (*args, *after)

    def kernel(*refs):
        body(*refs[:used], *refs[len(args) :])

    return pl.pallas_call(
        kernel,
        out_shape=out_shape,
        grid=grid,
        in_specs=in_specs,
        input_output_aliases=aliases or {},
        out_specs=out_specs or ([whole] * len(out_shape) if many else whole),
        scratch_shapes=list(scratch),
        compiler_params=pltpu.CompilerParams(vmem_limit_bytes=limit),
        cost_estimate=pl.CostEstimate(flops=cost[0], bytes_accessed=cost[1], transcendentals=0),
    )(*args)


def shape(dims, dtype):
    return jax.ShapeDtypeStruct(dims, dtype)


def front_body(
    x_hbm, w_hbm, q_hbm, k_hbm, v_hbm, g_hbm, reach_hbm, p0, p1, p2, p3, own_hbm, leaving_hbm,
    x_ref, w_ref, part_ref, own_ref, leaving_ref, reach_ref, in_sems, out_sems,
):
    head = lax.axis_index("head")
    core = lax.axis_index("seq") & 1
    ins, outs = [], []

    def load(src, dst):
        ins.append(pltpu.make_async_copy(src, dst, in_sems.at[len(ins)]))
        ins[-1].start()

    def store(src, dst):
        outs.append(pltpu.make_async_copy(src, dst, out_sems.at[len(outs)]))
        outs[-1].start()

    load(w_hbm, w_ref)
    load(x_hbm, x_ref)
    for side, ref in ((1 - core, leaving_ref), (core, own_ref)):
        for i, src in enumerate((q_hbm, k_hbm, v_hbm, g_hbm)):
            load(src.at[:, aligned(side, 256)], ref.at[pl.ds(TOK * i, TOK), :])
    load(reach_hbm, reach_ref)
    ins[0].wait()
    ins[1].wait()
    part_ref[...] = mm(w_ref[...], x_ref[...], 0, 1)
    for step, out in enumerate((p0, p1, p2, p3)):
        store(part_ref.at[aligned(lax.rem(head + step, 4), 32), :], out)
    ins[10].wait()
    lane = lax.broadcasted_iota(jnp.int32, (LEVELS, TOK), 1) // SPAN
    level = lax.broadcasted_iota(jnp.int32, (LEVELS, TOK), 0)
    reach = jnp.zeros((LEVELS, TOK), jnp.int32)
    for span in range(TOK // SPAN):
        reach = jnp.where(lane == span, reach_ref[span], reach)
    allowed = (level <= reach).astype(F32)
    allowed = jnp.concatenate([allowed[:, :256], allowed[:, 256:]], axis=0).astype(BF16)
    leaving_ref[4 * TOK :, :] = allowed
    own_ref[4 * TOK :, :] = allowed
    for copy in ins[2:6]:
        copy.wait()
    store(leaving_ref, leaving_hbm)
    for copy in ins[6:10]:
        copy.wait()
    store(own_ref, own_hbm)
    for copy in outs:
        copy.wait()


def gather_body(l0, l1, l2, l3, keep_ref, send_ref):
    core = lax.axis_index("seq") & 1
    keep = aligned(core, 16)
    send = aligned(1 - core, 16)
    keep_ref[...] = (l0[keep, :] + l1[keep, :]) + (l2[keep, :] + l3[keep, :])
    send_ref[...] = (l0[send, :] + l1[send, :]) + (l2[send, :] + l3[send, :])


Q, K, V, G = (slice(TOK * i, TOK * (i + 1)) for i in range(4))


def state_body(own_ref, sib_ref, so_ref, ss_ref, qto_ref, qts_ref, kto_ref, kts_ref, ao_ref, as_ref):
    for ref, state, query_t, key_t, mask in (
        (own_ref, so_ref, qto_ref, kto_ref, ao_ref), (sib_ref, ss_ref, qts_ref, kts_ref, as_ref),
    ):
        for i in range(2):
            lanes = slice(DIM * i, DIM * (i + 1))
            state[lanes, :] = mm(ref[K, lanes], ref[V, lanes], 0, 0) * INV
            query_t[lanes, :] = ref[Q, lanes].T
            key_t[lanes, :] = ref[K, lanes].T
        allowed = ref[4 * TOK :, :].astype(F32)
        mask[...] = jnp.concatenate([allowed[:8], allowed[8:]], axis=1)


def span_masks():
    src = lax.broadcasted_iota(jnp.int32, (256, 256), 0)
    dst = lax.broadcasted_iota(jnp.int32, (256, 256), 1)
    near, far = src // SPAN, dst // SPAN
    return [
        ((near == far) & (src <= dst)).astype(F32),
        ((near < far) & (near // 2 == far // 2)).astype(F32),
        (near // 2 < far // 2).astype(F32),
    ]


def rows_body(own_ref, sib_ref, qto_ref, qts_ref, so_ref, ss_ref, ro_ref, rs_ref, sco_ref, pro_ref, scs_ref, prs_ref):
    core = lax.axis_index("seq") & 1
    masks = span_masks()
    none = jnp.zeros((1, 256), F32)
    for block, (ref, query_t, state, out, score_ref, prob_ref) in enumerate((
        (own_ref, qto_ref, ss_ref, ro_ref, sco_ref, pro_ref), (sib_ref, qts_ref, so_ref, rs_ref, scs_ref, prs_ref),
    )):
        upper = (core != block).astype(F32)
        for i in range(2):
            lanes = slice(DIM * i, DIM * (i + 1))
            near = (state[lanes, :] * upper).astype(BF16)
            projected = mm(near, ref[G, lanes], 1, 1)
            near_row = jnp.sum(query_t[lanes, :].astype(F32) * projected, axis=0, keepdims=True)
            for a in range(2):
                cols = slice(256 * a, 256 * a + 256)
                end = 256 * a + 256
                scores = mm(ref[TOK : TOK + end, lanes], ref[cols, lanes], 1, 1) * INV
                probs = mm(ref[2 * TOK : 2 * TOK + end, lanes], ref[3 * TOK + 256 * a : 3 * TOK + end, lanes], 1, 1)
                kept = slice(768 * i + 256 * a, 768 * i + 256 * a + end)
                score_ref[kept, :] = scores
                prob_ref[kept, :] = probs
                prod = scores * probs
                diagonal = prod[256 * a :]
                sums = [jnp.sum(diagonal * mask, axis=0, keepdims=True) for mask in masks]
                sums.append(jnp.sum(prod[:256], axis=0, keepdims=True) if a else none)
                sums.append(near_row[:, cols])
                out[8 * i : 8 * i + 8, cols] = jnp.concatenate(sums + [none] * 3, axis=0)


def level_body(
    own_ref, sib_ref, qto_ref, qts_ref, ao_ref, as_ref, so_ref, ss_ref, lo_ref, ls_ref,
    go_ref, gs_ref, near_ref, own_slice_ref, m1_ref, m2_ref, m3_ref, scr,
):
    core = lax.axis_index("seq") & 1
    gates = [jax.nn.sigmoid(lo_ref[...]), jax.nn.sigmoid(ls_ref[...])]
    go_ref[...] = gates[0]
    gs_ref[...] = gates[1]
    scr[0:256, :] = so_ref[...] + ss_ref[...]
    for i in range(2):
        lanes = slice(DIM * i, DIM * (i + 1))
        grads = []
        for block, (ref, query_t, mask) in enumerate(((own_ref, qto_ref, ao_ref), (sib_ref, qts_ref, as_ref))):
            query = query_t[lanes, :].astype(F32)
            weight = gates[block][8 * i : 8 * i + 8] * mask[...]
            gated = [(weight[level : level + 1, :] * query).astype(BF16) for level in range(4, 8)]
            grads.append(mm(jnp.concatenate(gated, axis=0), ref[G, lanes]))
        near_ref[lanes, :] = jnp.where(core == 1, grads[0][:DIM], grads[1][:DIM]) * INV
        total = (grads[0][DIM:] + grads[1][DIM:]) * INV
        for level in range(3):
            row = 256 * (level + 1) + DIM * i
            scr[row : row + DIM, :] = total[DIM * level : DIM * (level + 1)]
    place = (lax.axis_index("seq") // 2) % 4
    own_slice_ref[0:64, :] = scr[aligned(place, 64), :]
    own_slice_ref[64:128, :] = scr[pl.ds(pl.multiple_of(768 + 64 * place, 64), 64), :]
    for step, out in ((1, m1_ref), (2, m2_ref), (3, m3_ref)):
        peer = lax.rem(place + step, 4)
        gradient = jnp.where((place ^ peer) == 1, 256, 512)
        start = jnp.where(peer < place, gradient, 0)
        out[0:256, :] = scr[pl.ds(pl.multiple_of(start, 256), 256), :].astype(BF16)
        for part in range(2):
            rows = scr[pl.ds(pl.multiple_of(768 * part + 64 * peer, 64), 64), :]
            out[256 + 64 * part : 320 + 64 * part, :] = rows.astype(BF16)


def along_x_body(own_ref, m1_ref, m2_ref, m3_ref, spread_ref, states_ref, later_ref):
    place = (lax.axis_index("seq") // 2) % 4
    got = [m1_ref[...].astype(F32), m2_ref[...].astype(F32), m3_ref[...].astype(F32)]
    states = [jnp.zeros((256, DIM), F32)] * 2
    later = jnp.zeros((256, DIM), F32)
    for step in range(1, 4):
        source = lax.rem(place + 4 - step, 4)
        part = got[step - 1][:256]
        earlier = (source < place).astype(F32)
        level5 = ((place ^ source) == 1).astype(F32)
        states = [states[0] + part * (earlier * level5), states[1] + part * (earlier * (1.0 - level5))]
        later = later + part * (1.0 - earlier)
    states_ref[0:256, :] = states[0].astype(BF16)
    states_ref[256:512, :] = states[1].astype(BF16)
    later_ref[...] = later
    total = own_ref[...] + got[0][256:] + (got[1][256:] + got[2][256:])
    here = lax.axis_index("seq") // 8
    for group in range(8):
        spread_ref[ORDER.index(group)] = jnp.where(group > here, total[:64], total[64:]).astype(BF16)


def along_z_body(r_ref, o_ref):
    here = lax.axis_index("seq") // 8
    before = jnp.zeros((64, DIM), F32)
    after = jnp.zeros((64, DIM), F32)
    for group in range(8):
        part = r_ref[ORDER.index(group)].astype(F32)
        before = before + part * (here > group).astype(F32)
        after = after + part * (here < group).astype(F32)
    o_ref[...] = jnp.concatenate([before, after], axis=0).astype(BF16)


def far_body(own_ref, r1, r2, r3, states_ref, near_ref, mine_ref, later_ref):
    place = (lax.axis_index("seq") // 2) % 4
    mine_ref[0:512, :] = states_ref[...]
    for step, ref in enumerate((own_ref, r1, r2, r3)):
        peer = 64 * lax.rem(place + 4 - step, 4)
        mine_ref[pl.ds(pl.multiple_of(512 + peer, 64), 64), :] = ref[0:64, :]
        rows = pl.ds(pl.multiple_of(peer, 64), 64)
        later_ref[rows, :] = near_ref[rows, :] + ref[64:128, :].astype(F32)


def far_projection(i, ref, mine_ref):
    lanes = slice(DIM * i, DIM * (i + 1))
    states = [mine_ref[256 * level + DIM * i : 256 * level + DIM * (i + 1), :] for level in range(3)]
    projected = mm(jnp.concatenate(states, axis=0), ref[G, lanes], 1, 1)
    return [projected[DIM * level : DIM * (level + 1)] for level in range(3)]


def cross_body(
    own_ref, sib_ref, qto_ref, qts_ref, ao_ref, as_ref, go_ref, gs_ref, ro_ref, rs_ref, mine_ref, gl_ref, co_ref, cs_ref
):
    outs = []
    for ref, query_t, mask, gates_ref, rows_ref, cross_ref in (
        (own_ref, qto_ref, ao_ref, go_ref, ro_ref, co_ref), (sib_ref, qts_ref, as_ref, gs_ref, rs_ref, cs_ref),
    ):
        for i in range(2):
            query = query_t[DIM * i : DIM * (i + 1), :].astype(F32)
            rows = slice(8 * i, 8 * i + 8)
            gates = gates_ref[rows, :]
            weight = gates * mask[...]
            parts = [jnp.zeros((5, TOK), F32)]
            total = None
            for level, term in enumerate(far_projection(i, ref, mine_ref)):
                parts.append(jnp.sum(query * term, axis=0, keepdims=True))
                weighted = weight[5 + level : 6 + level, :] * term
                total = weighted if total is None else total + weighted
            cross_ref[DIM * i : DIM * (i + 1), :] = total
            grads = (rows_ref[rows, :] + jnp.concatenate(parts, axis=0)) * mask[...]
            outs.append(grads * gates * (1.0 - gates))
    gl_ref[...] = jnp.concatenate(outs, axis=0).astype(BF16)


def tail_body(
    block, blk_ref, kt_ref, state_ref, near_ref, mask_ref, gates_ref, later_ref, cross_ref, score_ref, prob_ref,
    out_ref, token_ref,
):
    core = lax.axis_index("seq") & 1
    masks = span_masks()
    upper = (core != block).astype(F32)
    for i in range(2):
        lanes = slice(DIM * i, DIM * (i + 1))
        query, key, value, grad = blk_ref[Q, lanes], blk_ref[K, lanes], blk_ref[V, lanes], blk_ref[G, lanes]
        weight = gates_ref[8 * i : 8 * i + 8, :] * mask_ref[...]
        near = mm((state_ref[lanes, :] * upper).astype(BF16), grad, 1, 1)
        later = (later_ref[lanes, :] + near_ref[lanes, :] * (1.0 - upper)).astype(BF16)
        dk = mm(value, later, 1, 1)
        dv = mm(key, later)
        for a in range(2):
            cols = slice(256 * a, 256 * a + 256)
            end = 256 * a + 256
            kept = slice(768 * i + 256 * a, 768 * i + 256 * a + end)
            pair = sum(weight[level : level + 1, cols] * masks[level] for level in range(3))
            if a:
                pair = jnp.concatenate([jnp.broadcast_to(weight[3:4, cols], (256, 256)), pair], axis=0)
            scored = (pair * score_ref[kept, :]).astype(BF16)
            weighted = (pair * prob_ref[kept, :]).astype(BF16)
            total = mm(kt_ref[lanes, :end], weighted) * INV
            total = total + weight[4:5, cols] * near[:, cols] + cross_ref[lanes, cols]
            out_ref[cols, lanes] = total.astype(BF16).T
            more_k = mm(weighted, query[cols]) * INV
            more_v = mm(scored, grad[cols])
            if a:
                dk, dv = dk + more_k, dv + more_v
            else:
                dk = jnp.concatenate([dk[:256] + more_k, dk[256:]], axis=0)
                dv = jnp.concatenate([dv[:256] + more_v, dv[256:]], axis=0)
        out_ref[K, lanes] = dk.astype(BF16)
        out_ref[V, lanes] = dv.astype(BF16)
    token_ref[...] = jnp.zeros_like(token_ref)


def gradw_body(xo_ref, xs_ref, g0, g1, g2, g3, o0, o1, o2, o3, own_scr, sib_scr, full):
    head = lax.axis_index("head")
    for step, part in enumerate((g0, g1, g2, g3)):
        rows = aligned(lax.rem(head + 4 - step, 4), 16)
        own_scr[rows, :] = part[0:16, :]
        sib_scr[rows, :] = part[16:32, :]
    full[...] = mm(own_scr[...], xo_ref[...]) + mm(sib_scr[...], xs_ref[...])
    place = (lax.axis_index("seq") // 2) % 4
    for step, out in enumerate((o0, o1, o2, o3)):
        start = 256 * lax.rem(place + step, 4)
        for block in range(2):
            part = full[:, pl.ds(pl.multiple_of(start + DIM * block, DIM), DIM)]
            out[64 * block : 64 * block + 64, :] = part.astype(out.dtype)


def sum_x_body(own_ref, r1, r2, r3, o_ref):
    total = (own_ref[...] + r1[...].astype(F32)) + (r2[...].astype(F32) + r3[...].astype(F32))
    total = total.astype(BF16)
    for place in range(8):
        o_ref[place] = total


def sum_z_body(scale, r_ref, held_ref, o_ref, passed_ref):
    total = r_ref[0].astype(F32)
    for place in range(1, 8):
        total = total + r_ref[place].astype(F32)
    o_ref[...] = (total * scale).astype(BF16)


def pack_body(r0, r1, r2, r3, o_ref):
    for step, ref in enumerate((r0, r1, r2, r3)):
        o_ref[DIM * step : DIM * (step + 1), :] = ref[...]


def place_body(own_ref, recv_ref, dq_hbm, dk_hbm, dv_hbm, token_ref, sems):
    token_ref[...] = jnp.zeros_like(token_ref)
    core = lax.axis_index("seq") & 1
    copies = []
    for i, out in enumerate((dq_hbm, dk_hbm, dv_hbm)):
        rows = pl.ds(TOK * i, TOK)
        copies.append(pltpu.make_async_copy(own_ref.at[rows, :], out.at[:, aligned(core, 256)], sems.at[2 * i]))
        copies.append(pltpu.make_async_copy(recv_ref.at[rows, :], out.at[:, aligned(1 - core, 256)], sems.at[2 * i + 1]))
    for copy in copies:
        copy.start()
    for copy in copies:
        copy.wait()


def join_body(mine_ref, other_ref, w_hbm, w_ref, sems):
    place = (lax.axis_index("seq") // 2) % 4
    core = lax.axis_index("seq") & 1
    mine, other = mine_ref[...].astype(F32), other_ref[...].astype(F32)
    halves = [jnp.where(core == 0, mine, other), jnp.where(core == 0, other, mine)]
    copies = []
    for step in range(4):
        for block in range(2):
            row = DIM * step + 64 * block
            parts = [half[row + 16 * group : row + 16 * group + 16] for group in range(4) for half in halves]
            at = 2 * step + block
            w_ref[DIM * at : DIM * (at + 1), :] = jnp.concatenate(parts, axis=0).T
        rows = aligned(lax.rem(place + 4 - step, 4), 256)
        copies.append(
            pltpu.make_async_copy(w_ref.at[pl.ds(256 * step, 256), :], w_hbm.at[rows, :], sems.at[step])
        )
        copies[-1].start()
    for copy in copies:
        copy.wait()


def shards(layer_input, gate_weight, queries, key_vectors, value_vectors, grad_output, reach_level):
    seq_count = lax.axis_size("seq")
    columns = [[8 * z + place for z in ORDER] for place in range(8)]
    swap = [(d, d ^ 1) for d in range(seq_count)]

    def sibling(value):
        return lax.ppermute(value, "seq", swap)

    def rotate_x(value, step):
        pairs = [(d, d // 8 * 8 + (d + 2 * step) % 8) for d in range(seq_count)]
        return lax.ppermute(value, "seq", pairs)

    def rotate(value, step):
        return lax.ppermute(value, "head", [(h, (h + step) % 4) for h in range(4)])

    whole = pl.BlockSpec(memory_space=pltpu.VMEM)
    hbm = pl.BlockSpec(memory_space=pl.ANY)

    tok16 = shape((16, TOK), F32)
    mask8 = shape((LEVELS, TOK), F32)
    half = shape((256, DIM), F32)

    *parts, own, leaving = call(
        front_body,
        [shape((32, TOK), F32)] * 4 + [shape((4 * TOK + 16, 256), BF16)] * 2,
        (layer_input, gate_weight, queries, key_vectors, value_vectors, grad_output, reach_level),
        in_specs=[hbm] * 7,
        out_specs=[hbm] * 6,
        scratch=[
            pltpu.VMEM((TOK, 1024), BF16), pltpu.VMEM((1024, DIM), BF16), pltpu.VMEM((DIM, TOK), F32),
            pltpu.VMEM((4 * TOK + 16, 256), BF16), pltpu.VMEM((4 * TOK + 16, 256), BF16),
            pltpu.SMEM((LEVELS,), jnp.int32), pltpu.SemaphoreType.DMA((11,)), pltpu.SemaphoreType.DMA((6,)),
        ],
        limit=VMEM_ALL,
    )
    logits = [parts[0]] + [rotate(parts[step], step) for step in range(1, 4)]
    sib = sibling(leaving)
    sib_input = sibling(layer_input)
    state_own, state_sib, qt_own, qt_sib, kt_own, kt_sib, allow_own, allow_sib = call(
        state_body, [half, half] + [shape((256, TOK), BF16)] * 4 + [mask8, mask8],
        (own, sib),
    )
    pairs = shape((1536, 256), F32)
    rows_own, rows_sib, sc_own, pr_own, sc_sib, pr_sib = call(
        rows_body, [tok16, tok16] + [pairs] * 4, (own, sib, qt_own, qt_sib, state_own, state_sib)
    )
    logits_own, logits_send = call(gather_body, [tok16, tok16], tuple(logits), after=(rows_own,))

    message = shape((384, DIM), BF16)
    eighth = shape((DIM, DIM), BF16)
    gates_own, gates_sib, near, own_slice, *messages = call(
        level_body, [tok16, tok16, half, shape((DIM, DIM), F32), message, message, message],
        (own, sib, qt_own, qt_sib, allow_own, allow_sib, state_own, state_sib, logits_own, sibling(logits_send)),
        scratch=[pltpu.VMEM((1024, DIM), F32)],
        after=(sib_input, rows_own),
    )
    spread, close_states, close_later = call(
        along_x_body, [shape((8, 64, DIM), BF16), shape((512, DIM), BF16), half],
        (own_slice, *(rotate_x(messages[step - 1], step) for step in (1, 2, 3))),
    )
    got = call(along_z_body, eighth, (lax.all_to_all(spread, "seq", 0, 0, axis_index_groups=columns),))
    mine, later = call(
        far_body, [shape((768, DIM), BF16), half],
        (got, *(rotate_x(got, step) for step in (1, 2, 3)), close_states, close_later),
    )
    tok256 = shape((256, TOK), F32)
    grad_logits, cross_own, cross_sib = call(
        cross_body, [shape((32, TOK), BF16), tok256, tok256],
        (own, sib, qt_own, qt_sib, allow_own, allow_sib, gates_own, gates_sib, rows_own, rows_sib, mine),
    )

    gl = [grad_logits] + [rotate(grad_logits, step) for step in range(1, 4)]
    def tail(which, blk, key_t, state, allowed, gates, cross, scores, probs, after):
        return call(
            functools.partial(tail_body, which), [shape((3 * TOK, 256), BF16), shape((8, DIM), F32)],
            (blk, key_t, state, near, allowed, gates, later, cross, scores, probs), after=after, cost=(4 * 10**9, 16 * 10**6),
        )

    out_sib, token = tail(1, sib, kt_sib, state_own, allow_sib, gates_sib, cross_sib, sc_sib, pr_sib, (grad_logits,))
    out_own, token = tail(0, own, kt_own, state_sib, allow_own, gates_own, cross_own, sc_own, pr_own, (token,))
    quarter = shape((DIM, DIM), BF16)
    sums = call(
        gradw_body, [shape((DIM, DIM), F32)] + [quarter] * 3, (layer_input, sib_input, *gl),
        scratch=[pltpu.VMEM((64, TOK), BF16), pltpu.VMEM((64, TOK), BF16), pltpu.VMEM((64, 1024), F32)],
        after=(token,),
    )
    got3 = [sums[0]] + [rotate_x(sums[step], step) for step in range(1, 4)]
    spread = call(sum_x_body, shape((8, DIM, DIM), BF16), tuple(got3))
    got4 = lax.all_to_all(spread, "seq", 0, 0, axis_index_groups=columns)
    scale = 1.0 / math.sqrt(TOK * seq_count)
    mine_sum, out_sib = call(
        functools.partial(sum_z_body, scale), [quarter, shape((3 * TOK, 256), BF16)], (got4, out_sib),
        in_specs=[whole, hbm], out_specs=[whole, hbm], aliases={1: 1},
    )
    out_recv = sibling(out_sib)
    got5 = [mine_sum] + [rotate_x(mine_sum, step) for step in range(1, 4)]
    *grads, token = call(
        place_body, [shape((TOK, 512), BF16)] * 3 + [shape((8, DIM), F32)], (out_own, out_recv),
        out_specs=[hbm] * 3 + [whole], scratch=[pltpu.SemaphoreType.DMA((6,))], after=(mine_sum,),
    )
    w_half = call(pack_body, shape((512, DIM), BF16), tuple(got5), after=(token,))
    grad_weight = call(
        join_body, shape((1024, DIM), F32), (w_half, sibling(w_half)),
        out_specs=hbm,
        scratch=[pltpu.VMEM((1024, DIM), F32), pltpu.SemaphoreType.DMA((4,))],
    )
    return (*grads, grad_weight)


def solution(mesh):
    placed = (
        P("seq", "head"),
        P("head", None),
        P("seq", "head"),
        P("seq", "head"),
        P("seq", "head"),
        P("seq", "head"),
        P("seq"),
    )
    return jax.shard_map(
        shards,
        mesh=mesh,
        in_specs=placed,
        out_specs=(P("seq", "head"), P("seq", "head"), P("seq", "head"), P("head", None)),
        check_vma=False,
    )
```
